32 devices in a mesh: dp: 16 (over z, x, core), fsdp: 2 (over y).
Axes of the slice: x: 2, y: 2, z: 4, core: 2. Of those that a mesh axis runs over, the one named last changes fastest.
Arguments:
- tokens: bfloat16 [32768, 768], P(('dp', 'fsdp')), may hold values from -8 to 8
- segment_ids: int32 [64, 512], P(('dp', 'fsdp')), may hold values from 0 to 3, never falling along the last dimension, each value on 1 to 256 neighbouring positions
- valid: int32 [64, 512], P(('dp', 'fsdp')), may hold values from 0 to 1, as said below
- input_weight: bfloat16 [768, 2304], P(('dp', 'fsdp')), may hold values from -0.21875 to 0.21875
- query_bias: bfloat16 [768], P(('dp', 'fsdp')), may hold values from -3 to 3
- value_bias: bfloat16 [768], P(('dp', 'fsdp')), may hold values from -3 to 3
- output_weight: bfloat16 [768, 768], P(('dp', 'fsdp')), may hold values from -1.25 to 1.25
- output_bias: bfloat16 [768], P(('dp', 'fsdp')), may hold values from -3 to 3
- first_gain: bfloat16 [768], P(('dp', 'fsdp')), may hold values from 0.099609375 to 1.8984375
- first_shift: bfloat16 [768], P(('dp', 'fsdp')), may hold values from -3 to 3
- expand_weight: bfloat16 [768, 3072], P(('dp', 'fsdp')), may hold values from -0.21875 to 0.21875
- expand_bias: bfloat16 [3072], P(('dp', 'fsdp')), may hold values from -3 to 3
- shrink_weight: bfloat16 [3072, 768], P(('dp', 'fsdp')), may hold values from -0.15625 to 0.15625
- shrink_bias: bfloat16 [768], P(('dp', 'fsdp')), may hold values from -3 to 3
- second_gain: bfloat16 [768], P(('dp', 'fsdp')), may hold values from 0.099609375 to 1.8984375
- second_shift: bfloat16 [768], P(('dp', 'fsdp')), may hold values from -3 to 3
- cotangent: bfloat16 [32768, 768], P(('dp', 'fsdp')), may hold values from -6 to 6
Outputs:
- layer_output: bfloat16 [32768, 768], P(('dp', 'fsdp'))
- token_gradient: float32 [32768, 768], P(('dp', 'fsdp'))
- statistics: float32 [4], replicated
- input_weight_gradient: float32 [768, 2304], P(('dp', 'fsdp'))
- query_bias_gradient: float32 [768], P(('dp', 'fsdp'))
- value_bias_gradient: float32 [768], P(('dp', 'fsdp'))
- output_weight_gradient: float32 [768, 768], P(('dp', 'fsdp'))
- output_bias_gradient: float32 [768], P(('dp', 'fsdp'))
- first_gain_gradient: float32 [768], P(('dp', 'fsdp'))
- first_shift_gradient: float32 [768], P(('dp', 'fsdp'))
- expand_weight_gradient: float32 [768, 3072], P(('dp', 'fsdp'))
- expand_bias_gradient: float32 [3072], P(('dp', 'fsdp'))
- shrink_weight_gradient: float32 [3072, 768], P(('dp', 'fsdp'))
- shrink_bias_gradient: float32 [768], P(('dp', 'fsdp'))
- second_gain_gradient: float32 [768], P(('dp', 'fsdp'))
- second_shift_gradient: float32 [768], P(('dp', 'fsdp'))
The draws below stay inside these ranges and needn't reach their ends.
Inputs may be any that keep to these rules, and one draw needn't show every extreme that they name: 1 marks a valid token; the first token of every sequence is valid.
All inputs are finite; a program needn't handle non-finite values.
Results may differ from the reference program's by a relative error of at most 0.014.
Values may be sent and summed in bfloat16 or wider, within the bound.
A program may use at most 192 MiB of HBM per device.

```python
import math
import jax
import jax.numpy as jnp
import numpy as np
from jax import lax

D = 768
HEAD_DIM = 64
FF = 3072
LEN = 512
DOCS = 4
SEQS = 64
TOKENS = 32768


def draw_tokens(key, part):
    key = jax.random.fold_in(key, 3)
    values = jax.random.truncated_normal(key, -4.0, 4.0, (TOKENS, D), jnp.float32)
    return values.astype(jnp.bfloat16)


def draw_valid(key, part):
    key = jax.random.fold_in(key, 5)
    levels = jax.random.randint(key, (SEQS, LEN), 0, 3 * SEQS)
    rising = SEQS + 2 * jnp.arange(SEQS, dtype=jnp.int32)[:, None]
    first = jnp.arange(LEN, dtype=jnp.int32)[None, :] == 0
    return jnp.where((levels < rising) | first, 1, 0).astype(jnp.int32)


def level_of(stream_key, dims, shards, low, largest):
    def one(axis_at, blocks):
        steps = jax.random.uniform(jax.random.fold_in(jax.random.fold_in(stream_key, 6), axis_at), (blocks,), jnp.float32, low / len(shards), largest / len(shards))
        return jnp.repeat(jnp.exp(steps), dims[axis_at] // blocks).reshape((-1,) + (1,) * (len(dims) - axis_at - 1))

    loudness = one(*shards[0])
    for cut in shards[1:]:
        loudness = loudness * one(*cut)
    return loudness


def profile(count, total, limit, skew):
    loads = [(1 << 20) // math.isqrt(grade ** skew) + 1 for grade in range(2, count + 1)]
    surplus, given = total - limit - (count - 1), [1] * (count - 1)
    while surplus > 0:
        free = [i for i in range(count - 1) if given[i] < limit]
        whole, left = sum([loads[i] for i in free]), surplus
        for i in free:
            more = min(limit - given[i], max(1, left * loads[i] // whole), surplus)
            given[i] = given[i] + more
            surplus = surplus - more
    return np.array([limit] + given)


def ragged_sizes(own_key, count, total, most, slope):
    if count == 2:
        one = jax.random.randint(own_key, (), max(1, total - most), min(most, total - 1) + 1)
        return jnp.stack([one, total - one])
    lengths = jnp.asarray(profile(count, total, most, slope), jnp.int32)
    couples = (count - 1) // 2
    giver, sink = lengths[1:1 + 2 * couples:2], lengths[2:2 + 2 * couples:2]
    room = jnp.minimum(giver - 1, most - sink)
    moved = jax.random.randint(jax.random.fold_in(own_key, 1), (couples,), 0, 1 << 20) % (room + 1)
    lengths = lengths.at[1:1 + 2 * couples:2].set(giver - moved).at[2:2 + 2 * couples:2].set(sink + moved)
    return lengths[jax.random.permutation(jax.random.fold_in(own_key, 2), count)]


def gaussian(rng, dims, scale, reach, shards=(), kind=jnp.bfloat16):
    drawn = scale * jax.random.normal(rng, dims, jnp.float32)
    if shards:
        drawn = drawn * level_of(rng, dims, shards, -0.22, 0.18)
    return jnp.clip(drawn, -reach, reach).astype(kind)


def setup_inputs(seed: int = 0) -> dict:
    arg_keys = jax.random.split(jax.random.key(seed), 18)
    tokens = draw_tokens(jax.random.fold_in(arg_keys[17], 71), 0)
    segment_ids = jax.vmap(lambda own: jnp.searchsorted(jnp.cumsum(ragged_sizes(own, DOCS, LEN, LEN // 2, 1)), jnp.arange(LEN), side="right"))(jax.random.split(arg_keys[1], SEQS)).reshape((SEQS, LEN)).astype(jnp.int32)
    valid = draw_valid(jax.random.fold_in(arg_keys[17], 71), 0)
    input_weight = gaussian(arg_keys[3], (D, 3 * D), D ** -0.5, 0.21875, ((0, 32),))
    query_bias = gaussian(arg_keys[4], (D,), 0.5, 3.0, ((0, 32),))
    value_bias = gaussian(arg_keys[5], (D,), 0.5, 3.0, ((0, 32),))
    output_weight = gaussian(arg_keys[6], (D, D), (D // 32) ** -0.5, 1.25, ((0, 32),))
    output_bias = gaussian(arg_keys[7], (D,), 0.5, 3.0, ((0, 32),))
    first_gain = jnp.clip(1.0 + 0.18 * jax.random.normal(arg_keys[8], (D,), jnp.float32), 0.099609375, 1.8984375).astype(jnp.bfloat16)
    first_shift = gaussian(arg_keys[9], (D,), 0.5, 3.0, ((0, 32),))
    expand_weight = gaussian(arg_keys[10], (D, FF), D ** -0.5, 0.21875, ((0, 32),))
    expand_bias = gaussian(arg_keys[11], (FF,), 0.5, 3.0, ((0, 32),))
    shrink_weight = gaussian(arg_keys[12], (FF, D), (FF // 2) ** -0.5, 0.15625, ((0, 32),))
    shrink_bias = gaussian(arg_keys[13], (D,), 0.5, 3.0, ((0, 32),))
    second_gain = jnp.clip(1.0 + 0.18 * jax.random.normal(arg_keys[14], (D,), jnp.float32), 0.099609375, 1.8984375).astype(jnp.bfloat16)
    second_shift = gaussian(arg_keys[15], (D,), 0.5, 3.0, ((0, 32),))
    cotangent = gaussian(arg_keys[16], (TOKENS, D), 1.0, 6.0, ((0, 32),))
    return {"tokens": tokens, "segment_ids": segment_ids, "valid": valid, "input_weight": input_weight, "query_bias": query_bias, "value_bias": value_bias, "output_weight": output_weight, "output_bias": output_bias, "first_gain": first_gain, "first_shift": first_shift, "expand_weight": expand_weight, "expand_bias": expand_bias, "shrink_weight": shrink_weight, "shrink_bias": shrink_bias, "second_gain": second_gain, "second_shift": second_shift, "cotangent": cotangent}


@jax.custom_vjp
def low(v):
    return lax.optimization_barrier(v.astype(jnp.bfloat16)).astype(jnp.float32)

@jax.custom_vjp
def low_back(v):
    return v

def low_keep(v):
    return (low(v), None)

def low_pass(kept, grad):
    return (grad,)

def back_keep(v):
    return (v, None)

def back_low(kept, grad):
    return (low(grad),)
low.defvjp(low_keep, low_pass)
low_back.defvjp(back_keep, back_low)
highest = lax.Precision.HIGHEST

def rounded_both(value):
    return low(low_back(value))

def layer_norm(value, gain, shift):
    centred = value - lax.optimization_barrier(jnp.mean(value, axis=-1, keepdims=True))
    spread = lax.optimization_barrier(jnp.mean(centred * centred, axis=-1, keepdims=True))
    return centred * lax.rsqrt(spread + 1e-12) * gain + shift

def gelu_exact(value):
    return 0.5 * value * (1.0 + lax.erf(value * 0.7071067811865476))

def attention_mask(segment_ids, valid):
    length = segment_ids.shape[1]
    same_doc = segment_ids[:, :, None] == segment_ids[:, None, :]
    diagonal = jnp.arange(length)[:, None] == jnp.arange(length)[None, :]
    return same_doc & ((valid[:, None, :] > 0) | diagonal[None])

def layer_forward(tokens, params, segment_ids, valid):
    input_weight, query_bias, value_bias, output_weight, output_bias, first_gain, first_shift, expand_weight, expand_bias, shrink_weight, shrink_bias, second_gain, second_shift = params
    sequences, length = segment_ids.shape
    features = tokens.shape[1]
    heads = features // HEAD_DIM
    shape_four = (sequences, length, heads, HEAD_DIM)
    combined = jnp.dot(tokens, input_weight, precision=highest)
    queries = rounded_both(combined[:, :features] + query_bias)
    key_rows = rounded_both(combined[:, features:2 * features])
    value_rows = rounded_both(combined[:, 2 * features:] + value_bias)
    raw_scores = jnp.einsum('sqhe,skhe->shqk', queries.reshape(shape_four), key_rows.reshape(shape_four), precision=highest) * HEAD_DIM ** (-0.5)
    allowed = attention_mask(segment_ids, valid)[:, None]
    scores = low_back(jnp.where(allowed, raw_scores, -1e+30))
    highest_score = lax.optimization_barrier(jnp.max(scores, axis=-1, keepdims=True))
    exponent = jnp.exp(scores - highest_score)
    probabilities = exponent / lax.optimization_barrier(jnp.sum(exponent, axis=-1, keepdims=True))
    attended = jnp.einsum('shqk,skhe->sqhe', low(probabilities), value_rows.reshape(shape_four), precision=highest)
    attended = rounded_both(attended.reshape(sequences * length, features))
    branch = low_back(jnp.dot(attended, output_weight, precision=highest) + output_bias)
    residual = tokens + branch
    normed = low(layer_norm(residual, first_gain, first_shift))
    hidden_pre = low_back(jnp.dot(normed, expand_weight, precision=highest) + expand_bias)
    activated = low(gelu_exact(hidden_pre))
    feedfwd = low_back(jnp.dot(activated, shrink_weight, precision=highest) + shrink_bias)
    second = normed + feedfwd
    result = layer_norm(second, second_gain, second_shift)
    counted = valid.reshape(-1).astype(jnp.float32)
    stat_sums = jnp.stack([jnp.sum(counted * lax.optimization_barrier(jnp.sum(jnp.square(low(member)), axis=-1))) for member in (residual, branch, second, feedfwd)])
    return (result, stat_sums)

def reference(tokens, segment_ids, valid, input_weight, query_bias, value_bias, output_weight, output_bias, first_gain, first_shift, expand_weight, expand_bias, shrink_weight, shrink_bias, second_gain, second_shift, cotangent):
    params = tuple((member.astype(jnp.float32) for member in (input_weight, query_bias, value_bias, output_weight, output_bias, first_gain, first_shift, expand_weight, expand_bias, shrink_weight, shrink_bias, second_gain, second_shift)))
    group_size = math.gcd(SEQS, max(1, 4096 // LEN))
    blocks = SEQS // group_size
    features = tokens.shape[1]
    token_blocks = tokens.astype(jnp.float32).reshape(blocks, group_size * LEN, features)
    cotangent_blocks = cotangent.astype(jnp.float32).reshape(blocks, group_size * LEN, features)
    segment_blocks = segment_ids.reshape(blocks, group_size, LEN)
    valid_blocks = valid.reshape(blocks, group_size, LEN)

    def one_block(carried, block_data):
        token_part, segment_part, valid_part, cotangent_part = block_data

        def forward(token_in, params_in):
            return layer_forward(token_in, params_in, segment_part, valid_part)
        result, pullback, block_sums = jax.vjp(forward, token_part, params, has_aux=True)
        token_grad, param_grads = pullback(cotangent_part)
        totals, stat_sums = carried
        return ((jax.tree.map(jnp.add, totals, param_grads), stat_sums + block_sums), (result.astype(jnp.bfloat16), token_grad))
    initial = (jax.tree.map(jnp.zeros_like, params), jnp.zeros((4,), jnp.float32))
    (gradients, stat_sums), (outputs, token_grads) = lax.scan(one_block, initial, (token_blocks, segment_blocks, valid_blocks, cotangent_blocks))
    valid_count = jnp.sum(valid.astype(jnp.float32))
    statistics = stat_sums / (features * valid_count)
    return (outputs.reshape(TOKENS, features), token_grads.reshape(TOKENS, features), statistics, gradients[0], gradients[1], gradients[2], gradients[3], gradients[4], gradients[5], gradients[6], gradients[7], gradients[8], gradients[9], gradients[10], gradients[11], gradients[12])
```

```python
import functools

import jax
import jax.numpy as jnp
from jax import lax
from jax.experimental import pallas as pl
from jax.experimental.pallas import tpu as pltpu
from jax.sharding import PartitionSpec as P

HEAD_DIM = 64
BLOCKS = 32

MESH = pl.DeviceIdType.MESH
ALL = slice(None)

class Net:
    def __init__(self, Z, Y):
        self.Z, self.Y = Z, Y
        dp, y = lax.axis_index("dp"), lax.axis_index("fsdp")
        self.fs = y
        self.at = {"z": dp // 4, "x": (dp // 2) % 2, "c": dp % 2, "y": y if Y == 2 else 0}
    def device(self, **moved):
        p = dict(self.at, **moved)
        return (p["z"] * 4 + p["x"] * 2 + p["c"], p["y"] if self.Y == 2 else self.fs)
    def across(self, axis):
        return self.device(**{axis: 1 - self.at[axis]})
    def barrier(self):
        bar = pltpu.get_barrier_semaphore()
        z, Z = self.at["z"], self.Z
        others = [self.across(axis) for axis in (["c", "x"] + (["y"] if self.Y == 2 else []))]
        others += [self.device(z=(z + k) % Z) for k in range(1, Z)]
        for other in others:
            pl.semaphore_signal(bar, inc=1, device_id=other, device_id_type=MESH)
        pl.semaphore_wait(bar, len(others))

def orders(Y):
    o = ["zxy", "xyz", "yzx"]
    return o if Y == 2 else [k.replace("y", "") for k in o]

def n_sems(Z):
    return 3 * 3 * 2 * max(1, Z - 1) + 1

def sem_id(Z, part, phase, step=0, down=0):
    return ((part * 3 + phase) * 2 + down) * max(1, Z - 1) + step

def gather_stages(net, buf, cols, ss, rs):
    Z, Y = net.Z, net.Y
    at = net.at
    def ref(idx, col):
        return buf.at[at["c"], idx["x"], idx["y"], idx["z"], :, pl.ds(*col)]
    def copy(idx, col, sem, device):
        r = ref(idx, col)
        return pltpu.make_async_remote_copy(src_ref=r, dst_ref=r, send_sem=ss.at[sem], recv_sem=rs.at[sem], device_id=device, device_id_type=MESH)
    ords = orders(Y)
    chains = []
    for part, order in enumerate(ords):
        col = cols[part]
        if col[1] == 0:
            continue
        steps = []
        done = set()
        for phase, axis in enumerate(order):
            base = {k: (ALL if k in done else at[k]) for k in "xyz"}
            if axis != "z":
                def make(base=base, col=col, axis=axis, sem=sem_id(Z, part, phase)):
                    mk = lambda: copy(base, col, sem, net.across(axis))
                    return (lambda: mk().start(), lambda: mk().wait_recv(), lambda: mk().wait_send())
                steps.append((phase, make()))
            else:
                for s in range(Z - 1):
                    def make(base=base, col=col, s=s, su=sem_id(Z, part, phase, s, 0), sd=sem_id(Z, part, phase, s, 1)):
                        z = at["z"]
                        up = lambda: copy(dict(base, z=z - s), col, su, net.device(z=z + 1))
                        dn = lambda: copy(dict(base, z=z + s), col, sd, net.device(z=z - 1))
                        can_up = (z - s >= 0) & (z + 1 < Z)
                        can_dn = (z + s < Z) & (z > 0)
                        ru = lambda: copy(dict(base, z=z - 1 - s), col, su, net.device(z=z - 1))
                        rd = lambda: copy(dict(base, z=z + 1 + s), col, sd, net.device(z=z + 1))
                        got_u, got_d = z - 1 - s >= 0, z + 1 + s < Z
                        def start():
                            pl.when(can_up)(lambda: up().start())
                            pl.when(can_dn)(lambda: dn().start())
                        def recv():
                            pl.when(got_u)(lambda: ru().wait_recv())
                            pl.when(got_d)(lambda: rd().wait_recv())
                        def send():
                            pl.when(can_up)(lambda: up().wait_send())
                            pl.when(can_dn)(lambda: dn().wait_send())
                        return start, recv, send
                    steps.append((phase, make()))
            done.add(axis)
        chains.append(steps)
    whole = cols[3]
    core_sem = n_sems(Z) - 1
    def core_copy():
        r = buf.at[at["c"], :, :, :, :, pl.ds(*whole)]
        return pltpu.make_async_remote_copy(src_ref=r, dst_ref=r, send_sem=ss.at[core_sem], recv_sem=rs.at[core_sem], device_id=net.across("c"), device_id_type=MESH)
    def core_recv():
        r = buf.at[1 - at["c"], :, :, :, :, pl.ds(*whole)]
        return pltpu.make_async_remote_copy(src_ref=r, dst_ref=r, send_sem=ss.at[core_sem], recv_sem=rs.at[core_sem], device_id=net.across("c"), device_id_type=MESH)
    return chains, core_copy, core_recv

def run_sync(chains):
    stages = []
    for phase in range(3):
        subs = [[st for ph, st in ch if ph == phase] for ch in chains]
        n = max(len(s) for s in subs)
        for k in range(n):
            def stage(k=k, subs=subs):
                for s in subs:
                    if k < len(s):
                        if k > 0:
                            s[k - 1][1]()
                        s[k][0]()
            stages.append(stage)
        def last(subs=subs):
            for s in subs:
                if s:
                    s[-1][1]()
        stages.append(last)
    return stages

def run_async(chains):
    stages = []
    n = max(len(c) for c in chains)
    for k in range(n + 1):
        def stage(k=k):
            for ch in chains:
                if 0 < k <= len(ch):
                    ch[k - 1][1][1]()
                if k < len(ch):
                    ch[k][1][0]()
        stages.append(stage)
    return stages


def add_into(dst, src, lead):
    total = 1
    for n in lead:
        total *= n
    def one(i, carry):
        idx = []
        for n in reversed(lead):
            idx.append(i % n); i = i // n
        idx = tuple(reversed(idx))
        dst[idx] = (dst[idx].astype(jnp.float32) + src[idx].astype(jnp.float32)).astype(dst.dtype)
        return carry
    if total == 1:
        one(0, 0)
    else:
        lax.fori_loop(0, total, one, 0)

def scatter_scratch(Z, Y, cols, R=48):
    size = {"x": 2, "y": Y, "z": Z}
    out = []
    for part, order in enumerate(orders(Y)):
        w = cols[part][1]
        out.append(pltpu.VMEM((2, Y, Z, R, w), jnp.bfloat16))
        free = [k for k in order]
        for axis in reversed(order):
            free.remove(axis)
            lead = tuple(size[k] for k in "xyz" if k in free)
            if axis == "z":
                out.append(pltpu.VMEM((2, Z - 1) + lead + (R, w), jnp.bfloat16))
            else:
                out.append(pltpu.VMEM(lead + (R, w), jnp.bfloat16))
    return out

def scatter_chains(net, buf, cols, scratch, ss, rs):
    Z, Y = net.Z, net.Y
    at = net.at
    size = {"x": 2, "y": Y, "z": Z}
    chains = []
    scratch = list(scratch)
    for part, order in enumerate(orders(Y)):
        col = pl.ds(*cols[part])
        bufs = [scratch.pop(0) for _ in range(len(order) + 1)]
        steps = []
        def ref(c, idx, col=col):
            return buf.at[c, idx["x"], idx["y"] if Y == 2 else 0, idx["z"], :, col]
        def rc(src, dst, sem, device):
            return pltpu.make_async_remote_copy(src_ref=src, dst_ref=dst, send_sem=ss.at[sem], recv_sem=rs.at[sem], device_id=device, device_id_type=MESH)
        def lead_of(free):
            return tuple(size[k] for k in "xyz" if k in free)
        allidx = {k: ALL for k in "xyz"}
        if Y != 2:
            allidx["y"] = 0
        def make_core(rb=bufs[0], part=part, ref=ref):
            sem = n_sems(Z) - 1 + part
            rbv = rb if Y == 2 else rb.at[:, 0]
            mk = lambda: rc(ref(1 - at["c"], allidx), rbv, sem, net.across("c"))
            def recv():
                mk().wait_recv()
                add_into(ref(at["c"], allidx), rbv, lead_of([k for k in "xyz" if k in order]))
            return (lambda: mk().start(), recv, lambda: mk().wait_send())
        steps.append((0, make_core()))
        free = list(order)
        for phase, axis in enumerate(reversed(order)):
            free.remove(axis)
            base = {k: (ALL if k in free else at[k]) for k in "xyz"}
            rb = bufs[1 + phase]
            lead = lead_of(free)
            if axis != "z":
                def make(base=base, axis=axis, rb=rb, lead=lead, sem=sem_id(Z, part, phase), ref=ref):
                    mk = lambda: rc(ref(at["c"], dict(base, **{axis: 1 - at[axis]})), rb, sem, net.across(axis))
                    def recv():
                        mk().wait_recv()
                        add_into(ref(at["c"], dict(base, **{axis: at[axis]})), rb, lead)
                    return (lambda: mk().start(), recv, lambda: mk().wait_send())
                steps.append((phase + 1, make()))
            else:
                for s in range(Z - 1):
                    def make(base=base, rb=rb, lead=lead, s=s, su=sem_id(Z, part, phase, s, 0), sd=sem_id(Z, part, phase, s, 1), ref=ref):
                        z = at["z"]
                        zr = Z - 1 - z
                        can_up = (z <= s) & (z < Z - 1)
                        can_dn = (zr <= s) & (z > 0)
                        up = lambda: rc(ref(at["c"], dict(base, z=Z - 1 - s + z)), rb.at[0, s], su, net.device(z=z + 1))
                        dn = lambda: rc(ref(at["c"], dict(base, z=s - zr)), rb.at[1, s], sd, net.device(z=z - 1))
                        got_u = (z - 1 <= s) & (z > 0)
                        got_d = (zr - 1 <= s) & (zr > 0)
                        def start():
                            pl.when(can_up)(lambda: up().start())
                            pl.when(can_dn)(lambda: dn().start())
                        def recv():
                            @pl.when(got_u)
                            def _():
                                rc(ref(at["c"], dict(base, z=z)), rb.at[0, s], su, net.device(z=z - 1)).wait_recv()
                                add_into(ref(at["c"], dict(base, z=Z - 2 - s + z)), rb.at[0, s], lead)
                            @pl.when(got_d)
                            def _():
                                rc(ref(at["c"], dict(base, z=z)), rb.at[1, s], sd, net.device(z=z + 1)).wait_recv()
                                add_into(ref(at["c"], dict(base, z=s + 1 - zr)), rb.at[1, s], lead)
                        def send():
                            pl.when(can_up)(lambda: up().wait_send())
                            pl.when(can_dn)(lambda: dn().wait_send())
                        return start, recv, send
                    steps.append((phase + 1, make()))
        chains.append(steps)
    return chains

def run_sync4(chains):
    stages = []
    for phase in range(4):
        subs = [[st for ph, st in ch if ph == phase] for ch in chains]
        n = max(len(s) for s in subs)
        for k in range(n):
            def stage(k=k, subs=subs):
                for s in subs:
                    if k < len(s):
                        if k > 0:
                            s[k - 1][1]()
                        s[k][0]()
            stages.append(stage)
        def last(subs=subs):
            for s in subs:
                if s:
                    s[-1][1]()
        stages.append(last)
    return stages


def layer_norm(value, gain, shift):
    centred = value - jnp.mean(value, axis=-1, keepdims=True)
    spread = jnp.mean(centred * centred, axis=-1, keepdims=True)
    return centred * lax.rsqrt(spread + 1e-12) * gain + shift


def gelu_exact(value):
    return 0.5 * value * (1.0 + lax.erf(value * 0.7071067811865476))


def attention_mask(segment_ids, valid):
    length = segment_ids.shape[1]
    same_doc = segment_ids[:, :, None] == segment_ids[:, None, :]
    diagonal = jnp.arange(length)[:, None] == jnp.arange(length)[None, :]
    return same_doc & ((valid[:, None, :] > 0) | diagonal[None])


def head_scores(queries, key_rows, allowed):
    raw_scores = jnp.einsum(
        "sqhe,skhe->shqk", queries, key_rows, preferred_element_type=jnp.float32
    ) * HEAD_DIM ** (-0.5)
    return jnp.where(allowed[:, None], raw_scores, -1e30)


def forward_pass(params, tokens, segment_ids, valid):
    (
        input_weight,
        query_bias,
        value_bias,
        output_weight,
        output_bias,
        first_gain,
        first_shift,
        expand_weight,
        expand_bias,
        shrink_weight,
        shrink_bias,
        second_gain,
        second_shift,
    ) = params
    sequences, length = segment_ids.shape
    features = tokens.shape[1]
    heads = features // HEAD_DIM
    shape_four = (sequences, length, heads, HEAD_DIM)
    combined = jnp.dot(tokens, input_weight, preferred_element_type=jnp.float32)
    queries = (
        (combined[:, :features] + query_bias.astype(jnp.float32))
        .astype(jnp.bfloat16)
        .reshape(shape_four)
    )
    key_rows = combined[:, features : 2 * features].astype(jnp.bfloat16).reshape(shape_four)
    value_rows = (
        (combined[:, 2 * features :] + value_bias.astype(jnp.float32))
        .astype(jnp.bfloat16)
        .reshape(shape_four)
    )
    allowed = attention_mask(segment_ids, valid)
    scores = head_scores(queries, key_rows, allowed)
    highest_score = jnp.max(scores, axis=-1, keepdims=True)
    exponent = jnp.exp(scores - highest_score)
    row_totals = jnp.sum(exponent, axis=-1, keepdims=True)
    log_total = highest_score + jnp.log(row_totals)
    weights_low = (exponent / row_totals).astype(jnp.bfloat16)
    attended = jnp.einsum(
        "shqk,skhe->sqhe", weights_low, value_rows, preferred_element_type=jnp.float32
    )
    attended = attended.astype(jnp.bfloat16).reshape(sequences * length, features)
    branch = jnp.dot(
        attended, output_weight, preferred_element_type=jnp.float32
    ) + output_bias.astype(jnp.float32)
    residual = tokens.astype(jnp.float32) + branch
    normed = layer_norm(
        residual, first_gain.astype(jnp.float32), first_shift.astype(jnp.float32)
    ).astype(jnp.bfloat16)
    hidden_pre = jnp.dot(
        normed, expand_weight, preferred_element_type=jnp.float32
    ) + expand_bias.astype(jnp.float32)
    activated = gelu_exact(hidden_pre).astype(jnp.bfloat16)
    feedfwd = jnp.dot(
        activated, shrink_weight, preferred_element_type=jnp.float32
    ) + shrink_bias.astype(jnp.float32)
    second = normed.astype(jnp.float32) + feedfwd
    result = layer_norm(second, second_gain.astype(jnp.float32), second_shift.astype(jnp.float32))
    counted = valid.reshape(-1).astype(jnp.float32)
    stat_sums = jnp.stack(
        [
            jnp.sum(
                counted
                * jnp.sum(jnp.square(member.astype(jnp.bfloat16).astype(jnp.float32)), axis=-1)
            )
            for member in (residual, branch, second, feedfwd)
        ]
    )
    stored = (
        queries,
        key_rows,
        value_rows,
        allowed,
        log_total,
        attended,
        residual,
        normed,
        hidden_pre,
        activated,
        second,
    )
    return (result, stat_sums, stored)


def backward_pass(params, tokens, stored, cotangent):
    (
        input_weight,
        query_bias,
        value_bias,
        output_weight,
        output_bias,
        first_gain,
        first_shift,
        expand_weight,
        expand_bias,
        shrink_weight,
        shrink_bias,
        second_gain,
        second_shift,
    ) = params
    (
        queries,
        key_rows,
        value_rows,
        allowed,
        log_total,
        attended,
        residual,
        normed,
        hidden_pre,
        activated,
        second,
    ) = stored
    features = tokens.shape[1]
    flat_shape = (tokens.shape[0], features)
    scale = HEAD_DIM ** (-0.5)
    second_value, second_pull = jax.vjp(
        layer_norm, second, second_gain.astype(jnp.float32), second_shift.astype(jnp.float32)
    )
    second_grad, second_gain_grad, second_shift_grad = second_pull(cotangent.astype(jnp.float32))
    feedfwd_grad = second_grad.astype(jnp.bfloat16)
    shrink_bias_grad = jnp.sum(feedfwd_grad, axis=0, dtype=jnp.float32)
    shrink_weight_grad = jnp.dot(activated.T, feedfwd_grad, preferred_element_type=jnp.float32)
    activated_grad = jnp.dot(feedfwd_grad, shrink_weight.T, preferred_element_type=jnp.float32)
    gelu_value, gelu_pull = jax.vjp(gelu_exact, hidden_pre)
    hidden_grad = gelu_pull(activated_grad)[0].astype(jnp.bfloat16)
    expand_bias_grad = jnp.sum(hidden_grad, axis=0, dtype=jnp.float32)
    expand_weight_grad = jnp.dot(normed.T, hidden_grad, preferred_element_type=jnp.float32)
    normed_grad = second_grad + jnp.dot(
        hidden_grad, expand_weight.T, preferred_element_type=jnp.float32
    )
    first_value, first_pull = jax.vjp(
        layer_norm, residual, first_gain.astype(jnp.float32), first_shift.astype(jnp.float32)
    )
    residual_grad, first_gain_grad, first_shift_grad = first_pull(normed_grad)
    branch_grad = residual_grad.astype(jnp.bfloat16)
    output_bias_grad = jnp.sum(branch_grad, axis=0, dtype=jnp.float32)
    output_weight_grad = jnp.dot(attended.T, branch_grad, preferred_element_type=jnp.float32)
    attended_grad = jnp.dot(branch_grad, output_weight.T, preferred_element_type=jnp.float32)
    attended_grad = attended_grad.astype(jnp.bfloat16).reshape(queries.shape)
    scores = head_scores(queries, key_rows, allowed)
    probabilities = jnp.exp(scores - log_total)
    weights_low = probabilities.astype(jnp.bfloat16)
    prob_grad = jnp.einsum(
        "sqhe,skhe->shqk", attended_grad, value_rows, preferred_element_type=jnp.float32
    )
    value_grad = jnp.einsum(
        "shqk,sqhe->skhe", weights_low, attended_grad, preferred_element_type=jnp.float32
    ).astype(jnp.bfloat16)
    inner = jnp.sum(probabilities * prob_grad, axis=-1, keepdims=True)
    score_grad = (probabilities * (prob_grad - inner)).astype(jnp.bfloat16)
    query_grad = (
        jnp.einsum("shqk,skhe->sqhe", score_grad, key_rows, preferred_element_type=jnp.float32)
        * scale
    ).astype(jnp.bfloat16)
    key_grad = (
        jnp.einsum("shqk,sqhe->skhe", score_grad, queries, preferred_element_type=jnp.float32)
        * scale
    ).astype(jnp.bfloat16)
    query_flat = query_grad.reshape(flat_shape)
    value_flat = value_grad.reshape(flat_shape)
    combined_grad = jnp.concatenate([query_flat, key_grad.reshape(flat_shape), value_flat], axis=1)
    query_bias_grad = jnp.sum(query_flat, axis=0, dtype=jnp.float32)
    value_bias_grad = jnp.sum(value_flat, axis=0, dtype=jnp.float32)
    input_weight_grad = jnp.dot(tokens.T, combined_grad, preferred_element_type=jnp.float32)
    token_grad = residual_grad + jnp.dot(
        combined_grad, input_weight.T, preferred_element_type=jnp.float32
    )
    gradients = (
        input_weight_grad,
        query_bias_grad,
        value_bias_grad,
        output_weight_grad,
        output_bias_grad,
        first_gain_grad,
        first_shift_grad,
        expand_weight_grad,
        expand_bias_grad,
        shrink_weight_grad,
        shrink_bias_grad,
        second_gain_grad,
        second_shift_grad,
    )
    return (token_grad, gradients)


def tiles_of(counts, first=0):
    out, at = [], first
    for count in counts:
        out.append((at * 128, count * 128))
        at += count
    return out + [(first * 128, sum(counts) * 128)]


GATHERED = tiles_of((14, 9, 14))
SCATTERED = tiles_of((14, 9, 13))


def gather_kernel(Z, Y, own_ref, all_ref, ss, rs, ls):
    net = Net(Z, Y)
    at = net.at
    own = all_ref.at[at["c"], at["x"], at["y"], at["z"]]
    load = pltpu.make_async_copy(own_ref, own, ls)
    load.start()
    net.barrier()
    load.wait()
    chains, core_copy, core_recv = gather_stages(net, all_ref, GATHERED, ss, rs)
    for stage in run_sync(chains):
        stage()
    core_copy().start()
    core_recv().wait_recv()
    for chain in chains:
        for _, step in chain:
            step[2]()
    core_copy().wait_send()


def gather_all(block, Z, Y):
    count = n_sems(Z)
    return pl.pallas_call(
        functools.partial(gather_kernel, Z, Y),
        out_shape=jax.ShapeDtypeStruct((2, 2, Y, Z) + block.shape, block.dtype),
        in_specs=[pl.BlockSpec(memory_space=pl.ANY)],
        out_specs=pl.BlockSpec(memory_space=pl.ANY),
        scratch_shapes=[
            pltpu.SemaphoreType.DMA((count,)),
            pltpu.SemaphoreType.DMA((count,)),
            pltpu.SemaphoreType.DMA,
        ],
        compiler_params=pltpu.CompilerParams(
            collective_id=0, has_side_effects=True, vmem_limit_bytes=60 * 2**20
        ),
        name="gather",
    )(block)


def small_steps(net, Z, Y):
    at = net.at
    out = [lambda: net.across("c"), lambda: net.across("x")]
    if Y == 2:
        out.append(lambda: net.across("y"))
    bit = 1
    while bit < Z:
        def partner(bit=bit):
            low = (at["z"] // bit) % 2
            return net.device(z=at["z"] + bit - 2 * bit * low)
        out.append(partner)
        bit *= 2
    return out


def scatter_kernel(Z, Y, parts_ref, small_ref, own_ref, sum_ref, buf, mine, theirs, ss, rs, sss, srs, ls, *scratch):
    net = Net(Z, Y)
    at = net.at
    load = pltpu.make_async_copy(parts_ref, buf, ls)
    load.start()
    mine[0] = small_ref[...]
    net.barrier()
    load.wait()
    chains = scatter_chains(net, buf, SCATTERED, scratch, ss, rs)
    stages = run_sync4(chains)
    partners = small_steps(net, Z, Y)
    copies = [
        pltpu.make_async_remote_copy(
            src_ref=mine.at[k], dst_ref=theirs.at[k], send_sem=sss.at[k], recv_sem=srs.at[k],
            device_id=partner(), device_id_type=MESH,
        )
        for k, partner in enumerate(partners)
    ]
    for k, stage in enumerate(stages):
        stage()
        if 0 < k <= len(copies):
            copies[k - 1].wait_recv()
            mine[k] = mine[k - 1] + theirs[k - 1]
        if k < len(copies):
            copies[k].start()
    sum_ref[...] = mine[len(copies)]
    for copy in copies:
        copy.wait_send()
    for chain in chains:
        for _, step in chain:
            step[2]()
    own_ref[...] = buf[at["c"], at["x"], at["y"], at["z"]].astype(jnp.float32)


def scatter_all(parts, small, Z, Y):
    count = n_sems(Z) + 3
    rounds = 2 + (Y == 2) + (Z - 1).bit_length()
    assert 2 ** (Z - 1).bit_length() == Z
    return pl.pallas_call(
        functools.partial(scatter_kernel, Z, Y),
        out_shape=(
            jax.ShapeDtypeStruct(parts.shape[4:], jnp.float32),
            jax.ShapeDtypeStruct(small.shape, jnp.float32),
        ),
        in_specs=[pl.BlockSpec(memory_space=pl.ANY), pl.BlockSpec(memory_space=pltpu.VMEM)],
        out_specs=[pl.BlockSpec(memory_space=pltpu.VMEM)] * 2,
        scratch_shapes=[
            pltpu.VMEM(parts.shape, jnp.bfloat16),
            pltpu.VMEM((rounds + 1,) + small.shape, jnp.float32),
            pltpu.VMEM((rounds,) + small.shape, jnp.float32),
            pltpu.SemaphoreType.DMA((count,)),
            pltpu.SemaphoreType.DMA((count,)),
            pltpu.SemaphoreType.DMA((rounds,)),
            pltpu.SemaphoreType.DMA((rounds,)),
            pltpu.SemaphoreType.DMA,
        ]
        + scatter_scratch(Z, Y, SCATTERED),
        compiler_params=pltpu.CompilerParams(
            collective_id=1, has_side_effects=True, vmem_limit_bytes=60 * 2**20
        ),
        name="scatter",
    )(parts, small)


def fold(rows):
    half = rows.shape[1] // 2
    return jnp.concatenate([rows[:, :half], rows[:, half:]], axis=0)


def per_device(
    Z,
    Y,
    fsdp,
    tokens,
    segment_ids,
    valid,
    input_weight,
    query_bias,
    value_bias,
    output_weight,
    output_bias,
    first_gain,
    first_shift,
    expand_weight,
    expand_bias,
    shrink_weight,
    shrink_bias,
    second_gain,
    second_shift,
    cotangent,
):
    vectors = (query_bias, value_bias, output_bias, first_gain, first_shift, shrink_bias, second_gain, second_shift)
    matrices = (input_weight, output_weight, expand_weight, shrink_weight)
    if Y == 1 and fsdp > 1:
        def whole(v):
            return lax.all_gather(v, "fsdp", axis=0, tiled=True)
        vectors, matrices, expand_bias = tuple(map(whole, vectors)), tuple(map(whole, matrices)), whole(expand_bias)
    rows = vectors[0].shape[0]
    features = tokens.shape[1]
    small = jnp.concatenate([jnp.stack(vectors), expand_bias.reshape(4, rows)], axis=0)
    small = jnp.pad(small, ((0, 2 * rows - 12), (0, 128 - rows)))
    last = matrices[3]
    last = jnp.concatenate([last[: 2 * rows], last[2 * rows :]], axis=1)
    block = jnp.concatenate([fold(matrices[0]), small, fold(matrices[1]), fold(matrices[2]), last], axis=1)
    gathered = gather_all(block, Z, Y)
    gathered = gathered.transpose(3, 1, 0, 2, 4, 5).reshape((BLOCKS,) + block.shape)

    def unfold(part):
        half = part.shape[2]
        return part.reshape(BLOCKS, 2, rows, half).transpose(0, 2, 1, 3).reshape(BLOCKS * rows, 2 * half)

    small = gathered[:, :12, 1152 : 1152 + rows]
    vector = small[:, :8].transpose(1, 0, 2).reshape(8, features)
    full_expand_bias = small[:, 8:].reshape(-1)
    full_last = gathered[:, :, 3200:].reshape(BLOCKS, 2 * rows, 2, features).transpose(0, 2, 1, 3).reshape(-1, features)
    params = (
        unfold(gathered[:, :, :1152]),
        vector[0],
        vector[1],
        unfold(gathered[:, :, 1280:1664]),
        vector[2],
        vector[3],
        vector[4],
        unfold(gathered[:, :, 1664:3200]),
        full_expand_bias,
        full_last,
        vector[5],
        vector[6],
        vector[7],
    )
    result, stat_sums, stored = forward_pass(params, tokens, segment_ids, valid)
    local_count = jnp.sum(valid, dtype=jnp.float32)
    token_grad, gradients = backward_pass(params, tokens, stored, cotangent)
    stats = jnp.pad(jnp.concatenate([stat_sums, local_count[None]]), (0, features - 5))
    small_grads = jnp.stack([gradients[k] for k in (1, 2, 4, 5, 6, 10, 11, 12)])
    small_grads = jnp.concatenate(
        [small_grads, gradients[8].reshape(4, features), stats[None], jnp.zeros((3, features), jnp.float32)]
    )

    def folded(grad):
        half = grad.shape[1] // 2
        return grad.reshape(BLOCKS, rows, 2, half).transpose(0, 2, 1, 3).reshape(BLOCKS, 2 * rows, half)

    last = gradients[9].reshape(BLOCKS, 2, 2 * rows, features).transpose(0, 2, 1, 3)
    parts = jnp.concatenate(
        [folded(gradients[0]), folded(gradients[3]), folded(gradients[7]), last.reshape(BLOCKS, 2 * rows, -1)],
        axis=2,
    ).astype(jnp.bfloat16)
    parts = parts.reshape((Z, 2, 2, Y) + parts.shape[1:]).transpose(2, 1, 3, 0, 4, 5)
    own, sums = scatter_all(parts, small_grads, Z, Y)

    def unfolded(part):
        return jnp.concatenate([part[:rows], part[rows:]], axis=1)

    weights = [
        unfolded(own[:, :1152]),
        unfolded(own[:, 1152:1536]),
        unfolded(own[:, 1536:3072]),
        jnp.concatenate([own[:, 3072 : 3072 + features], own[:, 3072 + features :]], axis=0),
    ]
    device = lax.axis_index("dp") * Y
    if Y == 2:
        device = device + lax.axis_index("fsdp")
    mine = lax.dynamic_slice(sums, (0, device * rows), (8, rows))
    mine_expand = lax.dynamic_slice(sums[8:12].reshape(-1), (device * 4 * rows,), (4 * rows,))
    totals = sums[12, :5]
    vectors = [mine[k] for k in range(8)]
    if Y == 1 and fsdp > 1:
        def share(v):
            return lax.psum_scatter(v, "fsdp", scatter_dimension=0, tiled=True)
        weights = [share(v) for v in weights]
        vectors = [share(v) for v in vectors]
        mine_expand = share(mine_expand)
        totals = lax.psum(totals, "fsdp")
    statistics = totals[:4] / (features * totals[4])
    return (
        result.astype(jnp.bfloat16),
        token_grad,
        statistics,
        weights[0],
        vectors[0],
        vectors[1],
        weights[1],
        vectors[2],
        vectors[3],
        vectors[4],
        weights[2],
        mine_expand,
        weights[3],
        vectors[5],
        vectors[6],
        vectors[7],
    )


def solution(mesh):
    dp, fsdp = mesh.shape["dp"], mesh.shape["fsdp"]
    Z, Y = dp // 4, (2 if dp * fsdp == BLOCKS else 1)
    in_specs = (
        P(("dp", "fsdp"), None),
        P(("dp", "fsdp"), None),
        P(("dp", "fsdp"), None),
        P(("dp", "fsdp"), None),
        P(("dp", "fsdp")),
        P(("dp", "fsdp")),
        P(("dp", "fsdp"), None),
        P(("dp", "fsdp")),
        P(("dp", "fsdp")),
        P(("dp", "fsdp")),
        P(("dp", "fsdp"), None),
        P(("dp", "fsdp")),
        P(("dp", "fsdp"), None),
        P(("dp", "fsdp")),
        P(("dp", "fsdp")),
        P(("dp", "fsdp")),
        P(("dp", "fsdp"), None),
    )
    out_specs = (
        P(("dp", "fsdp"), None),
        P(("dp", "fsdp"), None),
        P(),
        P(("dp", "fsdp"), None),
        P(("dp", "fsdp")),
        P(("dp", "fsdp")),
        P(("dp", "fsdp"), None),
        P(("dp", "fsdp")),
        P(("dp", "fsdp")),
        P(("dp", "fsdp")),
        P(("dp", "fsdp"), None),
        P(("dp", "fsdp")),
        P(("dp", "fsdp"), None),
        P(("dp", "fsdp")),
        P(("dp", "fsdp")),
        P(("dp", "fsdp")),
    )
    return jax.shard_map(
        functools.partial(per_device, Z, Y, fsdp), mesh=mesh, in_specs=in_specs, out_specs=out_specs, check_vma=False
    )
```

```python
import functools

import jax
import jax.numpy as jnp
from jax import lax
from jax.experimental import pallas as pl
from jax.experimental.pallas import tpu as pltpu
from jax.sharding import PartitionSpec as P

BLOCKS = 32
F32, BF16 = jnp.float32, jnp.bfloat16
LOG2E = 1.4426950408889634
MESH = pl.DeviceIdType.MESH
ALL = slice(None)
ANY = pl.BlockSpec(memory_space=pl.ANY)
VMEM = pl.BlockSpec(memory_space=pltpu.VMEM)
SDS = jax.ShapeDtypeStruct
DMA = pltpu.SemaphoreType.DMA
NT = (((1,), (1,)), ((), ()))
TN = (((0,), (0,)), ((), ()))
NN = (((1,), (0,)), ((), ()))
D, FF, LEN, PAIRS = 768, 3072, 512, 6
ROWS = 256


def tiles_of(counts):
    out, at = [], 0
    for count in counts:
        out.append((at * 128, count * 128))
        at += count
    return tuple(out)


def dot(a, b, dims=NN):
    return lax.dot_general(a, b, dims, preferred_element_type=F32)


def aligned(at, step, size=None):
    return pl.ds(pl.multiple_of(at * step, step), step if size is None else size)


def loop(count, body):
    def step(i, carry):
        body(i)
        return carry

    lax.fori_loop(0, count, step, 0)


def cost(flops, moved, exps=0):
    return pl.CostEstimate(flops=int(flops), bytes_accessed=int(moved), transcendentals=int(exps))


VMEM_LIMIT = 62 * 2**20


class Net:
    def __init__(self, Z, Y):
        self.Z, self.Y = Z, Y
        dp, y = lax.axis_index("dp"), lax.axis_index("fsdp")
        self.fsdp = y
        self.at = {"z": dp // 4, "x": (dp // 2) % 2, "c": dp % 2, "y": y if Y == 2 else 0}
        self.size = {"z": Z, "x": 2, "y": Y}
        self.orders = ["zxy", "xyz", "yzx"] if Y == 2 else ["zx", "xz", "zx"]
        self.own = dp * Y + (y if Y == 2 else 0)

    def device(self, **moved):
        p = dict(self.at, **moved)
        return (p["z"] * 4 + p["x"] * 2 + p["c"], p["y"] if self.Y == 2 else self.fsdp)

    def across(self, axis):
        return self.device(**{axis: 1 - self.at[axis]})

    def barrier(self):
        bar = pltpu.get_barrier_semaphore()
        z, Z = self.at["z"], self.Z
        others = [self.across(axis) for axis in (["c", "x", "y"] if self.Y == 2 else ["c", "x"])]
        others += [self.device(z=(z + k) % Z) for k in range(1, Z)]
        for other in others:
            pl.semaphore_signal(bar, inc=1, device_id=other, device_id_type=MESH)
        pl.semaphore_wait(bar, len(others))

    def place(self, i):
        Y = self.Y
        return ((i // Y) % 2, (i // (2 * Y)) % 2, i % Y, i // (4 * Y))

    def mine(self):
        at = self.at
        return (at["c"], at["x"], at["y"], at["z"])


def sem_count(Z):
    return 18 * (Z - 1) + 3


def sem_at(Z, part, phase, step=0, down=0):
    return ((part * 3 + phase) * 2 + down) * (Z - 1) + step


def remote(src, dst, sems, sem, device):
    return pltpu.make_async_remote_copy(
        src_ref=src,
        dst_ref=dst,
        send_sem=sems[0].at[sem],
        recv_sem=sems[1].at[sem],
        device_id=device,
        device_id_type=MESH,
    )


def gather_chains(net, buf, cols, sems):
    Z, at = net.Z, net.at
    chains = []
    for part, order in enumerate(net.orders):
        col = pl.ds(*cols[part])

        def block(core, idx, col=col):
            return buf.at[core, idx["x"], idx["y"], idx["z"], :, col]

        chain, done = [], set()
        for phase, axis in enumerate(order):
            base = {k: (ALL if k in done else at[k]) for k in "xyz"}
            for step in range(Z - 1 if axis == "z" else 1):
                up_sem, down_sem = (sem_at(Z, part, phase, step, d) for d in (0, 1))

                def swap(axis=axis, base=base, block=block, sem=up_sem):
                    def copy():
                        r = block(at["c"], base)
                        return remote(r, r, sems, sem, net.across(axis))

                    return lambda: copy().start(), lambda: copy().wait_recv(), lambda: copy().wait_send()

                def line(base=base, block=block, step=step, us=up_sem, ds=down_sem):
                    z = at["z"]

                    def copy(from_z, sem, to_z):
                        r = block(at["c"], dict(base, z=from_z))
                        return remote(r, r, sems, sem, net.device(z=to_z))

                    sends = (
                        ((z >= step) & (z + 1 < Z), lambda: copy(z - step, us, z + 1)),
                        ((z + step < Z) & (z > 0), lambda: copy(z + step, ds, z - 1)),
                    )
                    takes = (
                        (z - 1 - step >= 0, lambda: copy(z - 1 - step, us, z - 1)),
                        (z + 1 + step < Z, lambda: copy(z + 1 + step, ds, z + 1)),
                    )

                    def start():
                        for cond, make in sends:
                            pl.when(cond)(lambda make=make: make().start())

                    def receive():
                        for cond, make in takes:
                            pl.when(cond)(lambda make=make: make().wait_recv())

                    def sent():
                        for cond, make in sends:
                            pl.when(cond)(lambda make=make: make().wait_send())

                    return start, receive, sent

                chain.append((phase, line() if axis == "z" else swap()))
            done.add(axis)

        def core(block=block, sem=sem_count(Z) - 3 + part):
            every = {k: ALL for k in "xyz"}

            def copy(c):
                r = block(c, every)
                return remote(r, r, sems, sem, net.across("c"))

            c = at["c"]
            return lambda: copy(c).start(), lambda: copy(1 - c).wait_recv(), lambda: copy(c).wait_send()

        chain.append((len(order), core()))
        chains.append(chain)
    return chains


def add_into(dst, src, lead):
    total = 1
    for n in lead:
        total *= n

    def one(i):
        idx = []
        for n in reversed(lead):
            idx.append(i % n)
            i = i // n
        idx = tuple(reversed(idx))
        dst[idx] = (dst[idx].astype(F32) + src[idx].astype(F32)).astype(dst.dtype)

    if total == 1:
        one(0)
    else:
        loop(total, one)


def scatter_scratch(net_sizes, cols, rows=48):
    Z, Y = net_sizes
    size = {"x": 2, "y": Y, "z": Z}
    orders = ["zxy", "xyz", "yzx"] if Y == 2 else ["zx", "xz", "zx"]
    out = []
    for part, order in enumerate(orders):
        width = cols[part][1]
        free = list(order)
        out.append(pltpu.VMEM(tuple(size[k] for k in "xyz" if k in free) + (rows, width), BF16))
        for axis in reversed(order):
            free.remove(axis)
            lead = tuple(size[k] for k in "xyz" if k in free)
            if axis == "z":
                lead = (2, Z - 1) + lead
            out.append(pltpu.VMEM(lead + (rows, width), BF16))
    return out


def scatter_chains(net, buf, cols, scratch, sems):
    Z, at = net.Z, net.at
    scratch = list(scratch)
    chains = []
    for part, order in enumerate(net.orders):
        col = pl.ds(*cols[part])
        arrive = [scratch.pop(0) for _ in range(len(order) + 1)]

        def block(core, idx, col=col):
            return buf.at[core, idx["x"], idx.get("y", 0), idx["z"], :, col]

        def lead_of(free):
            return tuple(net.size[k] for k in "xyz" if k in free)

        def swap(send, keep, land, sem, device, lead):
            def copy():
                return remote(send(), land, sems, sem, device())

            def receive():
                copy().wait_recv()
                add_into(keep(), land, lead)

            return lambda: copy().start(), receive, lambda: copy().wait_send()

        every = {k: ALL for k in order}
        chain = [
            (
                0,
                swap(
                    lambda block=block, every=every: block(1 - at["c"], every),
                    lambda block=block, every=every: block(at["c"], every),
                    arrive[0],
                    sem_count(Z) - 3 + part,
                    lambda: net.across("c"),
                    lead_of(order),
                ),
            )
        ]
        free = list(order)
        for phase, axis in enumerate(reversed(order)):
            free.remove(axis)
            base = {k: (ALL if k in free else at[k]) for k in order}
            land, lead = arrive[1 + phase], lead_of(free)
            if axis != "z":
                chain.append(
                    (
                        phase + 1,
                        swap(
                            lambda block=block, base=base, axis=axis: block(at["c"], dict(base, **{axis: 1 - at[axis]})),
                            lambda block=block, base=base, axis=axis: block(at["c"], dict(base, **{axis: at[axis]})),
                            land,
                            sem_at(Z, part, phase),
                            lambda axis=axis: net.across(axis),
                            lead,
                        ),
                    )
                )
                continue
            for step in range(Z - 1):
                us, ds = (sem_at(Z, part, phase, step, d) for d in (0, 1))

                def line(base=base, block=block, step=step, us=us, ds=ds, land=land, lead=lead):
                    z = at["z"]
                    zr = Z - 1 - z

                    def copy(d, way, sem, to_z):
                        return remote(block(at["c"], dict(base, z=d)), land.at[way, step], sems, sem, net.device(z=to_z))

                    sends = (
                        ((z <= step) & (z < Z - 1), lambda: copy(Z - 1 - step + z, 0, us, z + 1)),
                        ((zr <= step) & (z > 0), lambda: copy(step - zr, 1, ds, z - 1)),
                    )
                    takes = (
                        ((z - 1 <= step) & (z > 0), lambda: copy(z, 0, us, z - 1), Z - 2 - step + z, 0),
                        ((zr - 1 <= step) & (zr > 0), lambda: copy(z, 1, ds, z + 1), step + 1 - zr, 1),
                    )

                    def start():
                        for cond, make in sends:
                            pl.when(cond)(lambda make=make: make().start())

                    def receive():
                        for cond, make, d, way in takes:

                            @pl.when(cond)
                            def _(make=make, d=d, way=way):
                                make().wait_recv()
                                add_into(block(at["c"], dict(base, z=d)), land.at[way, step], lead)

                    def sent():
                        for cond, make in sends:
                            pl.when(cond)(lambda make=make: make().wait_send())

                    return start, receive, sent

                chain.append((phase + 1, line()))
        chains.append(chain)
    return chains


def phased(chains):
    calls, pending = [], [None] * len(chains)
    for phase in range(1 + max(ph for chain in chains for ph, _ in chain)):
        subs = [[step for ph, step in chain if ph == phase] for chain in chains]
        for k in range(max(len(sub) for sub in subs)):
            todo = []
            for j, sub in enumerate(subs):
                if k < len(sub):
                    if pending[j] is not None:
                        todo.append(pending[j])
                    todo.append(sub[k][0])
                    pending[j] = sub[k][1]
            calls.append(todo)
    calls.append([p for p in pending if p is not None])
    return [lambda todo=todo: [call() for call in todo] and None for todo in calls]


def eager(chains):
    calls = []
    for k in range(1 + max(map(len, chains))):
        todo = []
        for chain in chains:
            if 0 < k <= len(chain):
                todo.append(chain[k - 1][1][1])
            if k < len(chain):
                todo.append(chain[k][1][0])
        calls.append(todo)
    return [lambda todo=todo: [call() for call in todo] and None for todo in calls]


def finish(chains):
    for chain in chains:
        for _, step in chain:
            step[2]()


def spread(i, first, calls, every=1):
    for k, call in enumerate(calls):
        pl.when(i == first + k * every)(call)


def head_mask(head, shape):
    lane = lax.broadcasted_iota(jnp.int32, shape, len(shape) - 1)
    return (lane < 64) if head == 0 else (lane >= 64)


def column(row, count=128):
    return jnp.broadcast_to(row, (count, row.shape[1])).T


def build_mask(mask, down, across):
    n = mask.shape[0]
    down = column(down)
    at = lax.broadcasted_iota(jnp.int32, (n, 128), 0)
    lane = lax.broadcasted_iota(jnp.int32, (n, 128), 1)
    for j in range(n // 128):
        tile = slice(j * 128, (j + 1) * 128)
        mask[:, tile] = jnp.where((down == across[:, tile]) | (at == lane + j * 128), 0.0, -1e30)


def gelu_pair(h):
    t = 1.0 / (1.0 + (0.3275911 * 0.7071067811865476) * jnp.abs(h))
    e = jnp.exp2(h * h * (-0.5 * LOG2E))
    poly = t * (
        0.5 * 0.254829592
        + t * (0.5 * -0.284496736 + t * (0.5 * 1.421413741 + t * (0.5 * -1.453152027 + t * (0.5 * 1.061405429))))
    )
    tail = poly * e
    cdf = jnp.where(h >= 0, 1.0 - tail, tail)
    return h * cdf, cdf + h * e * 0.3989422804014327


def normalise(v):
    centred = v - jnp.sum(v, axis=1, keepdims=True) * (1.0 / D)
    r = lax.rsqrt(jnp.sum(centred * centred, axis=1, keepdims=True) * (1.0 / D) + 1e-12)
    return centred * r, r


def norm_back(g, n, r, gain):
    scaled = g * gain
    mean = jnp.sum(scaled, axis=1, keepdims=True) * (1.0 / D)
    along = jnp.sum(scaled * n, axis=1, keepdims=True) * (1.0 / D)
    return r * (scaled - mean - n * along)


def down_sum(v):
    return jnp.sum(v, axis=0, keepdims=True)


def square_sum(value, counted):
    v = value.astype(BF16).astype(F32)
    v = v * v
    total = v[:, :128]
    for j in range(1, D // 128):
        total = total + v[:, j * 128 : (j + 1) * 128]
    return down_sum(total * counted)


def fold_own(shard, half):
    v = shard.astype(F32)
    return jnp.concatenate([v[:, :half], v[:, half:]], axis=0).astype(BF16)


def unfold(net, buf, first, half, dst):
    def pair(p):
        cols = slice(first, first + half)
        a = buf[net.place(2 * p) + (ALL, cols)].astype(F32)
        b = buf[net.place(2 * p + 1) + (ALL, cols)].astype(F32)
        rows = aligned(p, 48)
        dst[rows, :half] = jnp.concatenate([a[:24], b[:24]], axis=0).astype(BF16)
        dst[rows, half:] = jnp.concatenate([a[24:], b[24:]], axis=0).astype(BF16)

    loop(BLOCKS // 2, pair)


PLACES = {"qb": (1, 0), "vb": (1, 1), "ob": (1, 2), "fg": (1, 3), "fs": (2, 0), "sb": (2, 1), "sg": (2, 2), "ss": (2, 3)}


def add_small(small, name, value):
    row, at = PLACES[name]
    small[row : row + 1, at * D : (at + 1) * D] += value


def small_window(net, vectors, expand, tmp):
    tmp[...] = jnp.zeros_like(tmp)
    for k, ref in enumerate(vectors):
        tmp[k : k + 1, : 24] = ref[...].astype(F32)
    tmp[8:9, : 96] = expand[...].astype(F32)
    i = net.own
    v = pltpu.roll(tmp[0:8, :], (24 * i) % 128, axis=1)
    e = pltpu.roll(tmp[8:16, :], (96 * i) % 128, axis=1)
    both = jnp.concatenate([v, e], axis=0)
    return jnp.concatenate([both[:, :128], both[:, 128:]], axis=0).astype(BF16)


def small_params(net, buf, first, vec, exp):
    vec[...] = jnp.zeros_like(vec)
    exp[...] = jnp.zeros_like(exp)
    for i in range(BLOCKS):
        w = buf[net.place(i) + (slice(0, 32), slice(first, first + 128))].astype(F32)
        for ref, rows, tile in ((vec, 0, 24 * i // 128), (exp, 8, 96 * i // 128)):
            for k in range(2):
                if (tile + k) * 128 < ref.shape[1]:
                    ref[:, (tile + k) * 128 : (tile + k + 1) * 128] += w[16 * k + rows : 16 * k + rows + 8]


def project(x, w, vec, qkv):
    def body(i):
        r = aligned(i, ROWS)
        xv = x[r, :]
        for j in range(3):
            c = dot(xv, w[:, j * D : (j + 1) * D])
            if j != 1:
                c = c + vec[j // 2 : j // 2 + 1, :]
            c = c.astype(BF16)
            for p in range(PAIRS):
                qkv[j * PAIRS + p, r, :] = c[:, p * 128 : (p + 1) * 128]

    return body


def attend(qkv, mask, att, lse, seq, p):
    base = pl.multiple_of(seq * LEN, LEN)
    q, k, v = (qkv[j * PAIRS + p, pl.ds(base, LEN), :] for j in range(3))
    lane = lax.broadcasted_iota(jnp.int32, (LEN, 128), 1)
    out, logs = None, lse[pl.ds(base, LEN), :]
    for head in range(2):
        here = head_mask(head, k.shape)
        km, vm = jnp.where(here, k, jnp.zeros_like(k)), jnp.where(here, v, jnp.zeros_like(v))
        t = dot(q, km, NT) * (0.125 * LOG2E) + mask[seq]
        top = jnp.max(t, axis=1, keepdims=True)
        e = jnp.exp2(t - top)
        total = jnp.sum(e, axis=1, keepdims=True)
        o = dot(e.astype(BF16), vm) * (1.0 / total)
        out = o if out is None else out + o
        logs = jnp.where(lane == 2 * p + head, top + jnp.log2(total), logs)
    lse[pl.ds(base, LEN), :] = logs
    att[pl.ds(base, LEN), aligned(p, 128)] = out.astype(BF16)


def forward_kernel(Z, Y, groups, *refs):
    (x_h, cot_h, codes, w_in_s, w_out_s, w1_s, w2_s, qb, vb, ob, fg, fs, eb, sb, sg, ss_) = refs[:16]
    (res_h, qkv_h, att_h, normed_h, act_h, gp_h, df_h, lse_h, w_in_h, w_out_h, w1_h, w2_h, result_h, dsec_h, vec, small) = refs[16:32]
    (g1, g2, g3, w_in, w_out, w1, w2, x, qkv, mask, att, lse, lse_rows, wide, normed, act, gp, cot, exp, tmp, s1, r1, s2, r2, s3, r3, loads, outs, gsem) = refs[32:]
    net = Net(Z, Y)
    T = x.shape[0]
    seqs = T // LEN
    blocks = T // ROWS

    load_x = pltpu.make_async_copy(x_h, x, loads.at[0])
    load_x.start()
    load_cot = pltpu.make_async_copy(cot_h, cot, loads.at[1])
    load_cot.start()
    mine = net.mine()
    g1[mine + (ALL, slice(0, 1152))] = fold_own(w_in_s[...], 1152)
    g1[mine + (slice(0, 32), slice(1152, 1280))] = small_window(net, (qb, vb, ob, fg, fs, sb, sg, ss_), eb, tmp)
    g1[mine + (slice(32, 48), slice(1152, 1280))] = jnp.zeros((16, 128), BF16)
    net.barrier()
    chains = [gather_chains(net, g, cols, s) for g, cols, s in zip((g1, g2, g3), groups, ((s1, r1), (s2, r2), (s3, r3)))]
    first = eager(chains[0])
    first[0]()
    g2[mine + (ALL, slice(0, 384))] = fold_own(w_out_s[...], 384)
    g2[mine + (ALL, slice(384, 1920))] = fold_own(w1_s[...], 1536)
    g3[mine + (ALL, slice(0, D))] = w2_s[0:48, :]
    g3[mine + (ALL, slice(D, 2 * D))] = w2_s[48:96, :]
    small[...] = jnp.zeros_like(small)
    for s in range(seqs):
        build_mask(mask.at[s], codes[s, 0:1, :], codes[s, 1:2, :])
        valid = codes[s, 2:3, :]
        small[3:4, 512:640] += sum(valid[:, j * 128 : (j + 1) * 128] for j in range(LEN // 128))
    lse[...] = jnp.zeros_like(lse)
    for call in first[1:]:
        call()
    calls = phased(chains[1]) + phased(chains[2])
    n2 = len(phased(chains[1]))
    calls[0]()
    unfold(net, g1, 0, 1152, w_in)
    small_params(net, g1, 1152, vec, exp)
    load_x.wait()
    do_project = project(x, w_in, vec, qkv)

    def project_step(i):
        spread(i, 1, calls[1:4])
        do_project(i)

    loop(blocks, project_step)
    stores = []

    def store(src, dst):
        copy = pltpu.make_async_copy(src, dst, outs.at[len(stores)])
        copy.start()
        stores.append(copy)
        return copy

    store(qkv, qkv_h)
    store(w_in, w_in_h)

    def attend_step(i):
        spread(i, 1, calls[4 : n2 + 2], 1)
        attend(qkv, mask, att, lse, i // PAIRS, i % PAIRS)

    loop(seqs * PAIRS, attend_step)
    store_att = store(att, att_h)
    for s in range(seqs):
        rows = lse[s * LEN : (s + 1) * LEN, :].T
        for h in range(2 * PAIRS):
            lse_rows[s * 2 * PAIRS + h] = jnp.broadcast_to(rows[h : h + 1, :], (8, LEN))
    store(lse_rows, lse_h)
    unfold(net, g2, 0, 384, w_out)
    unfold(net, g2, 384, 1536, w1)
    store(w_out, w_out_h)
    store(w1, w1_h)

    def counted(i):
        per = LEN // ROWS
        return column(codes[i // per, 2:3, aligned(i % per, ROWS)])

    def out_step(i):
        spread(i, 0, calls[n2 + 2 : n2 + 6])
        r = aligned(i, ROWS)
        branch = dot(att[r, :], w_out[...]) + vec[2:3, :]
        residual = x[r, :].astype(F32) + branch
        wide[r, :] = residual
        n, _ = normalise(residual)
        normed[r, :] = (n * vec[3:4, :] + vec[4:5, :]).astype(BF16)
        live = counted(i)
        small[3:4, 0:128] += square_sum(residual, live)
        small[3:4, 128:256] += square_sum(branch, live)

    loop(blocks, out_step)
    store_wide = store(wide, res_h)
    store(normed, normed_h)

    def gp_copy(i):
        return pltpu.make_async_copy(gp.at[i % 2], gp_h.at[aligned(i, ROWS), :], gsem.at[i % 2])

    def expand_step(i):
        spread(i, 0, calls[n2 + 6 : n2 + 10])
        pl.when(i >= 2)(lambda: gp_copy(i).wait())
        r = aligned(i, ROWS)
        nv = normed[r, :]
        for j in range(FF // 512):
            c = slice(j * 512, (j + 1) * 512)
            a, g = gelu_pair(dot(nv, w1[:, c]) + exp[0:1, c])
            act[r, c] = a.astype(BF16)
            gp[i % 2, :, c] = g.astype(BF16)
        gp_copy(i).start()

    loop(blocks, expand_step)
    store(act, act_h)
    for call in calls[n2 + 10 :]:
        call()

    def unfold_last(i):
        blk = g3.at[net.place(i)]
        w2[aligned(i, 96, 48), :] = blk[:, :D]
        w2[pl.ds(pl.multiple_of(i * 96 + 48, 48), 48), :] = blk[:, D:]

    loop(BLOCKS, unfold_last)
    store(w2, w2_h)
    store_wide.wait()
    store_att.wait()
    load_cot.wait()

    def last_step(i):
        r = aligned(i, ROWS)
        feedfwd = dot(act[r, :], w2[...]) + vec[5:6, :]
        second = normed[r, :].astype(F32) + feedfwd
        n, rs = normalise(second)
        gain = vec[6:7, :]
        att[r, :] = (n * gain + vec[7:8, :]).astype(BF16)
        g = cot[r, :].astype(F32)
        grad = norm_back(g, n, rs, gain)
        wide[r, :] = grad
        low = grad.astype(BF16)
        x[r, :] = low
        add_small(small, "sg", down_sum(g * n))
        add_small(small, "ss", down_sum(g))
        add_small(small, "sb", down_sum(low.astype(F32)))
        live = counted(i)
        small[3:4, 256:384] += square_sum(second, live)
        small[3:4, 384:512] += square_sum(feedfwd, live)

    loop(blocks, last_step)
    stores = [copy for copy in stores if copy is not store_wide and copy is not store_att]
    ends = [
        pltpu.make_async_copy(wide, dsec_h, loads.at[0]),
        pltpu.make_async_copy(att, result_h, loads.at[1]),
        pltpu.make_async_copy(x, df_h, loads.at[2]),
    ]
    for copy in ends:
        copy.start()
    for k in (0, 1):
        gp_copy(blocks - 2 + k).wait()
    for copy in stores + ends:
        copy.wait()
    for chain in chains:
        finish(chain)


def forward(Z, Y, x, cot, codes, shards, vectors):
    T, S = x.shape[0], codes.shape[0]
    w_in_s, w_out_s, w1_s, w2_s = shards
    groups = (tiles_of((4, 2, 4)), tiles_of((6, 4, 5)), tiles_of((5, 3, 4)))
    blocks = (2, 2, Y, Z, 48)
    outs = [
        SDS((T, D), F32), SDS((3 * PAIRS, T, 128), BF16), SDS((T, D), BF16), SDS((T, D), BF16),
        SDS((T, FF), BF16), SDS((T, FF), BF16), SDS((T, D), BF16), SDS((S * 12, 8, LEN), F32),
        SDS((D, 3 * D), BF16), SDS((D, D), BF16), SDS((D, FF), BF16), SDS((FF, D), BF16),
        SDS((T, D), BF16), SDS((T, D), F32), SDS((8, D), F32), SDS((8, FF), F32),
    ]
    scratch = [
        pltpu.VMEM(blocks + (1280,), BF16), pltpu.VMEM(blocks + (1920,), BF16), pltpu.VMEM(blocks + (1536,), BF16),
        pltpu.VMEM((D, 3 * D), BF16), pltpu.VMEM((D, D), BF16), pltpu.VMEM((D, FF), BF16), pltpu.VMEM((FF, D), BF16),
        pltpu.VMEM((T, D), BF16), pltpu.VMEM((3 * PAIRS, T, 128), BF16), pltpu.VMEM((S, LEN, LEN), F32),
        pltpu.VMEM((T, D), BF16), pltpu.VMEM((T, 128), F32), pltpu.VMEM((S * 12, 8, LEN), F32),
        pltpu.VMEM((T, D), F32), pltpu.VMEM((T, D), BF16), pltpu.VMEM((T, FF), BF16), pltpu.VMEM((2, ROWS, FF), BF16),
        pltpu.VMEM((T, D), BF16), pltpu.VMEM((8, FF), F32), pltpu.VMEM((16, 256), F32),
    ] + [DMA((sem_count(Z),))] * 6 + [DMA((3,)), DMA((16,)), DMA((2,))]
    return pl.pallas_call(
        functools.partial(forward_kernel, Z, Y, groups),
        out_shape=outs,
        in_specs=[ANY, ANY] + [VMEM] * 14,
        out_specs=[ANY] * 14 + [VMEM] * 2,
        scratch_shapes=scratch,
        compiler_params=pltpu.CompilerParams(collective_id=0, has_side_effects=True, vmem_limit_bytes=VMEM_LIMIT),
        name="forward",
    )(x, cot, codes, w_in_s, w_out_s, w1_s, w2_s, *vectors)


def pack(net, buf, cols, left, right):
    def owner(i):
        rows = aligned(i, 24)
        v = jnp.concatenate([left[rows, :], right[rows, :]], axis=0).astype(BF16)
        buf[net.place(i) + (ALL, cols)] = v

    loop(BLOCKS, owner)


def feed_back_kernel(Z, Y, cols, *refs):
    (act_h, gp_h, df_h, dsec_h, normed_h, res_h, att_h, w1_h, w2_h, w_out_h, vec, small_in) = refs[:12]
    (p1_h, po_h, do_h, dres_h, w2_own, small) = refs[12:18]
    (df, wide, normed, normed_t, att, res, w1, w2, w_out, act, gp, dh, dw, p1, po, p2, ss, rs, loads, chunks, outs) = refs[18:39]
    scratch = refs[39:]
    net = Net(Z, Y)
    T = df.shape[0]
    blocks = T // ROWS

    def load(src, dst, k):
        copy = pltpu.make_async_copy(src, dst, loads.at[k])
        copy.start()
        return copy

    def act_copy(j):
        return pltpu.make_async_copy(act_h.at[:, aligned(j, 384)], act.at[j % 2], chunks.at[j % 2])

    def gp_copies(j):
        return [
            pltpu.make_async_copy(
                gp_h.at[:, pl.ds(pl.multiple_of(side * 1536 + j * 384, 128), 384)],
                gp.at[j % 2, side],
                chunks.at[2 + 2 * side + j % 2],
            )
            for side in range(2)
        ]

    act_copy(0).start()
    load_df = load(df_h, df, 0)
    act_copy(1).start()
    load_w2 = load(w2_h, w2, 1)
    load_normed = load(normed_h, normed, 2)
    for j in range(2):
        for copy in gp_copies(j):
            copy.start()
    load_w1 = load(w1_h, w1, 3)
    load_dsec = load(dsec_h, wide, 4)
    load_rest = [load(res_h, res, 5), load(att_h, att, 6), load(w_out_h, w_out, 7)]
    small[...] = small_in[...]
    net.barrier()
    load_df.wait()

    def shrink_step(j):
        act_copy(j).wait()
        v = dot(act[j % 2], df[...], TN).astype(BF16)
        for k in range(4):
            place = net.place(4 * j + k)
            p2[place + (ALL, slice(0, D))] = v[96 * k : 96 * k + 48]
            p2[place + (ALL, slice(D, 2 * D))] = v[96 * k + 48 : 96 * k + 96]
        pl.when(j + 2 < FF // 384)(lambda: act_copy(j + 2).start())

    loop(FF // 384, shrink_step)
    chains = scatter_chains(net, p2, cols, scratch, (ss, rs))
    calls = phased(chains)
    calls[0]()
    load_normed.wait()

    def turn(j):
        lanes = aligned(j, 128)
        normed_t[lanes, :] = normed[:, lanes].T

    loop(D // 128, turn)
    load_w2.wait()
    load_w1.wait()
    load_dsec.wait()
    points = calls[1:]

    def expand_step(j):
        for copy in gp_copies(j):
            copy.wait()
        for side in range(2):
            spread(j, 0, points[side::3])
            c = pl.ds(pl.multiple_of(side * 1536 + j * 384, 128), 384)
            for i in range(blocks // 2):
                r = slice(i * 2 * ROWS, (i + 1) * 2 * ROWS)
                d = (dot(df[r, :], w2[c, :], NT) * gp[j % 2, side, r, :].astype(F32)).astype(BF16)
                dh[r, side * 384 : side * 384 + 384] = d
                wide[r, :] += dot(d, w1[:, c], NT)
            small[0:1, c] += down_sum(dh[:, side * 384 : side * 384 + 384].astype(F32))
        spread(j, 0, points[2::3])

        @pl.when(j + 2 < 4)
        def _():
            for copy in gp_copies(j + 2):
                copy.start()

        dw[...] = dot(normed_t[...], dh[...])
        pack(net, p1, aligned(j, 384), dw.at[:, :384], dw.at[:, 384:])

    loop(4, expand_step)
    store_p1 = pltpu.make_async_copy(p1, p1_h, outs.at[0])
    store_p1.start()
    for copy in load_rest:
        copy.wait()
    late = points[12:]

    def norm_step(i):
        spread(i, 0, late[:4])
        r = aligned(i, ROWS)
        n, rsd = normalise(res[r, :])
        g = wide[r, :]
        grad = norm_back(g, n, rsd, vec[3:4, :])
        wide[r, :] = grad
        low = grad.astype(BF16)
        df[r, :] = low
        add_small(small, "fg", down_sum(g * n))
        add_small(small, "fs", down_sum(g))
        add_small(small, "ob", down_sum(low.astype(F32)))
        normed[r, :] = dot(low, w_out[...], NT).astype(BF16)

    loop(blocks, norm_step)
    stores = [store_p1, pltpu.make_async_copy(wide, dres_h, outs.at[1]), pltpu.make_async_copy(normed, do_h, outs.at[2])]
    for copy in stores[1:]:
        copy.start()
    for call in late[4:6]:
        call()
    dw[...] = dot(att[...], df[...], TN)
    pack(net, po, ALL, dw.at[:, :384], dw.at[:, 384:])
    stores.append(pltpu.make_async_copy(po, po_h, outs.at[3]))
    stores[-1].start()
    for call in late[6:]:
        call()
    own = p2[net.mine()]
    w2_own[0:48, :] = own[:, :D].astype(F32)
    w2_own[48:96, :] = own[:, D:].astype(F32)
    for copy in stores:
        copy.wait()
    finish(chains)


def feed_back(Z, Y, act, gp, df, dsec, normed, res, att, w1, w2, w_out, vec, small):
    T = df.shape[0]
    cols = tiles_of((5, 3, 4))
    blocks = (2, 2, Y, Z, 48)
    outs = [
        SDS(blocks + (1536,), BF16), SDS(blocks + (384,), BF16), SDS((T, D), BF16), SDS((T, D), F32),
        SDS((96, D), F32), SDS((8, FF), F32),
    ]
    rows = pltpu.VMEM((T, D), BF16)
    scratch = [
        rows, pltpu.VMEM((T, D), F32), rows, pltpu.VMEM((D, T), BF16), rows, pltpu.VMEM((T, D), F32),
        pltpu.VMEM((D, FF), BF16), pltpu.VMEM((FF, D), BF16), pltpu.VMEM((D, D), BF16),
        pltpu.VMEM((2, T, 384), BF16), pltpu.VMEM((2, 2, T, 384), BF16), rows, pltpu.VMEM((D, D), F32),
        pltpu.VMEM(blocks + (1536,), BF16), pltpu.VMEM(blocks + (384,), BF16), pltpu.VMEM(blocks + (1536,), BF16),
        DMA((sem_count(Z),)), DMA((sem_count(Z),)), DMA((8,)), DMA((6,)), DMA((4,)),
    ] + scatter_scratch((Z, Y), cols)
    return pl.pallas_call(
        functools.partial(feed_back_kernel, Z, Y, cols),
        out_shape=outs,
        in_specs=[ANY] * 10 + [VMEM] * 2,
        out_specs=[ANY] * 4 + [VMEM] * 2,
        scratch_shapes=scratch,
        compiler_params=pltpu.CompilerParams(collective_id=1, has_side_effects=True, vmem_limit_bytes=VMEM_LIMIT),
        name="feed_back",
    )(act, gp, df, dsec, normed, res, att, w1, w2, w_out, vec, small)


def attend_back(qkv, do, mask_t, lse, d, small, seq, p):
    base = pl.multiple_of(seq * LEN, LEN)
    rows = pl.ds(base, LEN)
    lanes = aligned(p, 128)
    q, k, v = (qkv[j * PAIRS + p, rows, :] for j in range(3))
    g = do[rows, lanes]
    kt = k.T
    dk = dv = None
    dqt = []
    for h in range(2):
        here = head_mask(h, k.shape)
        km, vm, qm, gm = (jnp.where(here, a, jnp.zeros_like(a)) for a in (k, v, q, g))
        t = dot(km, q, NT) * (0.125 * LOG2E) + mask_t[seq] - lse[seq * 2 * PAIRS + 2 * p + h, 0:1, :]
        pt = jnp.exp2(t)
        dp = dot(vm, g, NT)
        w = pt * dp
        ds = (w - pt * jnp.sum(w, axis=0, keepdims=True)).astype(BF16)
        dvh = dot(pt.astype(BF16), gm)
        dkh = dot(ds, qm)
        dv = dvh if dv is None else dv + dvh
        dk = dkh if dk is None else dk + dkh
        dqt.append(dot(kt[64 * h : 64 * h + 64, :], ds))
    dq = (jnp.concatenate(dqt, axis=0).T * 0.125).astype(BF16)
    dv = dv.astype(BF16)
    d[rows, lanes] = dq
    d[rows, pl.ds(pl.multiple_of(D + p * 128, 128), 128)] = (dk * 0.125).astype(BF16)
    d[rows, pl.ds(pl.multiple_of(2 * D + p * 128, 128), 128)] = dv
    small[1:2, lanes] += down_sum(dq.astype(F32))
    small[1:2, pl.ds(pl.multiple_of(D + p * 128, 128), 128)] += down_sum(dv.astype(F32))


def small_partners(net):
    out = [lambda: net.across("c"), lambda: net.across("x")]
    if net.Y == 2:
        out.append(lambda: net.across("y"))
    bit = 1
    while bit < net.Z:
        def partner(bit=bit):
            z = net.at["z"]
            return net.device(z=z + bit - 2 * bit * ((z // bit) % 2))

        out.append(partner)
        bit *= 2
    return out


def attend_back_kernel(Z, Y, cols, *refs):
    (qkv_h, do_h, x_h, w_in_h, dres_h, p1_h, po_h, codes, lse, small_in) = refs[:10]
    dx_h, w_in_own, w_out_own, w1_own, stats, exp_own = refs[10:16]
    vectors = refs[16:24]
    (qkv, do, d, x, x_t, w_in, wide, mask_t, dw, g2, g1, mine, theirs, edge, s2, r2, s1, r1, sss, srs, loads, outs) = refs[24:46]
    scratch = refs[46:]
    half = len(scratch) // 2
    net = Net(Z, Y)
    T = x.shape[0]
    seqs, blocks = T // LEN, T // ROWS

    def load(src, dst, k):
        copy = pltpu.make_async_copy(src, dst, loads.at[k])
        copy.start()
        return copy

    load_parts = [load(p1_h, g2.at[:, :, :, :, :, pl.ds(384, 1536)], 0), load(po_h, g2.at[:, :, :, :, :, pl.ds(0, 384)], 1)]
    load_heads = [load(qkv_h, qkv, 2), load(do_h, do, 3)]
    load_x = load(x_h, x, 4)
    load_rest = [load(w_in_h, w_in, 5), load(dres_h, wide, 6)]
    small = mine.at[0]
    small[...] = small_in[...]
    net.barrier()
    for copy in load_parts:
        copy.wait()
    chains2 = scatter_chains(net, g2, cols[0], scratch[:half], (s2, r2))
    chains1 = scatter_chains(net, g1, cols[1], scratch[half:], (s1, r1))
    calls = phased(chains2)
    calls[0]()
    for s in range(seqs):
        build_mask(mask_t.at[s], codes[s, 1:2, :], codes[s, 0:1, :])
    load_x.wait()

    def turn(j):
        lanes = aligned(j, 128)
        x_t[lanes, :] = x[:, lanes].T

    loop(D // 128, turn)
    for copy in load_heads:
        copy.wait()

    def attend_step(i):
        spread(i, 0, calls[1:])
        attend_back(qkv, do, mask_t, lse, d, small, i // PAIRS, i % PAIRS)

    loop(seqs * PAIRS, attend_step)
    own2 = g2[net.mine()].astype(F32)
    w_out_own[...] = jnp.concatenate([own2[:24, :384], own2[24:, :384]], axis=1)
    w1_own[...] = jnp.concatenate([own2[:24, 384:], own2[24:, 384:]], axis=1)

    def weight_step(j):
        left = pl.ds(pl.multiple_of(j * 384, 128), 384)
        right = pl.ds(pl.multiple_of(1152 + j * 384, 128), 384)
        dw[:, :384] = dot(x_t[...], d[:, left])
        dw[:, 384:] = dot(x_t[...], d[:, right])
        pack(net, g1, aligned(j, 384), dw.at[:, :384], dw.at[:, 384:])

    loop(3, weight_step)
    calls = eager(chains1)
    partners = small_partners(net)
    sums = [
        remote(mine.at[k], theirs.at[k], (sss, srs), k, partner()) for k, partner in enumerate(partners)
    ]

    def small_call(k):
        if 0 < k <= len(sums):
            sums[k - 1].wait_recv()
            mine[k] = mine[k - 1] + theirs[k - 1]
        if k < len(sums):
            sums[k].start()

    calls = [lambda k=k, call=call: (call(), small_call(k)) and None for k, call in enumerate(calls)]
    assert len(calls) > len(sums)
    calls[0]()
    for copy in load_rest:
        copy.wait()

    def token_step(i):
        spread(i, 0, calls[1:5])
        r = aligned(i, ROWS)
        wide[r, :] += dot(d[r, :], w_in[...], NT)

    loop(blocks, token_step)
    store = pltpu.make_async_copy(wide, dx_h, outs.at[0])
    store.start()
    for call in calls[5:]:
        call()
    own1 = g1[net.mine()].astype(F32)
    w_in_own[...] = jnp.concatenate([own1[:24], own1[24:]], axis=1)
    total = mine[len(sums)]
    edge[:, FF:] = jnp.zeros((8, 128), F32)
    edge[:, :FF] = total
    lane = lax.broadcasted_iota(jnp.int32, (1, 128), 1)
    packed = jnp.zeros((1, 128), F32)
    for k in range(5):
        packed = jnp.where(lane == k, jnp.sum(total[3:4, k * 128 : (k + 1) * 128], axis=1, keepdims=True), packed)
    stats[...] = packed

    def window(at):
        tile = at // 128
        return pltpu.roll(edge[:, pl.ds(pl.multiple_of(tile * 128, 128), 256)], (256 - at % 128) % 256, axis=1)

    exp_own[...] = window(96 * net.own)[0:1, :96]
    for k in range(4):
        w = window(D * k + 24 * net.own)
        vectors[k][...] = w[1:2, :24]
        vectors[4 + k][...] = w[2:3, :24]
    store.wait()
    for copy in sums:
        copy.wait_send()
    finish(chains2)
    finish(chains1)


def attention_back(Z, Y, qkv, do, x, w_in, dres, p1, po, codes, lse, small):
    T, S = x.shape[0], codes.shape[0]
    cols = (tiles_of((6, 4, 5)), tiles_of((4, 2, 3)))
    blocks = (2, 2, Y, Z, 48)
    rounds = 2 + (Y == 2) + (Z - 1).bit_length()
    assert 2 ** (Z - 1).bit_length() == Z
    outs = [
        SDS((T, D), F32), SDS((24, 3 * D), F32), SDS((24, D), F32), SDS((24, FF), F32), SDS((1, 128), F32), SDS((1, 96), F32),
    ] + [SDS((1, 24), F32)] * 8
    rows = pltpu.VMEM((T, D), BF16)
    scratch = [
        pltpu.VMEM(qkv.shape, BF16), rows, pltpu.VMEM((T, 3 * D), BF16), rows, pltpu.VMEM((D, T), BF16),
        pltpu.VMEM((D, 3 * D), BF16), pltpu.VMEM((T, D), F32), pltpu.VMEM((S, LEN, LEN), F32), pltpu.VMEM((D, D), F32),
        pltpu.VMEM(blocks + (1920,), BF16), pltpu.VMEM(blocks + (1152,), BF16),
        pltpu.VMEM((rounds + 1, 8, FF), F32), pltpu.VMEM((rounds, 8, FF), F32), pltpu.VMEM((8, FF + 128), F32),
    ] + [DMA((sem_count(Z),))] * 4 + [DMA((rounds,))] * 2 + [DMA((7,)), DMA((1,))]
    scratch += scatter_scratch((Z, Y), cols[0]) + scatter_scratch((Z, Y), cols[1])
    return pl.pallas_call(
        functools.partial(attend_back_kernel, Z, Y, cols),
        out_shape=outs,
        in_specs=[ANY] * 7 + [VMEM] * 3,
        out_specs=[ANY] + [VMEM] * 13,
        scratch_shapes=scratch,
        compiler_params=pltpu.CompilerParams(collective_id=2, has_side_effects=True, vmem_limit_bytes=VMEM_LIMIT),
        name="attend_back",
    )(qkv, do, x, w_in, dres, p1, po, codes, lse, small)


def per_device(
    Z, Y, fsdp, tokens, segment_ids, valid, input_weight, query_bias, value_bias, output_weight, output_bias,
    first_gain, first_shift, expand_weight, expand_bias, shrink_weight, shrink_bias, second_gain, second_shift, cotangent,
):
    shards = (input_weight, output_weight, expand_weight, shrink_weight)
    vectors = (query_bias, value_bias, output_bias, first_gain, first_shift, expand_bias, shrink_bias, second_gain, second_shift)
    split = Y == 1 and fsdp > 1
    if split:
        def whole(v):
            return lax.all_gather(v, "fsdp", axis=0, tiled=True)

        shards, vectors = tuple(map(whole, shards)), tuple(map(whole, vectors))
    vectors = [v.reshape(1, -1) for v in vectors]
    codes = jnp.stack([segment_ids, jnp.where(valid > 0, segment_ids, -1), valid], axis=1).astype(F32)
    codes = jnp.pad(codes, ((0, 0), (0, 5), (0, 0)))
    (res, qkv, att, normed, act, gp, df, lse, w_in, w_out, w1, w2, result, dsec, vec, small) = forward(
        Z, Y, tokens, cotangent, codes, shards, vectors
    )
    p1, po, do, dres, w2_own, small = feed_back(Z, Y, act, gp, df, dsec, normed, res, att, w1, w2, w_out, vec, small)
    (dx, w_in_own, w_out_own, w1_own, stats, exp_own, *own) = attention_back(
        Z, Y, qkv, do, tokens, w_in, dres, p1, po, codes, lse, small
    )
    weights = [w_in_own, w_out_own, w1_own, w2_own]
    own = [v.reshape(-1) for v in own]
    exp_own = exp_own.reshape(-1)
    totals = stats[0, :5]
    if split:
        def share(v):
            return lax.psum_scatter(v, "fsdp", scatter_dimension=0, tiled=True)

        weights, own, exp_own = [share(v) for v in weights], [share(v) for v in own], share(exp_own)
        totals = lax.psum(totals, "fsdp")
    qb, vb, ob, fg, fs, sb, sg, ss = own
    return (
        result, dx, totals[:4] / (D * totals[4]), weights[0], qb, vb, weights[1], ob, fg, fs,
        weights[2], exp_own, weights[3], sb, sg, ss,
    )


def solution(mesh):
    dp, fsdp = mesh.shape["dp"], mesh.shape["fsdp"]
    Z, Y = dp // 4, (2 if dp * fsdp == BLOCKS else 1)
    matrix, vector = P(("dp", "fsdp"), None), P(("dp", "fsdp"))
    params = (matrix, vector, vector, matrix, vector, vector, vector, matrix, vector, matrix, vector, vector, vector)
    return jax.shard_map(
        functools.partial(per_device, Z, Y, fsdp),
        mesh=mesh,
        in_specs=(matrix, matrix, matrix) + params + (matrix,),
        out_specs=(matrix, matrix, P()) + params,
        check_vma=False,
    )
```

```python
import functools

import jax
import jax.numpy as jnp
from jax import lax
from jax.experimental import pallas as pl
from jax.experimental.pallas import tpu as pltpu
from jax.sharding import PartitionSpec as P

BLOCKS = 32
F32, BF16 = jnp.float32, jnp.bfloat16
LOG2E = 1.4426950408889634
MESH = pl.DeviceIdType.MESH
ALL = slice(None)
ANY = pl.BlockSpec(memory_space=pl.ANY)
VMEM = pl.BlockSpec(memory_space=pltpu.VMEM)
SDS = jax.ShapeDtypeStruct
DMA = pltpu.SemaphoreType.DMA
NT = (((1,), (1,)), ((), ()))
TN = (((0,), (0,)), ((), ()))
NN = (((1,), (0,)), ((), ()))
D, FF, LEN, PAIRS = 768, 3072, 512, 6
ROWS = 256


def dot(a, b, dims=NN):
    return lax.dot_general(a, b, dims, preferred_element_type=F32)


def aligned(at, step, size=None):
    return pl.ds(pl.multiple_of(at * step, step), step if size is None else size)


def loop(count, body):
    def step(i, carry):
        body(i)
        return carry

    lax.fori_loop(0, count, step, 0)


VMEM_LIMIT = 62 * 2**20


class Net:
    def __init__(self, Z, Y):
        self.Z, self.Y = Z, Y
        dp, y = lax.axis_index("dp"), lax.axis_index("fsdp")
        self.fsdp = y
        self.at = {"z": dp // 4, "x": (dp // 2) % 2, "c": dp % 2, "y": y if Y == 2 else 0}
        self.own = dp * Y + (y if Y == 2 else 0)

    def device(self, **moved):
        p = dict(self.at, **moved)
        return (p["z"] * 4 + p["x"] * 2 + p["c"], p["y"] if self.Y == 2 else self.fsdp)

    def across(self, axis):
        return self.device(**{axis: 1 - self.at[axis]})

    def z_away(self, k):
        return (self.at["z"] + k) % self.Z

    def barrier(self):
        bar = pltpu.get_barrier_semaphore()
        others = [self.across(axis) for axis in (["c", "x", "y"] if self.Y == 2 else ["c", "x"])]
        others += [self.device(z=self.z_away(k)) for k in range(1, self.Z)]
        for other in others:
            pl.semaphore_signal(bar, inc=1, device_id=other, device_id_type=MESH)
        pl.semaphore_wait(bar, len(others))

    def place(self, i):
        Y = self.Y
        return ((i // Y) % 2, (i // (2 * Y)) % 2, i % Y, i // (4 * Y))

    def mine(self):
        at = self.at
        return (at["c"], at["x"], at["y"], at["z"])


TOP, LOW = pl.ds(0, 32), pl.ds(32, 16)
STEPS = 5


def sem_count(Z):
    return 2 * (Z - 1) + 5


def sem_ids(Z):
    n = Z - 1
    return {"tz": 0, "lz": n, "tx": 2 * n, "ty": 2 * n + 1, "lx": 2 * n + 2, "ly": 2 * n + 3, "c": 2 * n + 4}


def remote(src, dst, sems, sem, device):
    return pltpu.make_async_remote_copy(
        src_ref=src,
        dst_ref=dst,
        send_sem=sems[0].at[sem],
        recv_sem=sems[1].at[sem],
        device_id=device,
        device_id_type=MESH,
    )


class Move:
    def __init__(self, pairs):
        self.pairs = pairs

    def start(self):
        for send, _ in self.pairs:
            send().start()

    def receive(self):
        for _, take in self.pairs:
            take().wait_recv()

    def sent(self):
        for send, _ in self.pairs:
            send().wait_send()


def gather_moves(net, buf, sems):
    Z, Y, at, ids = net.Z, net.Y, net.at, sem_ids(net.Z)
    c, x, y, z = at["c"], at["x"], at["y"], at["z"]

    def swap(axis, ours, theirs, sem):
        device = net.across(axis)
        return [(lambda: remote(ours(), ours(), sems, sem, device), lambda: remote(theirs(), theirs(), sems, sem, device))]

    def along_z(part, sem):
        def pair(k):
            return (
                lambda: remote(part(z), part(z), sems, sem + k - 1, net.device(z=net.z_away(k))),
                lambda: remote(part(net.z_away(Z - k)), part(net.z_away(Z - k)), sems, sem + k - 1, net.device(z=net.z_away(k))),
            )

        return [pair(k) for k in range(1, Z)]

    yy = y if Y == 1 else ALL
    moves = [
        along_z(lambda zz: buf.at[c, x, y, zz, TOP], ids["tz"]),
        swap("x", lambda: buf.at[c, x, y, :, TOP], lambda: buf.at[c, 1 - x, y, :, TOP], ids["tx"])
        + along_z(lambda zz: buf.at[c, x, yy, zz, LOW], ids["lz"]),
        swap("x", lambda: buf.at[c, x, yy, :, LOW], lambda: buf.at[c, 1 - x, yy, :, LOW], ids["lx"]),
        swap("c", lambda: buf.at[c], lambda: buf.at[1 - c], ids["c"]),
    ]
    if Y == 2:
        moves[0] += swap("y", lambda: buf.at[c, x, y, z, LOW], lambda: buf.at[c, x, 1 - y, z, LOW], ids["ly"])
        moves[2] += swap("y", lambda: buf.at[c, :, y, :, TOP], lambda: buf.at[c, :, 1 - y, :, TOP], ids["ty"])
    return [Move(pairs) for pairs in moves]


def gather_steps(net, buf, sems):
    moves = gather_moves(net, buf, sems)

    def step(k):
        if k > 0:
            moves[k - 1].receive()
        if k < len(moves):
            moves[k].start()

    return [lambda k=k: step(k) for k in range(STEPS)], moves


def lands(Z, Y, width):
    shapes = [(2, Y, Z, 48), (2, Z, 32), (Y, Z, 16), (Z, 32), (Z - 1, Y, 16), (Z - 1, 32), (16,)]
    return [pltpu.VMEM(shape + (width,), BF16) for shape in shapes]


def add_blocks(count, at, dst, src):
    def one(i):
        idx = at(i)
        dst[idx] = dst[idx] + src[idx]

    loop(count, one)


def scatter_steps(net, buf, land, sems, finish):
    Z, Y, at, ids = net.Z, net.Y, net.at, sem_ids(net.Z)
    c, x, y, z = at["c"], at["x"], at["y"], at["z"]
    core, top_y, low_x, top_x, low_z, top_z, low_y = land

    def swap(axis, what, where, sem):
        device = net.across(axis)

        def make():
            return remote(what(), where, sems, sem, device)

        return [(make, make)]

    def along_z(part, where, sem):
        def make(k):
            return lambda: remote(part(net.z_away(k)), where.at[k - 1], sems, sem + k - 1, net.device(z=net.z_away(k)))

        return [(make(k), make(k)) for k in range(1, Z)]

    yy = y if Y == 1 else ALL
    low_x_land, low_z_land = (low_x.at[0], low_z.at[:, 0]) if Y == 1 else (low_x, low_z)
    moves = [
        swap("c", lambda: buf.at[1 - c], core, ids["c"]),
        swap("x", lambda: buf.at[c, 1 - x, yy, :, LOW], low_x_land, ids["lx"]),
        swap("x", lambda: buf.at[c, 1 - x, y, :, TOP], top_x, ids["tx"])
        + along_z(lambda zz: buf.at[c, x, yy, zz, LOW], low_z_land, ids["lz"]),
        along_z(lambda zz: buf.at[c, x, y, zz, TOP], top_z, ids["tz"]),
    ]
    if Y == 2:
        moves[1] += swap("y", lambda: buf.at[c, :, 1 - y, :, TOP], top_y, ids["ty"])
        moves[3] += swap("y", lambda: buf.at[c, x, 1 - y, z, LOW], low_y, ids["ly"])
    moves = [Move(pairs) for pairs in moves]

    def sum_z(mine, where):
        total = mine.astype(F32)
        for k in range(Z - 1):
            total = total + where(k).astype(F32)
        return total

    def step(k):
        if k > 0:
            moves[k - 1].receive()
        if k == 1:
            add_blocks(2 * Y * Z, lambda i: (i // (Y * Z), (i // Z) % Y, i % Z), buf.at[c], core)
        if k == 2:
            if Y == 2:
                add_blocks(2 * Z, lambda i: (i // Z, i % Z), buf.at[c, :, y, :, TOP], top_y)
            add_blocks(Y * Z, lambda i: (i // Z, i % Z), buf.at[c, x, :, :, LOW], low_x)
        if k == 3:
            add_blocks(Z, lambda i: (i,), buf.at[c, x, y, :, TOP], top_x)
            for j in range(Y):
                own = buf.at[c, x, j, z, LOW]
                own[...] = sum_z(own[...], lambda i: low_z[i, j]).astype(BF16)
        if k < 4:
            moves[k].start()
        else:
            finish(0, 32, sum_z(buf[c, x, y, z, TOP], lambda i: top_z[i]))
            rest = buf[c, x, y, z, LOW].astype(F32)
            finish(32, 16, rest + low_y[...].astype(F32) if Y == 2 else rest)

    return [lambda k=k: step(k) for k in range(STEPS)], moves


def train(steps, first=0):
    calls = []
    for t in range(len(steps) + STEPS - 1):
        todo = [steps[g][t - g] for g in range(len(steps)) if 0 <= t - g < STEPS]
        calls.append(lambda todo=todo: [call() for call in todo] and None)
    return calls


def spread(i, first, calls, every=1):
    for k, call in enumerate(calls):
        pl.when(i == first + k * every)(call)


def head_mask(head, shape):
    lane = lax.broadcasted_iota(jnp.int32, shape, len(shape) - 1)
    return (lane < 64) if head == 0 else (lane >= 64)


def column(row, count=128):
    return jnp.broadcast_to(row, (count, row.shape[1])).T


def build_mask(mask, down, across):
    n = mask.shape[0]
    down = column(down)
    at = lax.broadcasted_iota(jnp.int32, (n, 128), 0)
    lane = lax.broadcasted_iota(jnp.int32, (n, 128), 1)
    for j in range(n // 128):
        tile = slice(j * 128, (j + 1) * 128)
        mask[:, tile] = jnp.where((down == across[:, tile]) | (at == lane + j * 128), 0.0, -1e30)


def gelu_pair(h):
    t = 1.0 / (1.0 + (0.3275911 * 0.7071067811865476) * jnp.abs(h))
    e = jnp.exp2(h * h * (-0.5 * LOG2E))
    poly = t * (
        0.5 * 0.254829592
        + t * (0.5 * -0.284496736 + t * (0.5 * 1.421413741 + t * (0.5 * -1.453152027 + t * (0.5 * 1.061405429))))
    )
    tail = poly * e
    cdf = jnp.where(h >= 0, 1.0 - tail, tail)
    return h * cdf, cdf + h * e * 0.3989422804014327


def normalise(v):
    centred = v - jnp.sum(v, axis=1, keepdims=True) * (1.0 / D)
    r = lax.rsqrt(jnp.sum(centred * centred, axis=1, keepdims=True) * (1.0 / D) + 1e-12)
    return centred * r, r


def norm_back(g, n, r, gain):
    scaled = g * gain
    mean = jnp.sum(scaled, axis=1, keepdims=True) * (1.0 / D)
    along = jnp.sum(scaled * n, axis=1, keepdims=True) * (1.0 / D)
    return r * (scaled - mean - n * along)


def down_sum(v):
    return jnp.sum(v, axis=0, keepdims=True)


def square_sum(value, counted):
    v = value.astype(BF16).astype(F32)
    v = v * v
    total = v[:, :128]
    for j in range(1, D // 128):
        total = total + v[:, j * 128 : (j + 1) * 128]
    return down_sum(total * counted)


def fold(rows, half):
    return jnp.concatenate([rows[:, :half], rows[:, half:]], axis=0).astype(BF16)


def unfold(net, buf, half, dst, at=0):
    def pair(p):
        a = buf[net.place(2 * p) + (ALL, slice(0, half))].astype(F32)
        b = buf[net.place(2 * p + 1) + (ALL, slice(0, half))].astype(F32)
        rows = aligned(p, 48)
        dst[rows, at : at + half] = jnp.concatenate([a[:24], b[:24]], axis=0).astype(BF16)
        dst[rows, at + half : at + 2 * half] = jnp.concatenate([a[24:], b[24:]], axis=0).astype(BF16)

    loop(BLOCKS // 2, pair)


PLACES = {"qb": (1, 0), "vb": (1, 1), "ob": (1, 2), "fg": (1, 3), "fs": (2, 0), "sb": (2, 1), "sg": (2, 2), "ss": (2, 3)}


def add_small(small, name, value):
    row, at = PLACES[name]
    small[row : row + 1, at * D : (at + 1) * D] += value


def small_window(net, vectors, expand, tmp):
    tmp[...] = jnp.zeros_like(tmp)
    for k, ref in enumerate(vectors):
        tmp[k : k + 1, : 24] = ref[...].astype(F32)
    tmp[8:9, : 96] = expand[...].astype(F32)
    i = net.own
    v = pltpu.roll(tmp[0:8, :], (24 * i) % 128, axis=1)
    e = pltpu.roll(tmp[8:16, :], (96 * i) % 128, axis=1)
    both = jnp.concatenate([v, e], axis=0)
    return jnp.concatenate([both[:, :128], both[:, 128:]], axis=0).astype(BF16)


def small_params(net, buf, first, vec, exp):
    vec[...] = jnp.zeros_like(vec)
    exp[...] = jnp.zeros_like(exp)
    for i in range(BLOCKS):
        w = buf[net.place(i) + (slice(0, 32), slice(first, first + 128))].astype(F32)
        for ref, rows, tile in ((vec, 0, 24 * i // 128), (exp, 8, 96 * i // 128)):
            for k in range(2):
                if (tile + k) * 128 < ref.shape[1]:
                    ref[:, (tile + k) * 128 : (tile + k + 1) * 128] += w[16 * k + rows : 16 * k + rows + 8]


def third_of(rows, t):
    return jnp.concatenate([rows[:, j * D + t * 256 : j * D + (t + 1) * 256] for j in range(3)], axis=1)


def attend(qkv, mask, att, lse, seq, p):
    base = pl.multiple_of(seq * LEN, LEN)
    q, k, v = (qkv[j * PAIRS + p, pl.ds(base, LEN), :] for j in range(3))
    lane = lax.broadcasted_iota(jnp.int32, (LEN, 128), 1)
    out, logs = None, lse[pl.ds(base, LEN), :]
    for head in range(2):
        here = head_mask(head, k.shape)
        km, vm = jnp.where(here, k, jnp.zeros_like(k)), jnp.where(here, v, jnp.zeros_like(v))
        t = dot(q, km, NT) * (0.125 * LOG2E) + mask[seq]
        top = jnp.max(t, axis=1, keepdims=True)
        e = jnp.exp2(t - top)
        total = jnp.sum(e, axis=1, keepdims=True)
        o = dot(e.astype(BF16), vm) * (1.0 / total)
        out = o if out is None else out + o
        logs = jnp.where(lane == 2 * p + head, top + jnp.log2(total), logs)
    lse[pl.ds(base, LEN), :] = logs
    att[pl.ds(base, LEN), aligned(p, 128)] = out.astype(BF16)


def forward_kernel(Z, Y, *refs):
    (x_h, cot_h, segment, valid, w_in_s, w_out_s, w1_s, w2_s, qb, vb, ob, fg, fs, eb, sb, sg, ss) = refs[:17]
    (res_h, qkv_h, att_h, normed_h, act_h, gp_h, df_h, lse_h, w_in_h, w_out_h, w1_h, w2_h, result_h, dsec_h) = refs[17:31]
    vec, small, stats = refs[31:34]
    bufs = refs[34:44]
    (w_in, w_out, w1, w2, x, qkv, mask, att, lse, lse_rows, wide, normed, act, gp, cot, exp, tmp) = refs[44:61]
    ssem, rsem, loads, outs, gsem = refs[61:]
    net = Net(Z, Y)
    T = x.shape[0]
    seqs = T // LEN
    blocks = T // ROWS

    load_x = pltpu.make_async_copy(x_h, x, loads.at[0])
    load_x.start()
    load_cot = pltpu.make_async_copy(cot_h, cot, loads.at[1])
    load_cot.start()
    mine = net.mine()
    own_in = w_in_s[...].astype(F32)
    own_1 = w1_s[...].astype(F32)
    bufs[0][mine + (ALL, slice(0, 384))] = fold(third_of(own_in, 0), 384)
    bufs[0][mine + (slice(0, 32), slice(384, 512))] = small_window(net, (qb, vb, ob, fg, fs, sb, sg, ss), eb, tmp)
    bufs[0][mine + (slice(32, 48), slice(384, 512))] = jnp.zeros((16, 128), BF16)
    net.barrier()
    steps, moves = [], []
    for g, buf in enumerate(bufs):
        calls, sends = gather_steps(net, buf, (ssem.at[g], rsem.at[g]))
        steps.append(calls)
        moves += sends
    calls = train(steps)
    for t in (1, 2):
        bufs[t][mine] = fold(third_of(own_in, t), 384)
    calls[0]()
    bufs[3][mine] = fold(w_out_s[...].astype(F32), 384)
    for t in range(3):
        bufs[4 + t][mine] = fold(own_1[:, t * 1024 : (t + 1) * 1024], 512)
        bufs[7 + t][mine + (ALL, slice(0, 256))] = w2_s[0:48, t * 256 : (t + 1) * 256]
        bufs[7 + t][mine + (ALL, slice(256, 512))] = w2_s[48:96, t * 256 : (t + 1) * 256]
    calls[1]()
    small[...] = jnp.zeros_like(small)
    stats[...] = jnp.zeros_like(stats)
    for s in range(seqs):
        seg = segment[s : s + 1, :].astype(F32)
        live = valid[s : s + 1, :].astype(F32)
        build_mask(mask.at[s], seg, jnp.where(live > 0, seg, -1.0))
        stats[4:5, :] += sum(live[:, j * 128 : (j + 1) * 128] for j in range(LEN // 128))
    lse[...] = jnp.zeros_like(lse)
    calls[2]()
    calls[3]()
    calls[4]()
    small_params(net, bufs[0], 384, vec, exp)
    load_x.wait()
    stores = []

    def store(src, dst):
        copy = pltpu.make_async_copy(src, dst, outs.at[len(stores)])
        copy.start()
        stores.append(copy)
        return copy

    for t in range(3):
        unfold(net, bufs[t], 384, w_in.at[t])

        def project(i):
            r = aligned(i, ROWS)
            c = dot(x[r, :], w_in[t])
            for j in range(3):
                part = c[:, j * 256 : (j + 1) * 256]
                if j != 1:
                    part = part + vec[j // 2 : j // 2 + 1, t * 256 : (t + 1) * 256]
                part = part.astype(BF16)
                for u in range(2):
                    qkv[j * PAIRS + 2 * t + u, r, :] = part[:, u * 128 : (u + 1) * 128]

        loop(blocks, project)

        def attend_step(i):
            spread(i, *((2, calls[5:6]), (1, calls[6:7]), (0, calls[7:9], 2))[t])
            attend(qkv, mask, att, lse, i // 2, 2 * t + i % 2)

        loop(2 * seqs, attend_step)
    store(qkv, qkv_h)
    store(w_in, w_in_h)
    store_att = store(att, att_h)
    for s in range(seqs):
        rows = lse[s * LEN : (s + 1) * LEN, :].T
        for h in range(2 * PAIRS):
            lse_rows[s * 2 * PAIRS + h] = jnp.broadcast_to(rows[h : h + 1, :], (8, LEN))
    store(lse_rows, lse_h)
    unfold(net, bufs[3], 384, w_out)
    store(w_out, w_out_h)

    def out_step(i):
        spread(i, 2, calls[9:10])
        r = aligned(i, ROWS)
        branch = dot(att[r, :], w_out[...]) + vec[2:3, :]
        residual = x[r, :].astype(F32) + branch
        wide[r, :] = residual
        n, _ = normalise(residual)
        normed[r, :] = (n * vec[3:4, :] + vec[4:5, :]).astype(BF16)
        live = live_rows(i)
        stats[0:1, :] += square_sum(residual, live)
        stats[1:2, :] += square_sum(branch, live)

    def live_rows(i):
        return live_col[aligned(i, ROWS), :]

    live_col = lse
    for s in range(seqs):
        live_col[s * LEN : (s + 1) * LEN, :] = column(valid[s : s + 1, :].astype(F32))
    loop(blocks, out_step)
    store_wide = store(wide, res_h)
    store(normed, normed_h)

    def gp_copy(t, i):
        slot = (t * blocks + i) % 2
        return pltpu.make_async_copy(
            gp.at[slot], gp_h.at[aligned(i, ROWS), pl.ds(t * 1024, 1024)], gsem.at[slot]
        )

    for t in range(3):
        unfold(net, bufs[4 + t], 512, w1, t * 1024)

        def expand_step(i):
            spread(i, 2, calls[10 + t : 11 + t])
            r = aligned(i, ROWS)
            nv = normed[r, :]
            slot = (t * blocks + i) % 2
            if t == 0:
                pl.when(i >= 2)(lambda: gp_copy(t, i).wait())
            else:
                gp_copy(t, i).wait()
            for j in range(2):
                c = slice(t * 1024 + j * 512, t * 1024 + (j + 1) * 512)
                a, g = gelu_pair(dot(nv, w1[:, c]) + exp[0:1, c])
                act[r, c] = a.astype(BF16)
                gp[slot, :, j * 512 : (j + 1) * 512] = g.astype(BF16)
            gp_copy(t, i).start()

        loop(blocks, expand_step)
    store(w1, w1_h)
    store(act, act_h)
    store_wide.wait()
    for t in range(3):
        if t == 2:
            calls[13]()

        def unfold_last(i, t=t):
            blk = bufs[7 + t].at[net.place(i)]
            c = slice(t * 256, (t + 1) * 256)
            w2[aligned(i, 96, 48), c] = blk[:, :256]
            w2[pl.ds(pl.multiple_of(i * 96 + 48, 48), 48), c] = blk[:, 256:]

        loop(BLOCKS, unfold_last)
        if t < 2:

            def shrink_step(i, t=t):
                r = aligned(i, ROWS)
                wide[r, t * 256 : (t + 1) * 256] = dot(act[r, :], w2[:, t * 256 : (t + 1) * 256])

            loop(blocks, shrink_step)
    store(w2, w2_h)
    store_att.wait()
    load_cot.wait()

    def last_step(i):
        r = aligned(i, ROWS)
        feedfwd = jnp.concatenate([wide[r, :512], dot(act[r, :], w2[:, 512:])], axis=1) + vec[5:6, :]
        second = normed[r, :].astype(F32) + feedfwd
        n, rs = normalise(second)
        gain = vec[6:7, :]
        att[r, :] = (n * gain + vec[7:8, :]).astype(BF16)
        g = cot[r, :].astype(F32)
        grad = norm_back(g, n, rs, gain)
        wide[r, :] = grad
        low = grad.astype(BF16)
        x[r, :] = low
        add_small(small, "sg", down_sum(g * n))
        add_small(small, "ss", down_sum(g))
        add_small(small, "sb", down_sum(low.astype(F32)))
        live = live_rows(i)
        stats[2:3, :] += square_sum(second, live)
        stats[3:4, :] += square_sum(feedfwd, live)

    loop(blocks, last_step)
    ends = [
        pltpu.make_async_copy(wide, dsec_h, loads.at[0]),
        pltpu.make_async_copy(att, result_h, loads.at[1]),
        pltpu.make_async_copy(x, df_h, loads.at[2]),
    ]
    for copy in ends:
        copy.start()
    for k in (0, 1):
        gp_copy(2, blocks - 2 + k).wait()
    for copy in stores:
        if copy is not store_wide and copy is not store_att:
            copy.wait()
    for copy in ends:
        copy.wait()
    for move in moves:
        move.sent()


def forward(Z, Y, x, cot, segment, valid, shards, vectors):
    T, S = x.shape[0], segment.shape[0]
    blocks = (2, 2, Y, Z, 48)
    widths = (512, 384, 384, 384) + (512,) * 6
    outs = [
        SDS((T, D), F32), SDS((3 * PAIRS, T, 128), BF16), SDS((T, D), BF16), SDS((T, D), BF16),
        SDS((T, FF), BF16), SDS((T, FF), BF16), SDS((T, D), BF16), SDS((S * 12, 8, LEN), F32),
        SDS((3, D, D), BF16), SDS((D, D), BF16), SDS((D, FF), BF16), SDS((FF, D), BF16),
        SDS((T, D), BF16), SDS((T, D), F32), SDS((8, D), F32), SDS((8, FF), F32), SDS((8, 128), F32),
    ]
    scratch = [pltpu.VMEM(blocks + (w,), BF16) for w in widths] + [
        pltpu.VMEM((3, D, D), BF16), pltpu.VMEM((D, D), BF16), pltpu.VMEM((D, FF), BF16), pltpu.VMEM((FF, D), BF16),
        pltpu.VMEM((T, D), BF16), pltpu.VMEM((3 * PAIRS, T, 128), BF16), pltpu.VMEM((S, LEN, LEN), F32),
        pltpu.VMEM((T, D), BF16), pltpu.VMEM((T, 128), F32), pltpu.VMEM((S * 12, 8, LEN), F32),
        pltpu.VMEM((T, D), F32), pltpu.VMEM((T, D), BF16), pltpu.VMEM((T, FF), BF16), pltpu.VMEM((2, ROWS, 1024), BF16),
        pltpu.VMEM((T, D), BF16), pltpu.VMEM((8, FF), F32), pltpu.VMEM((16, 256), F32),
        DMA((len(widths), sem_count(Z))), DMA((len(widths), sem_count(Z))), DMA((3,)), DMA((16,)), DMA((2,)),
    ]
    return pl.pallas_call(
        functools.partial(forward_kernel, Z, Y),
        out_shape=outs,
        in_specs=[ANY, ANY] + [VMEM] * 15,
        out_specs=[ANY] * 14 + [VMEM] * 3,
        scratch_shapes=scratch,
        compiler_params=pltpu.CompilerParams(collective_id=0, has_side_effects=True, vmem_limit_bytes=VMEM_LIMIT),
        name="forward",
    )(x, cot, segment, valid, *shards, *vectors)


def pack(net, buf, left, right):
    width = left.shape[1]

    def owner(i):
        rows = aligned(i, 24)
        v = jnp.concatenate([left[rows, :], right[rows, :]], axis=0).astype(BF16)
        buf[net.place(i) + (ALL, slice(0, width))] = v

    loop(BLOCKS, owner)


def all_sum_steps(net, mine, theirs, sems):
    partners = ["c", "x", "y"] if net.Y == 2 else ["c", "x"]
    devices = [net.across(axis) for axis in partners]
    bit = 1
    while bit < net.Z:
        z = net.at["z"]
        devices.append(net.device(z=z + bit - 2 * bit * ((z // bit) % 2)))
        bit *= 2
    copies = [remote(mine.at[k], theirs.at[k], sems, k, device) for k, device in enumerate(devices)]

    def step(k):
        if k > 0:
            copies[k - 1].wait_recv()
            mine[k] = mine[k - 1] + theirs[k - 1]
        if k < len(copies):
            copies[k].start()

    return [lambda k=k: step(k) for k in range(len(copies) + 1)], copies


def rounds_of(Z, Y):
    assert 2 ** (Z - 1).bit_length() == Z
    return 2 + (Y == 2) + (Z - 1).bit_length()


def feed_back_kernel(Z, Y, *refs):
    (act_h, gp_h, df_h, dsec_h, normed_h, res_h, att_h, w1_h, w2_h, w_out_h, vec, small_in, stats_in) = refs[:13]
    p1_h, po_h, do_h, dres_h, w2_own, small, stats = refs[13:20]
    p2, p1 = refs[20:23], refs[23:26]
    (df, wide, normed, normed_t, att, res, w1, w2, w_out, act, gp, dh, dw, po, sum_mine, sum_theirs) = refs[26:42]
    ssem, rsem, sss, srs, loads, chunks, outs = refs[42:49]
    land = refs[49:]
    net = Net(Z, Y)
    T = df.shape[0]
    blocks = T // ROWS

    def load(src, dst, k):
        copy = pltpu.make_async_copy(src, dst, loads.at[k])
        copy.start()
        return copy

    def act_copy(j):
        return pltpu.make_async_copy(act_h.at[:, aligned(j, 384)], act.at[j % 2], chunks.at[j % 2])

    def gp_copy(t):
        return pltpu.make_async_copy(gp_h.at[:, pl.ds(t * 1024, 1024)], gp.at[t % 2], chunks.at[2 + t % 2])

    act_copy(0).start()
    load_df = load(df_h, df, 0)
    act_copy(1).start()
    load_w2 = load(w2_h, w2, 1)
    load_normed = load(normed_h, normed, 2)
    gp_copy(0).start()
    load_w1 = load(w1_h, w1, 3)
    load_dsec = load(dsec_h, wide, 4)
    gp_copy(1).start()
    load_rest = [load(res_h, res, 5), load(att_h, att, 6), load(w_out_h, w_out, 7)]
    small[...] = small_in[...]
    sum_mine[0] = stats_in[...]
    net.barrier()
    load_df.wait()

    def shrink_step(j):
        act_copy(j).wait()
        v = dot(act[j % 2], df[...], TN).astype(BF16)
        for k in range(4):
            place = net.place(4 * j + k)
            for t in range(3):
                c = slice(256 * t, 256 * t + 256)
                p2[t][place + (ALL, slice(0, 256))] = v[96 * k : 96 * k + 48, c]
                p2[t][place + (ALL, slice(256, 512))] = v[96 * k + 48 : 96 * k + 96, c]
        pl.when(j + 2 < FF // 384)(lambda: act_copy(j + 2).start())

    loop(FF // 384, shrink_step)
    steps, moves = [], []
    for t in range(3):

        def finish(first, rows, total, t=t):
            w2_own[first : first + rows, t * 256 : (t + 1) * 256] = total[:, :256]
            w2_own[48 + first : 48 + first + rows, t * 256 : (t + 1) * 256] = total[:, 256:]

        calls, sends = scatter_steps(net, p2[t], land[7 * t : 7 * t + 7], (ssem.at[t], rsem.at[t]), finish)
        steps.append(calls)
        moves += sends
    calls = train(steps)
    sum_calls, sum_copies = all_sum_steps(net, sum_mine, sum_theirs, (sss, srs))
    calls = [lambda k=k, call=call: (call(), sum_calls[k]() if k < len(sum_calls) else None) and None for k, call in enumerate(calls)]
    assert len(sum_calls) <= len(calls)
    calls[0]()
    load_normed.wait()

    def turn(j):
        lanes = aligned(j, 128)
        normed_t[lanes, :] = normed[:, lanes].T

    loop(D // 128, turn)
    calls[1]()
    load_w2.wait()
    load_w1.wait()
    load_dsec.wait()
    stores = []

    def store(src, dst):
        copy = pltpu.make_async_copy(src, dst, outs.at[len(stores)])
        copy.start()
        stores.append(copy)

    for t in range(3):
        gp_copy(t).wait()
        c = slice(t * 1024, (t + 1) * 1024)

        def expand_step(i, t=t, c=c):
            r = aligned(i, 2 * ROWS)
            d = (dot(df[r, :], w2[c, :], NT) * gp[t % 2, r, :].astype(F32)).astype(BF16)
            dh[r, :] = d
            small[0:1, c] += down_sum(d.astype(F32))
            wide[r, :] += dot(d, w1[:, c], NT)

        loop(blocks // 2, expand_step)
        if t == 0:
            gp_copy(2).start()
        if t < 2:
            calls[2 + 2 * t]()
        dw[...] = dot(normed_t[...], dh[...])
        pack(net, p1[t], dw.at[:, :512], dw.at[:, 512:])
        store(p1[t], p1_h.at[t])
        if t < 2:
            calls[3 + 2 * t]()
    for copy in load_rest:
        copy.wait()

    def norm_step(i):
        r = aligned(i, ROWS)
        n, rsd = normalise(res[r, :])
        g = wide[r, :]
        grad = norm_back(g, n, rsd, vec[3:4, :])
        wide[r, :] = grad
        low = grad.astype(BF16)
        df[r, :] = low
        add_small(small, "fg", down_sum(g * n))
        add_small(small, "fs", down_sum(g))
        add_small(small, "ob", down_sum(low.astype(F32)))
        normed[r, :] = dot(low, w_out[...], NT).astype(BF16)

    loop(blocks, norm_step)
    store(wide, dres_h)
    store(normed, do_h)
    dw[:, :D] = dot(att[...], df[...], TN)
    pack(net, po, dw.at[:, :384], dw.at[:, 384:D])
    store(po, po_h)
    calls[6]()
    stats[...] = sum_mine[len(sum_copies)]
    for copy in stores:
        copy.wait()
    for copy in sum_copies:
        copy.wait_send()
    for move in moves:
        move.sent()


def feed_back(Z, Y, act, gp, df, dsec, normed, res, att, w1, w2, w_out, vec, small, stats):
    T = df.shape[0]
    blocks = (2, 2, Y, Z, 48)
    rounds = rounds_of(Z, Y)
    outs = [
        SDS((3,) + blocks + (512,), BF16), SDS(blocks + (384,), BF16), SDS((T, D), BF16), SDS((T, D), F32),
        SDS((96, D), F32), SDS((8, FF), F32), SDS((8, 128), F32),
    ]
    rows = pltpu.VMEM((T, D), BF16)
    scratch = [pltpu.VMEM(blocks + (512,), BF16)] * 6 + [
        rows, pltpu.VMEM((T, D), F32), rows, pltpu.VMEM((D, T), BF16), rows, pltpu.VMEM((T, D), F32),
        pltpu.VMEM((D, FF), BF16), pltpu.VMEM((FF, D), BF16), pltpu.VMEM((D, D), BF16),
        pltpu.VMEM((2, T, 384), BF16), pltpu.VMEM((2, T, 1024), BF16), pltpu.VMEM((T, 1024), BF16),
        pltpu.VMEM((D, 1024), F32), pltpu.VMEM(blocks + (384,), BF16),
        pltpu.VMEM((rounds + 1, 8, 128), F32), pltpu.VMEM((rounds, 8, 128), F32),
        DMA((3, sem_count(Z))), DMA((3, sem_count(Z))), DMA((rounds,)), DMA((rounds,)), DMA((8,)), DMA((4,)), DMA((6,)),
    ] + lands(Z, Y, 512) * 3
    return pl.pallas_call(
        functools.partial(feed_back_kernel, Z, Y),
        out_shape=outs,
        in_specs=[ANY] * 10 + [VMEM] * 3,
        out_specs=[ANY] * 4 + [VMEM] * 3,
        scratch_shapes=scratch,
        compiler_params=pltpu.CompilerParams(collective_id=1, has_side_effects=True, vmem_limit_bytes=VMEM_LIMIT),
        name="feed_back",
    )(act, gp, df, dsec, normed, res, att, w1, w2, w_out, vec, small, stats)


def attend_back(qkv, do, mask_t, lse, d, small, seq, p, u):
    base = pl.multiple_of(seq * LEN, LEN)
    rows = pl.ds(base, LEN)
    lanes = aligned(p, 128)
    q, k, v = (qkv[j * PAIRS + p, rows, :] for j in range(3))
    g = do[rows, lanes]
    kt = k.T
    dk = dv = None
    dqt = []
    for h in range(2):
        here = head_mask(h, k.shape)
        km, vm, qm, gm = (jnp.where(here, a, jnp.zeros_like(a)) for a in (k, v, q, g))
        t = dot(km, q, NT) * (0.125 * LOG2E) + mask_t[seq] - lse[seq * 2 * PAIRS + 2 * p + h, 0:1, :]
        pt = jnp.exp2(t)
        dp = dot(vm, g, NT)
        w = pt * dp
        ds = (w - pt * jnp.sum(w, axis=0, keepdims=True)).astype(BF16)
        dvh = dot(pt.astype(BF16), gm)
        dkh = dot(ds, qm)
        dv = dvh if dv is None else dv + dvh
        dk = dkh if dk is None else dk + dkh
        dqt.append(dot(kt[64 * h : 64 * h + 64, :], ds))
    dq = (jnp.concatenate(dqt, axis=0).T * 0.125).astype(BF16)
    dv = dv.astype(BF16)
    d[rows, aligned(u, 128)] = dq
    d[rows, pl.ds(pl.multiple_of(256 + u * 128, 128), 128)] = (dk * 0.125).astype(BF16)
    d[rows, pl.ds(pl.multiple_of(512 + u * 128, 128), 128)] = dv
    small[1:2, lanes] += down_sum(dq.astype(F32))
    small[1:2, pl.ds(pl.multiple_of(D + p * 128, 128), 128)] += down_sum(dv.astype(F32))


def pack_small(net, buf, small, edge):
    edge[:, FF:] = jnp.zeros((8, 128), F32)
    edge[:, :FF] = small[...]

    for i in range(BLOCKS):
        rows = []
        for k in range(2):
            tile = 24 * i // 128 + k
            for row in (1, 2):
                for j in range(4):
                    at = j * D + tile * 128
                    rows.append(edge[row : row + 1, at : at + 128])
            at = (96 * i // 128 + k) * 128
            rows.append(edge[0:8, at : at + 128])
        buf[net.place(i) + (slice(0, 32), slice(384, 512))] = jnp.concatenate(rows, axis=0).astype(BF16)


def attend_back_kernel(Z, Y, *refs):
    (qkv_h, do_h, x_h, w_in_h, dres_h, p1_h, po_h, segment, valid, lse, small_in) = refs[:11]
    dx_h, in_own, out_own, w1_own = refs[11:15]
    parts = refs[15:22]
    (qkv, do, x, x_t, w_in, wide, mask_t, dw, small, edge) = refs[22:32]
    d = refs[32:35]
    ssem, rsem, loads, outs = refs[35:39]
    land = refs[39:]
    net = Net(Z, Y)
    T = x.shape[0]
    seqs, blocks = T // LEN, T // ROWS

    def load(src, dst, k):
        copy = pltpu.make_async_copy(src, dst, loads.at[k])
        copy.start()
        return copy

    load_parts = [load(p1_h.at[t], parts[t], t) for t in range(3)] + [load(po_h, parts[3], 3)]
    load_heads = [load(qkv_h, qkv, 4), load(do_h, do, 5)]
    load_x = load(x_h, x, 6)
    load_rest = [load(w_in_h, w_in, 7), load(dres_h, wide, 8)]
    small[...] = small_in[...]
    net.barrier()
    steps, moves = [], []
    for g in range(7):

        def finish(first, rows, total, g=g):
            own = (w1_own.at[g], out_own, in_own.at[g - 4 if g > 3 else 0])[0 if g < 3 else 1 if g == 3 else 2]
            own[first : first + rows, : total.shape[1]] = total

        calls, sends = scatter_steps(net, parts[g], land[7 * g : 7 * g + 7], (ssem.at[g], rsem.at[g]), finish)
        steps.append(calls)
        moves += sends

    def move(*todo):
        def call():
            for g, k in todo:
                steps[g][k]()

        return call

    load_parts[0].wait()
    move((0, 0))()
    for s in range(seqs):
        seg = segment[s : s + 1, :].astype(F32)
        build_mask(mask_t.at[s], jnp.where(valid[s : s + 1, :] > 0, seg, -1.0), seg)
    load_x.wait()

    def turn(j):
        lanes = aligned(j, 128)
        x_t[lanes, :] = x[:, lanes].T

    loop(D // 128, turn)
    load_parts[1].wait()
    move((0, 1), (1, 0))()
    for copy in load_heads + load_parts[2:]:
        copy.wait()
    plan = (
        ((1, move((0, 2), (1, 1), (2, 0))), (3, move((0, 3), (1, 2), (2, 1), (3, 0)))),
        ((1, move((1, 4), (2, 3), (3, 2), (4, 1))), (3, move((2, 4), (3, 3), (4, 2)))),
        ((1, move((4, 4), (5, 1))), (3, move((5, 2)))),
    )
    after = (
        move((0, 4), (1, 3), (2, 2), (3, 1), (4, 0)),
        move((3, 4), (4, 3), (5, 0)),
        move((5, 3), (6, 0)),
    )
    for t in range(3):

        def attend_step(i, t=t):
            for at, call in plan[t]:
                spread(i, at, [call])
            attend_back(qkv, do, mask_t, lse, d[t], small, i // 2, 2 * t + i % 2, i % 2)

        loop(2 * seqs, attend_step)
        dw[...] = dot(x_t[...], d[t][...])
        pack(net, parts[4 + t], dw.at[:, :384], dw.at[:, 384:])
        if t == 2:
            pack_small(net, parts[6], small, edge)
            parts[6][:, :, :, :, 32:48, 384:512] = jnp.zeros(parts[6].shape[:4] + (16, 128), BF16)
        after[t]()
    for copy in load_rest:
        copy.wait()

    def token_step(i):
        spread(i, 1, [move((5, 4), (6, 1)), move((6, 2))], 2)
        r = aligned(i, ROWS)
        wide[r, :] += dot(d[0][r, :], w_in[0], NT) + dot(d[1][r, :], w_in[1], NT) + dot(d[2][r, :], w_in[2], NT)

    loop(blocks, token_step)
    store = pltpu.make_async_copy(wide, dx_h, outs.at[0])
    store.start()
    move((6, 3), (6, 4))()
    store.wait()
    for copies in moves:
        copies.sent()


def attention_back(Z, Y, qkv, do, x, w_in, dres, p1, po, segment, valid, lse, small):
    T, S = x.shape[0], segment.shape[0]
    blocks = (2, 2, Y, Z, 48)
    widths = (512, 512, 512, 384, 384, 384, 512)
    outs = [SDS((T, D), F32), SDS((3, 48, 512), F32), SDS((48, 384), F32), SDS((3, 48, 512), F32)]
    rows = pltpu.VMEM((T, D), BF16)
    scratch = [pltpu.VMEM(blocks + (w,), BF16) for w in widths] + [
        pltpu.VMEM(qkv.shape, BF16), rows, rows, pltpu.VMEM((D, T), BF16),
        pltpu.VMEM((3, D, D), BF16), pltpu.VMEM((T, D), F32), pltpu.VMEM((S, LEN, LEN), F32), pltpu.VMEM((D, D), F32),
        pltpu.VMEM((8, FF), F32), pltpu.VMEM((8, FF + 128), F32), rows, rows, rows,
        DMA((7, sem_count(Z))), DMA((7, sem_count(Z))), DMA((9,)), DMA((1,)),
    ]
    for w in widths:
        scratch += lands(Z, Y, w)
    return pl.pallas_call(
        functools.partial(attend_back_kernel, Z, Y),
        out_shape=outs,
        in_specs=[ANY] * 7 + [VMEM] * 4,
        out_specs=[ANY] + [VMEM] * 3,
        scratch_shapes=scratch,
        compiler_params=pltpu.CompilerParams(collective_id=2, has_side_effects=True, vmem_limit_bytes=VMEM_LIMIT),
        name="attend_back",
    )(qkv, do, x, w_in, dres, p1, po, segment, valid, lse, small)


def hand_out_kernel(own_index, in_own, out_own, w1_own, w2_own, stats, *refs):
    w_in, w_out, w1, w2, mean, exp = refs[:6]
    vectors = refs[6:]
    for t in range(3):
        v = in_own[t, :, :384]
        v = jnp.concatenate([v[:24], v[24:]], axis=1)
        for j in range(3):
            w_in[:, j * D + t * 256 : j * D + (t + 1) * 256] = v[:, j * 256 : (j + 1) * 256]
        w1[:, t * 1024 : t * 1024 + 512] = w1_own[t, :24, :]
        w1[:, t * 1024 + 512 : (t + 1) * 1024] = w1_own[t, 24:, :]
    w_out[:, :384] = out_own[:24, :]
    w_out[:, 384:] = out_own[24:, :]
    w2[...] = w2_own[...]
    i = own_index()

    def window(first, rows, at):
        pair = jnp.concatenate([in_own[2, first : first + rows, 384:], in_own[2, 16 + first : 16 + first + rows, 384:]], axis=1)
        return pltpu.roll(pair, (256 - at % 128) % 256, axis=1)

    w = window(0, 8, 24 * i)
    for k in range(8):
        vectors[k][...] = w[k : k + 1, :24]
    exp[...] = window(8, 8, 96 * i)[0:1, :96]
    lane = lax.broadcasted_iota(jnp.int32, (1, 128), 1)
    total = jnp.sum(stats[...], axis=1, keepdims=True)
    packed = jnp.zeros((1, 128), F32)
    for k in range(5):
        packed = jnp.where(lane == k, total[k : k + 1, :], packed)
    mean[...] = packed


def hand_out(Z, Y, in_own, out_own, w1_own, w2_own, stats):
    def own_index():
        return lax.axis_index("dp") * Y + (lax.axis_index("fsdp") if Y == 2 else 0)

    outs = [
        SDS((24, 3 * D), F32), SDS((24, D), F32), SDS((24, FF), F32), SDS((96, D), F32), SDS((1, 128), F32), SDS((1, 96), F32),
    ] + [SDS((1, 24), F32)] * 8
    return pl.pallas_call(
        functools.partial(hand_out_kernel, own_index),
        out_shape=outs,
        in_specs=[VMEM] * 5,
        out_specs=[VMEM] * len(outs),
        name="hand_out",
    )(in_own, out_own, w1_own, w2_own, stats)


def per_device(
    Z, Y, fsdp, tokens, segment_ids, valid, input_weight, query_bias, value_bias, output_weight, output_bias,
    first_gain, first_shift, expand_weight, expand_bias, shrink_weight, shrink_bias, second_gain, second_shift, cotangent,
):
    shards = (input_weight, output_weight, expand_weight, shrink_weight)
    vectors = (query_bias, value_bias, output_bias, first_gain, first_shift, expand_bias, shrink_bias, second_gain, second_shift)
    split = Y == 1 and fsdp > 1
    if split:
        def whole(v):
            return lax.all_gather(v, "fsdp", axis=0, tiled=True)

        shards, vectors = tuple(map(whole, shards)), tuple(map(whole, vectors))
    vectors = [v.reshape(1, -1) for v in vectors]
    (res, qkv, att, normed, act, gp, df, lse, w_in, w_out, w1, w2, result, dsec, vec, small, stats) = forward(
        Z, Y, tokens, cotangent, segment_ids, valid, shards, vectors
    )
    p1, po, do, dres, w2_own, small, stats = feed_back(
        Z, Y, act, gp, df, dsec, normed, res, att, w1, w2, w_out, vec, small, stats
    )
    dx, in_own, out_own, w1_own = attention_back(
        Z, Y, qkv, do, tokens, w_in, dres, p1, po, segment_ids, valid, lse, small
    )
    (*weights, stats, exp_own, qb, vb, ob, fg, fs, sb, sg, ss) = hand_out(Z, Y, in_own, out_own, w1_own, w2_own, stats)
    own = [v.reshape(-1) for v in (qb, vb, ob, fg, fs, sb, sg, ss, exp_own)]
    totals = stats[0, :5]
    if split:
        def share(v):
            return lax.psum_scatter(v, "fsdp", scatter_dimension=0, tiled=True)

        weights, own = [share(v) for v in weights], [share(v) for v in own]
        totals = lax.psum(totals, "fsdp")
    qb, vb, ob, fg, fs, sb, sg, ss, exp_own = own
    return (
        result, dx, totals[:4] / (D * totals[4]), weights[0], qb, vb, weights[1], ob, fg, fs,
        weights[2], exp_own, weights[3], sb, sg, ss,
    )


def solution(mesh):
    dp, fsdp = mesh.shape["dp"], mesh.shape["fsdp"]
    Z, Y = dp // 4, (2 if dp * fsdp == BLOCKS else 1)
    matrix, vector = P(("dp", "fsdp"), None), P(("dp", "fsdp"))
    params = (matrix, vector, vector, matrix, vector, vector, vector, matrix, vector, matrix, vector, vector, vector)
    return jax.shard_map(
        functools.partial(per_device, Z, Y, fsdp),
        mesh=mesh,
        in_specs=(matrix, matrix, matrix) + params + (matrix,),
        out_specs=(matrix, matrix, P()) + params,
        check_vma=False,
    )
```

```python
import functools

import jax
import jax.numpy as jnp
from jax import lax
from jax.experimental import pallas as pl
from jax.experimental.pallas import tpu as pltpu
from jax.sharding import PartitionSpec as P

BLOCKS = 32
F32, BF16 = jnp.float32, jnp.bfloat16
LOG2E = 1.4426950408889634
MESH = pl.DeviceIdType.MESH
ALL = slice(None)
ANY = pl.BlockSpec(memory_space=pl.ANY)
VMEM = pl.BlockSpec(memory_space=pltpu.VMEM)
SDS = jax.ShapeDtypeStruct
DMA = pltpu.SemaphoreType.DMA
NT = (((1,), (1,)), ((), ()))
TN = (((0,), (0,)), ((), ()))
NN = (((1,), (0,)), ((), ()))
D, FF, LEN, PAIRS = 768, 3072, 512, 6
ROWS = 256


def dot(a, b, dims=NN):
    return lax.dot_general(a, b, dims, preferred_element_type=F32)


def aligned(at, step, size=None):
    return pl.ds(pl.multiple_of(at * step, step), step if size is None else size)


def loop(count, body):
    def step(i, carry):
        body(i)
        return carry

    lax.fori_loop(0, count, step, 0)


VMEM_LIMIT = 62 * 2**20


class Net:
    def __init__(self, Z, Y):
        self.Z, self.Y = Z, Y
        dp, y = lax.axis_index("dp"), lax.axis_index("fsdp")
        self.fsdp = y
        self.at = {"z": dp // 4, "x": (dp // 2) % 2, "c": dp % 2, "y": y if Y == 2 else 0}
        self.own = dp * Y + (y if Y == 2 else 0)

    def device(self, **moved):
        p = dict(self.at, **moved)
        return (p["z"] * 4 + p["x"] * 2 + p["c"], p["y"] if self.Y == 2 else self.fsdp)

    def across(self, axis):
        return self.device(**{axis: 1 - self.at[axis]})

    def z_away(self, k):
        return (self.at["z"] + k) % self.Z

    def barrier(self):
        bar = pltpu.get_barrier_semaphore()
        others = [self.across(axis) for axis in (["c", "x", "y"] if self.Y == 2 else ["c", "x"])]
        others += [self.device(z=self.z_away(k)) for k in range(1, self.Z)]
        for other in others:
            pl.semaphore_signal(bar, inc=1, device_id=other, device_id_type=MESH)
        pl.semaphore_wait(bar, len(others))

    def place(self, i):
        Y = self.Y
        return ((i // Y) % 2, (i // (2 * Y)) % 2, i % Y, i // (4 * Y))

    def mine(self):
        at = self.at
        return (at["c"], at["x"], at["y"], at["z"])


TOP, LOW = pl.ds(0, 32), pl.ds(32, 16)
STEPS = 5


def sem_count(Z):
    return 2 * (Z - 1) + 5


def sem_ids(Z):
    n = Z - 1
    return {"tz": 0, "lz": n, "tx": 2 * n, "ty": 2 * n + 1, "lx": 2 * n + 2, "ly": 2 * n + 3, "c": 2 * n + 4}


def remote(src, dst, sems, sem, device):
    return pltpu.make_async_remote_copy(
        src_ref=src,
        dst_ref=dst,
        send_sem=sems[0].at[sem],
        recv_sem=sems[1].at[sem],
        device_id=device,
        device_id_type=MESH,
    )


class Move:
    def __init__(self, pairs):
        self.pairs = pairs

    def start(self):
        for send, _ in self.pairs:
            send().start()

    def receive(self):
        for _, take in self.pairs:
            take().wait_recv()

    def sent(self):
        for send, _ in self.pairs:
            send().wait_send()


def gather_moves(net, buf, sems):
    Z, Y, at, ids = net.Z, net.Y, net.at, sem_ids(net.Z)
    c, x, y, z = at["c"], at["x"], at["y"], at["z"]

    def swap(axis, ours, theirs, sem):
        device = net.across(axis)
        return [(lambda: remote(ours(), ours(), sems, sem, device), lambda: remote(theirs(), theirs(), sems, sem, device))]

    def along_z(part, sem):
        def pair(k):
            return (
                lambda: remote(part(z), part(z), sems, sem + k - 1, net.device(z=net.z_away(k))),
                lambda: remote(part(net.z_away(Z - k)), part(net.z_away(Z - k)), sems, sem + k - 1, net.device(z=net.z_away(k))),
            )

        return [pair(k) for k in range(1, Z)]

    yy = y if Y == 1 else ALL
    moves = [
        along_z(lambda zz: buf.at[c, x, y, zz, TOP], ids["tz"]),
        swap("x", lambda: buf.at[c, x, y, :, TOP], lambda: buf.at[c, 1 - x, y, :, TOP], ids["tx"])
        + along_z(lambda zz: buf.at[c, x, yy, zz, LOW], ids["lz"]),
        swap("x", lambda: buf.at[c, x, yy, :, LOW], lambda: buf.at[c, 1 - x, yy, :, LOW], ids["lx"]),
        swap("c", lambda: buf.at[c], lambda: buf.at[1 - c], ids["c"]),
    ]
    if Y == 2:
        moves[0] += swap("y", lambda: buf.at[c, x, y, z, LOW], lambda: buf.at[c, x, 1 - y, z, LOW], ids["ly"])
        moves[2] += swap("y", lambda: buf.at[c, :, y, :, TOP], lambda: buf.at[c, :, 1 - y, :, TOP], ids["ty"])
    return [Move(pairs) for pairs in moves]


def gather_steps(net, buf, sems):
    moves = gather_moves(net, buf, sems)

    def step(k):
        if k > 0:
            moves[k - 1].receive()
        if k < len(moves):
            moves[k].start()

    return [lambda k=k: step(k) for k in range(STEPS)], moves


def lands(Z, Y, width):
    shapes = [(2, Y, Z, 48), (2, Z, 32), (Y, Z, 16), (Z, 32), (Z - 1, Y, 16), (Z - 1, 32), (16,)]
    return [pltpu.VMEM(shape + (width,), BF16) for shape in shapes]


def add_blocks(count, at, dst, src):
    def one(i):
        idx = at(i)
        dst[idx] = dst[idx] + src[idx]

    loop(count, one)


def scatter_steps(net, buf, land, sems, finish):
    Z, Y, at, ids = net.Z, net.Y, net.at, sem_ids(net.Z)
    c, x, y, z = at["c"], at["x"], at["y"], at["z"]
    core, top_y, low_x, top_x, low_z, top_z, low_y = land

    def swap(axis, what, where, sem):
        device = net.across(axis)

        def make():
            return remote(what(), where, sems, sem, device)

        return [(make, make)]

    def along_z(part, where, sem):
        def make(k):
            return lambda: remote(part(net.z_away(k)), where.at[k - 1], sems, sem + k - 1, net.device(z=net.z_away(k)))

        return [(make(k), make(k)) for k in range(1, Z)]

    yy = y if Y == 1 else ALL
    low_x_land, low_z_land = (low_x.at[0], low_z.at[:, 0]) if Y == 1 else (low_x, low_z)
    moves = [
        swap("c", lambda: buf.at[1 - c], core, ids["c"]),
        swap("x", lambda: buf.at[c, 1 - x, yy, :, LOW], low_x_land, ids["lx"]),
        swap("x", lambda: buf.at[c, 1 - x, y, :, TOP], top_x, ids["tx"])
        + along_z(lambda zz: buf.at[c, x, yy, zz, LOW], low_z_land, ids["lz"]),
        along_z(lambda zz: buf.at[c, x, y, zz, TOP], top_z, ids["tz"]),
    ]
    if Y == 2:
        moves[1] += swap("y", lambda: buf.at[c, :, 1 - y, :, TOP], top_y, ids["ty"])
        moves[3] += swap("y", lambda: buf.at[c, x, 1 - y, z, LOW], low_y, ids["ly"])
    moves = [Move(pairs) for pairs in moves]

    def sum_z(mine, where):
        total = mine.astype(F32)
        for k in range(Z - 1):
            total = total + where(k).astype(F32)
        return total

    def step(k):
        if k > 0:
            moves[k - 1].receive()
        if k == 1:
            add_blocks(2 * Y * Z, lambda i: (i // (Y * Z), (i // Z) % Y, i % Z), buf.at[c], core)
        if k == 2:
            if Y == 2:
                add_blocks(2 * Z, lambda i: (i // Z, i % Z), buf.at[c, :, y, :, TOP], top_y)
            add_blocks(Y * Z, lambda i: (i // Z, i % Z), buf.at[c, x, :, :, LOW], low_x)
        if k == 3:
            add_blocks(Z, lambda i: (i,), buf.at[c, x, y, :, TOP], top_x)
            for j in range(Y):
                own = buf.at[c, x, j, z, LOW]
                own[...] = sum_z(own[...], lambda i: low_z[i, j]).astype(BF16)
        if k < 4:
            moves[k].start()
        else:
            finish(0, 32, sum_z(buf[c, x, y, z, TOP], lambda i: top_z[i]))
            rest = buf[c, x, y, z, LOW].astype(F32)
            finish(32, 16, rest + low_y[...].astype(F32) if Y == 2 else rest)

    return [lambda k=k: step(k) for k in range(STEPS)], moves


def together(todo):
    def call():
        for one in todo:
            one()

    return call


def train(steps, offsets):
    calls = []
    for t in range(len(steps) + offsets[-1]):
        todo = [steps[g][k] for g in range(len(steps)) for k in range(STEPS) if g + offsets[k] == t]
        calls.append(together(todo))
    return calls


def spread(i, first, calls, every=1):
    for k, call in enumerate(calls):
        pl.when(i == first + k * every)(call)


FORWARD_PLAN = (
    ((0, 0), (1, 0), (0, 1), (1, 1), (2, 0), (3, 0), (0, 2), (4, 0), (2, 1), (3, 1), (1, 2), (0, 3),),
    ((5, 0), (4, 1), (6, 0), (8, 0), (2, 2), (0, 4),),
    (),
    (),
    ((1, 3),),
    (),
    ((3, 2),),
    (),
    ((4, 2), (2, 3), (1, 4),),
    ((5, 1),),
    (),
    (),
    ((6, 1), (7, 0),),
    (),
    ((8, 1),),
    ((3, 3), (5, 2), (2, 4),),
    ((9, 0),),
    (),
    (),
    ((6, 2),),
    ((4, 3),),
    ((7, 1),),
    ((3, 4),),
    (),
    (),
    ((8, 2), (4, 4),),
    (),
    ((9, 1),),
    ((5, 3), (7, 2),),
    ((6, 3),),
    (),
    (),
    ((5, 4),),
    ((9, 2),),
    ((6, 4),),
    (),
    ((8, 3),),
    (),
    ((7, 3),),
    (),
    (),
    (),
    ((7, 4),),
    (),
    ((9, 3),),
    ((8, 4),),
    (),
    (),
    ((9, 4),),
)

BACKWARD_PLAN = (
    (),
    (),
    ((0, 0),),
    ((1, 0),),
    ((0, 1),),
    (),
    (),
    ((3, 0),),
    (),
    (),
    ((2, 0), (0, 2), (1, 1),),
    (),
    (),
    ((0, 3),),
    ((2, 1), (4, 0),),
    (),
    (),
    (),
    ((5, 0),),
    ((1, 2),),
    ((4, 1), (2, 2),),
    (),
    ((6, 0), (0, 4), (3, 1), (5, 1),),
    (),
    ((2, 3), (1, 3), (7, 0),),
    ((6, 1),),
    ((4, 2), (3, 2),),
    ((5, 2), (1, 4), (7, 1),),
    ((8, 0), (3, 3),),
    ((2, 4), (4, 3),),
    ((5, 3),),
    (),
    ((8, 1),),
    ((9, 0), (6, 2),),
    ((5, 4), (7, 2), (9, 1), (6, 3),),
    ((8, 2), (3, 4), (7, 3),),
    ((4, 4), (9, 2),),
    ((8, 3), (6, 4), (9, 3),),
    ((7, 4), (8, 4), (9, 4),),
)


def head_mask(head, shape):
    lane = lax.broadcasted_iota(jnp.int32, shape, len(shape) - 1)
    return (lane < 64) if head == 0 else (lane >= 64)


def column(row, count=128):
    return jnp.broadcast_to(row, (count, row.shape[1])).T


def build_mask(mask, down, across):
    n = mask.shape[0]
    down = column(down)
    at = lax.broadcasted_iota(jnp.int32, (n, 128), 0)
    lane = lax.broadcasted_iota(jnp.int32, (n, 128), 1)
    for j in range(n // 128):
        tile = slice(j * 128, (j + 1) * 128)
        mask[:, tile] = jnp.where((down == across[:, tile]) | (at == lane + j * 128), 0.0, -1e30).astype(mask.dtype)


def gelu_pair(h):
    cdf = 0.5 + 0.5 * lax.erf(h * 0.7071067811865476)
    return h * cdf, cdf + h * jnp.exp2(h * h * (-0.5 * LOG2E)) * 0.3989422804014327


def normalise(v):
    centred = v - jnp.sum(v, axis=1, keepdims=True) * (1.0 / D)
    r = lax.rsqrt(jnp.sum(centred * centred, axis=1, keepdims=True) * (1.0 / D) + 1e-12)
    return centred * r, r


def norm_back(g, n, r, gain):
    scaled = g * gain
    mean = jnp.sum(scaled, axis=1, keepdims=True) * (1.0 / D)
    along = jnp.sum(scaled * n, axis=1, keepdims=True) * (1.0 / D)
    return r * (scaled - mean - n * along)


def down_sum(v):
    return jnp.sum(v, axis=0, keepdims=True)


def square_sum(value, counted):
    v = value.astype(BF16).astype(F32)
    v = v * v
    total = v[:, :128]
    for j in range(1, D // 128):
        total = total + v[:, j * 128 : (j + 1) * 128]
    return down_sum(total * counted)


def fold(rows, half):
    return jnp.concatenate([rows[:, :half], rows[:, half:]], axis=0).astype(BF16)


def unfold(net, buf, half, dst, at=0):
    def pair(p):
        a = buf[net.place(2 * p) + (ALL, slice(0, half))].astype(F32)
        b = buf[net.place(2 * p + 1) + (ALL, slice(0, half))].astype(F32)
        rows = aligned(p, 48)
        dst[rows, at : at + half] = jnp.concatenate([a[:24], b[:24]], axis=0).astype(BF16)
        dst[rows, at + half : at + 2 * half] = jnp.concatenate([a[24:], b[24:]], axis=0).astype(BF16)

    loop(BLOCKS // 2, pair)


PLACES = {"qb": (1, 0), "vb": (1, 1), "ob": (1, 2), "fg": (1, 3), "fs": (2, 0), "sb": (2, 1), "sg": (2, 2), "ss": (2, 3)}


def add_small(small, name, value):
    row, at = PLACES[name]
    small[row : row + 1, at * D : (at + 1) * D] += value


def small_window(net, vectors, expand, tmp):
    tmp[...] = jnp.zeros_like(tmp)
    for k, ref in enumerate(vectors):
        tmp[k : k + 1, : 24] = ref[...].astype(F32)
    tmp[8:9, : 96] = expand[...].astype(F32)
    i = net.own
    v = pltpu.roll(tmp[0:8, :], (24 * i) % 128, axis=1)
    e = pltpu.roll(tmp[8:16, :], (96 * i) % 128, axis=1)
    both = jnp.concatenate([v, e], axis=0)
    return jnp.concatenate([both[:, :128], both[:, 128:]], axis=0).astype(BF16)


def small_params(net, buf, first, vec, exp):
    vec[...] = jnp.zeros_like(vec)
    exp[...] = jnp.zeros_like(exp)
    for i in range(BLOCKS):
        w = buf[net.place(i) + (slice(0, 32), slice(first, first + 128))].astype(F32)
        for ref, rows, tile in ((vec, 0, 24 * i // 128), (exp, 8, 96 * i // 128)):
            for k in range(2):
                if (tile + k) * 128 < ref.shape[1]:
                    ref[:, (tile + k) * 128 : (tile + k + 1) * 128] += w[16 * k + rows : 16 * k + rows + 8]


def third_of(rows, t):
    return jnp.concatenate([rows[:, j * D + t * 256 : j * D + (t + 1) * 256] for j in range(3)], axis=1)


def attend(qkv, mask, att, lse, seq, p):
    T = att.shape[0]
    base = pl.multiple_of(seq * LEN, LEN)
    lanes = aligned(p, 128)
    q, k, v = (qkv[pl.ds(pl.multiple_of(j * T + seq * LEN, LEN), LEN), lanes] for j in range(3))
    lane = lax.broadcasted_iota(jnp.int32, (LEN, 128), 1)
    zero = jnp.zeros_like(k)
    here = [head_mask(h, k.shape) for h in range(2)]
    scores = [dot(q, jnp.where(m, k, zero), NT) for m in here]
    weights, totals, logs = [], [], lse[pl.ds(base, LEN), :]
    for h in range(2):
        t = scores[h] * (0.125 * LOG2E) + mask[seq]
        top = jnp.max(t, axis=1, keepdims=True)
        e = jnp.exp2(t - top)
        total = jnp.sum(e, axis=1, keepdims=True)
        weights.append(e.astype(BF16))
        totals.append(total)
        logs = jnp.where(lane == 2 * p + h, top + jnp.log2(total), logs)
    out = sum(dot(weights[h], jnp.where(here[h], v, zero)) * (1.0 / totals[h]) for h in range(2))
    lse[pl.ds(base, LEN), :] = logs
    att[pl.ds(base, LEN), lanes] = out.astype(BF16)


def forward_kernel(Z, Y, plan, *refs):
    (x_h, cot_h, segment, valid, w_in_s, w_out_s, w1_s, w2_s, qb, vb, ob, fg, fs, eb, sb, sg, ss) = refs[:17]
    (res_h, qkv_h, att_h, normed_h, act_h, gp_h, df_h, lse_h, w_in_h, w_out_h, w1_h, w2_h, result_h, dsec_h) = refs[17:31]
    vec, small, stats = refs[31:34]
    bufs = refs[34:44]
    (w_in, w_out, w1, w2, x, qkv, mask, att, lse, lse_rows, wide, normed, act, gp, cot, exp, tmp) = refs[44:61]
    ssem, rsem, loads, outs, gsem = refs[61:]
    net = Net(Z, Y)
    T = x.shape[0]
    seqs = T // LEN
    blocks = T // ROWS

    load_x = pltpu.make_async_copy(x_h, x, loads.at[0])
    load_x.start()
    load_cot = pltpu.make_async_copy(cot_h, cot, loads.at[1])
    load_cot.start()
    mine = net.mine()
    own_in = w_in_s[...].astype(F32)
    own_1 = w1_s[...].astype(F32)
    bufs[0][mine + (ALL, slice(0, 384))] = fold(third_of(own_in, 0), 384)
    bufs[0][mine + (slice(0, 32), slice(384, 512))] = small_window(net, (qb, vb, ob, fg, fs, sb, sg, ss), eb, tmp)
    bufs[0][mine + (slice(32, 48), slice(384, 512))] = jnp.zeros((16, 128), BF16)
    for t in (1, 2):
        bufs[t][mine] = fold(third_of(own_in, t), 384)
    bufs[3][mine] = fold(w_out_s[...].astype(F32), 384)
    for t in range(3):
        bufs[4 + t][mine] = fold(own_1[:, t * 1024 : (t + 1) * 1024], 512)
        bufs[7 + t][mine + (ALL, slice(0, 256))] = w2_s[0:48, t * 256 : (t + 1) * 256]
        bufs[7 + t][mine + (ALL, slice(256, 512))] = w2_s[48:96, t * 256 : (t + 1) * 256]
    net.barrier()
    steps, moves = [], []
    for g, buf in enumerate(bufs):
        calls, sends = gather_steps(net, buf, (ssem.at[g], rsem.at[g]))
        steps.append(calls)
        moves += sends
    plan = list(plan)

    def move():
        return together([steps[g][k] for g, k in plan.pop(0)])

    move()()
    small[...] = jnp.zeros_like(small)
    stats[...] = jnp.zeros_like(stats)
    for s in range(seqs):
        seg = segment[s : s + 1, :].astype(F32)
        live = valid[s : s + 1, :].astype(F32)
        build_mask(mask.at[s], seg, jnp.where(live > 0, seg, -1.0))
        stats[4:5, :] += sum(live[:, j * 128 : (j + 1) * 128] for j in range(LEN // 128))
    lse[...] = jnp.zeros_like(lse)
    move()()
    small_params(net, bufs[0], 384, vec, exp)
    load_x.wait()
    stores = []

    def store(src, dst):
        copy = pltpu.make_async_copy(src, dst, outs.at[len(stores)])
        copy.start()
        stores.append(copy)
        return copy

    for t in range(3):
        if t > 0:
            move()()
        unfold(net, bufs[t], 384, w_in, t * D)
        inner = [move(), move()]

        def project(i):
            spread(i, 0, inner)
            r = aligned(i, 2 * ROWS)
            c = dot(x[r, :], w_in[:, t * D : (t + 1) * D])
            for j in range(3):
                part = c[:, j * 256 : (j + 1) * 256]
                if j != 1:
                    part = part + vec[j // 2 : j // 2 + 1, t * 256 : (t + 1) * 256]
                part = part.astype(BF16)
                qkv[pl.ds(pl.multiple_of(j * T + i * 2 * ROWS, 2 * ROWS), 2 * ROWS), t * 256 : (t + 1) * 256] = part

        loop(blocks // 2, project)
        inner = [move() for _ in range(2 * seqs)]

        def attend_step(i):
            spread(i, 0, inner)
            attend(qkv, mask, att, lse, i // 2, 2 * t + i % 2)

        loop(2 * seqs, attend_step)
    store(qkv, qkv_h)
    store(w_in, w_in_h)
    store_att = store(att, att_h)
    for s in range(seqs):
        rows = lse[s * LEN : (s + 1) * LEN, :].T
        for h in range(2 * PAIRS):
            lse_rows[s * 2 * PAIRS + h] = jnp.broadcast_to(rows[h : h + 1, :], (8, LEN))
    store(lse_rows, lse_h)
    move()()
    unfold(net, bufs[3], 384, w_out)
    store(w_out, w_out_h)

    def out_step(i):
        spread(i, 0, inner)
        r = aligned(i, ROWS)
        branch = dot(att[r, :], w_out[...]) + vec[2:3, :]
        residual = x[r, :].astype(F32) + branch
        wide[r, :] = residual
        n, _ = normalise(residual)
        normed[r, :] = (n * vec[3:4, :] + vec[4:5, :]).astype(BF16)
        live = live_rows(i)
        stats[0:1, :] += square_sum(residual, live)
        stats[1:2, :] += square_sum(branch, live)

    def live_rows(i):
        return live_col[aligned(i, ROWS), :]

    live_col = lse
    for s in range(seqs):
        live_col[s * LEN : (s + 1) * LEN, :] = column(valid[s : s + 1, :].astype(F32))
    inner = [move() for _ in range(blocks)]
    loop(blocks, out_step)
    store_wide = store(wide, res_h)
    store(normed, normed_h)

    def gp_copy(t, i):
        slot = (t * blocks + i) % 2
        return pltpu.make_async_copy(
            gp.at[slot], gp_h.at[aligned(i, ROWS), pl.ds(t * 1024, 1024)], gsem.at[slot]
        )

    for t in range(3):
        move()()
        unfold(net, bufs[4 + t], 512, w1, t * 1024)
        inner = [move() for _ in range(blocks)]

        def expand_step(i):
            spread(i, 0, inner)
            r = aligned(i, ROWS)
            nv = normed[r, :]
            slot = (t * blocks + i) % 2
            if t == 0:
                pl.when(i >= 2)(lambda: gp_copy(t, i).wait())
            else:
                gp_copy(t, i).wait()
            for j in range(2):
                c = slice(t * 1024 + j * 512, t * 1024 + (j + 1) * 512)
                a, g = gelu_pair(dot(nv, w1[:, c]) + exp[0:1, c])
                act[r, c] = a.astype(BF16)
                gp[slot, :, j * 512 : (j + 1) * 512] = g.astype(BF16)
            gp_copy(t, i).start()

        loop(blocks, expand_step)
    store(w1, w1_h)
    store(act, act_h)
    store_wide.wait()
    for t in range(3):
        move()()

        def unfold_last(i, t=t):
            blk = bufs[7 + t].at[net.place(i)]
            c = slice(t * 256, (t + 1) * 256)
            w2[aligned(i, 96, 48), c] = blk[:, :256]
            w2[pl.ds(pl.multiple_of(i * 96 + 48, 48), 48), c] = blk[:, 256:]

        loop(BLOCKS, unfold_last)
        if t < 2:
            inner = [move(), move()]

            def shrink_step(i, t=t):
                spread(i, 0, inner)
                r = aligned(i, 2 * ROWS)
                wide[r, t * 256 : (t + 1) * 256] = dot(act[r, :], w2[:, t * 256 : (t + 1) * 256])

            loop(blocks // 2, shrink_step)
    assert not plan
    store(w2, w2_h)
    store_att.wait()
    load_cot.wait()

    def last_step(i):
        r = aligned(i, ROWS)
        feedfwd = jnp.concatenate([wide[r, :512], dot(act[r, :], w2[:, 512:])], axis=1) + vec[5:6, :]
        second = normed[r, :].astype(F32) + feedfwd
        n, rs = normalise(second)
        gain = vec[6:7, :]
        att[r, :] = (n * gain + vec[7:8, :]).astype(BF16)
        g = cot[r, :].astype(F32)
        grad = norm_back(g, n, rs, gain)
        wide[r, :] = grad
        low = grad.astype(BF16)
        x[r, :] = low
        add_small(small, "sg", down_sum(g * n))
        add_small(small, "ss", down_sum(g))
        add_small(small, "sb", down_sum(low.astype(F32)))
        live = live_rows(i)
        stats[2:3, :] += square_sum(second, live)
        stats[3:4, :] += square_sum(feedfwd, live)

    loop(blocks, last_step)
    ends = [
        pltpu.make_async_copy(wide, dsec_h, loads.at[0]),
        pltpu.make_async_copy(att, result_h, loads.at[1]),
        pltpu.make_async_copy(x, df_h, loads.at[2]),
    ]
    for copy in ends:
        copy.start()
    for k in (0, 1):
        gp_copy(2, blocks - 2 + k).wait()
    for copy in stores:
        if copy is not store_wide and copy is not store_att:
            copy.wait()
    for copy in ends:
        copy.wait()
    for move in moves:
        move.sent()


def forward(Z, Y, x, cot, segment, valid, shards, vectors):
    T, S = x.shape[0], segment.shape[0]
    blocks = (2, 2, Y, Z, 48)
    widths = (512, 384, 384, 384) + (512,) * 6
    outs = [
        SDS((T, D), F32), SDS((3 * T, D), BF16), SDS((T, D), BF16), SDS((T, D), BF16),
        SDS((T, FF), BF16), SDS((T, FF), BF16), SDS((T, D), BF16), SDS((S * 12, 8, LEN), F32),
        SDS((D, 3 * D), BF16), SDS((D, D), BF16), SDS((D, FF), BF16), SDS((FF, D), BF16),
        SDS((T, D), BF16), SDS((T, D), F32), SDS((8, D), F32), SDS((8, FF), F32), SDS((8, 128), F32),
    ]
    scratch = [pltpu.VMEM(blocks + (w,), BF16) for w in widths] + [
        pltpu.VMEM((D, 3 * D), BF16), pltpu.VMEM((D, D), BF16), pltpu.VMEM((D, FF), BF16), pltpu.VMEM((FF, D), BF16),
        pltpu.VMEM((T, D), BF16), pltpu.VMEM((3 * T, D), BF16), pltpu.VMEM((S, LEN, LEN), F32),
        pltpu.VMEM((T, D), BF16), pltpu.VMEM((T, 128), F32), pltpu.VMEM((S * 12, 8, LEN), F32),
        pltpu.VMEM((T, D), F32), pltpu.VMEM((T, D), BF16), pltpu.VMEM((T, FF), BF16), pltpu.VMEM((2, ROWS, 1024), BF16),
        pltpu.VMEM((T, D), BF16), pltpu.VMEM((8, FF), F32), pltpu.VMEM((16, 256), F32),
        DMA((len(widths), sem_count(Z))), DMA((len(widths), sem_count(Z))), DMA((3,)), DMA((16,)), DMA((2,)),
    ]
    return pl.pallas_call(
        functools.partial(forward_kernel, Z, Y, FORWARD_PLAN),
        out_shape=outs,
        in_specs=[ANY, ANY] + [VMEM] * 15,
        out_specs=[ANY] * 14 + [VMEM] * 3,
        scratch_shapes=scratch,
        compiler_params=pltpu.CompilerParams(collective_id=0, has_side_effects=True, vmem_limit_bytes=VMEM_LIMIT),
        name="forward",
    )(x, cot, segment, valid, *shards, *vectors)


def pack(net, buf, left, right):
    width = left.shape[1]

    def owner(i):
        rows = aligned(i, 24)
        v = jnp.concatenate([left[rows, :], right[rows, :]], axis=0).astype(BF16)
        buf[net.place(i) + (ALL, slice(0, width))] = v

    loop(BLOCKS, owner)


def all_sum_steps(net, mine, theirs, sems):
    partners = ["c", "x", "y"] if net.Y == 2 else ["c", "x"]
    devices = [net.across(axis) for axis in partners]
    bit = 1
    while bit < net.Z:
        z = net.at["z"]
        devices.append(net.device(z=z + bit - 2 * bit * ((z // bit) % 2)))
        bit *= 2
    copies = [remote(mine.at[k], theirs.at[k], sems, k, device) for k, device in enumerate(devices)]

    def step(k):
        if k > 0:
            copies[k - 1].wait_recv()
            mine[k] = mine[k - 1] + theirs[k - 1]
        if k < len(copies):
            copies[k].start()

    return [lambda k=k: step(k) for k in range(len(copies) + 1)], copies


def rounds_of(Z, Y):
    assert 2 ** (Z - 1).bit_length() == Z
    return 2 + (Y == 2) + (Z - 1).bit_length()


def attend_back(qkv, do, mask_t, lse, d, small, seq, p, u):
    T = do.shape[0]
    rows = aligned(seq, LEN)
    lanes = aligned(p, 128)
    q, k, v = (qkv[pl.ds(pl.multiple_of(j * T + seq * LEN, LEN), LEN), lanes] for j in range(3))
    g = do[rows, lanes]
    kt = k.T
    dk = dv = None
    dqt = []
    for h in range(2):
        here = head_mask(h, k.shape)
        km, vm, qm, gm = (jnp.where(here, a, jnp.zeros_like(a)) for a in (k, v, q, g))
        t = dot(km, q, NT) * (0.125 * LOG2E) + mask_t[seq] - lse[seq * 2 * PAIRS + 2 * p + h, 0:1, :]
        pt = jnp.exp2(t)
        dp = dot(vm, g, NT)
        w = pt * dp
        ds = (w - pt * jnp.sum(w, axis=0, keepdims=True)).astype(BF16)
        dvh = dot(pt.astype(BF16), gm)
        dkh = dot(ds, qm)
        dv = dvh if dv is None else dv + dvh
        dk = dkh if dk is None else dk + dkh
        dqt.append(dot(kt[64 * h : 64 * h + 64, :], ds))
    dq = (jnp.concatenate(dqt, axis=0).T * 0.125).astype(BF16)
    dv = dv.astype(BF16)
    d[rows, aligned(u, 128)] = dq
    d[rows, pl.ds(pl.multiple_of(256 + u * 128, 128), 128)] = (dk * 0.125).astype(BF16)
    d[rows, pl.ds(pl.multiple_of(512 + u * 128, 128), 128)] = dv
    small[1:2, lanes] += down_sum(dq.astype(F32))
    small[1:2, pl.ds(pl.multiple_of(D + p * 128, 128), 128)] += down_sum(dv.astype(F32))


def pack_small(net, buf, small):
    for i in range(BLOCKS):
        rows = []
        for k in range(2):
            tile = 24 * i // 128 + k
            for row in (1, 2):
                for j in range(4):
                    at = j * D + tile * 128
                    rows.append(small[row : row + 1, at : at + 128])
            at = (96 * i // 128 + k) * 128
            rows.append(small[0:8, at : at + 128])
        buf[net.place(i) + (slice(0, 32), slice(384, 512))] = jnp.concatenate(rows, axis=0).astype(BF16)


def backward_kernel(Z, Y, plan, *refs):
    (act_h, gp_h, df_h, dsec_h, normed_h, res_h, att_h, qkv_h, x_h, w1_h, w2_h, w_out_h, w_in_h) = refs[:13]
    vec, small_in, stats_in, segment, valid, lse = refs[13:19]
    dx_h, w2_own, w1_own, out_own, in_own, stats = refs[19:25]
    parts = refs[25:32]
    (df, wide, normed, normed_t, att, res, w1, w2, w_out, act, gp, dh, dw, mask_t, small, sum_mine, sum_theirs) = refs[32:49]
    ssem, rsem, sss, srs, loads, chunks, outs = refs[49:56]
    land = refs[56:]
    net = Net(Z, Y)
    T = df.shape[0]
    seqs, blocks = T // LEN, T // ROWS
    plan = list(plan)

    def load(src, dst, k):
        return pltpu.make_async_copy(src, dst, loads.at[k])

    def act_copy(j):
        return pltpu.make_async_copy(act_h.at[:, aligned(j, 384)], act.at[j % 2], chunks.at[j % 2])

    def gp_copy(t):
        return pltpu.make_async_copy(gp_h.at[:, pl.ds(t * 1024, 1024)], gp.at[t % 2], chunks.at[2 + t % 2])

    load_df = load(df_h, df, 0)
    load_w2 = load(w2_h, w2, 1)
    load_normed = load(normed_h, normed, 2)
    load_w1 = load(w1_h, w1, 3)
    load_dsec = load(dsec_h, wide, 4)
    load_res, load_att, load_out = load(res_h, res, 5), load(att_h, att, 6), load(w_out_h, w_out, 7)
    load_qkv, load_in, load_x = load(qkv_h, w2, 8), load(w_in_h, w1.at[:, pl.ds(0, 3 * D)], 9), load(x_h, att, 10)
    act_copy(0).start()
    load_df.start()
    act_copy(1).start()
    small[:, :FF] = small_in[...]
    small[:, FF:] = jnp.zeros((8, 128), F32)
    sum_mine[0] = stats_in[...]
    for s in range(seqs):
        seg = segment[s : s + 1, :].astype(F32)
        build_mask(mask_t.at[s], jnp.where(valid[s : s + 1, :] > 0, seg, -1.0), seg)
    net.barrier()
    load_df.wait()
    waiting = (load_w2, load_normed, gp_copy(0), load_dsec, load_w1, gp_copy(1), load_res, load_att)

    def shrink_step(j):
        spread(j, 0, [copy.start for copy in waiting])
        act_copy(j).wait()
        v = dot(act[j % 2], df[...], TN).astype(BF16)
        for k in range(4):
            place = net.place(4 * j + k)
            for t in range(3):
                c = slice(256 * t, 256 * t + 256)
                parts[t][place + (ALL, slice(0, 256))] = v[96 * k : 96 * k + 48, c]
                parts[t][place + (ALL, slice(256, 512))] = v[96 * k + 48 : 96 * k + 96, c]
        pl.when(j + 2 < FF // 384)(lambda: act_copy(j + 2).start())

    loop(FF // 384, shrink_step)
    load_out.start()
    steps, moves = [], []
    for g in range(10):
        group = parts[g] if g < 7 else parts[g - 7]
        lines = land[7 * (g % 7) : 7 * (g % 7) + 7]
        if g in (7, 8):
            group, *lines = (r.at[(ALL,) * (len(r.shape) - 1) + (pl.ds(0, 384),)] for r in (group, *lines))
        calls, sends = scatter_steps(net, group, lines, (ssem.at[g], rsem.at[g]), finish_of(g, w2_own, w1_own, out_own, in_own))
        steps.append(calls)
        moves.append(sends)
    sum_calls, sum_copies = all_sum_steps(net, sum_mine, sum_theirs, (sss, srs))

    def move():
        todo = [steps[g][k] for g, k in plan.pop(0)]
        if sum_calls:
            todo.append(sum_calls.pop(0))
        return together(todo)

    def sent(g):
        for copies in moves[g]:
            copies.sent()

    move()()
    load_normed.wait()

    def turn(j):
        lanes = aligned(j, 128)
        normed_t[lanes, :] = normed[:, lanes].T

    loop(D // 128, turn)
    move()()
    load_w2.wait()
    load_w1.wait()
    load_dsec.wait()
    for t in range(3):
        gp_copy(t).wait()
        c = slice(t * 1024, (t + 1) * 1024)
        inner = [move(), move()]

        def expand_step(i, t=t, c=c):
            spread(i, 0, inner)
            r = aligned(i, 2 * ROWS)
            d = (dot(df[r, :], w2[c, :], NT) * gp[t % 2, r, :].astype(F32)).astype(BF16)
            dh[r, :] = d
            small[0:1, c] += down_sum(d.astype(F32))
            wide[r, :] += dot(d, w1[:, c], NT)

        loop(blocks // 2, expand_step)
        if t == 0:
            gp_copy(2).start()
        move()()
        dw[...] = dot(normed_t[...], dh[...])
        pack(net, parts[3 + t], dw.at[:, :512], dw.at[:, 512:])
        move()()
    load_qkv.start()
    load_in.start()
    load_res.wait()
    load_att.wait()
    load_out.wait()
    inner = [move() for _ in range(blocks)]

    def norm_step(i):
        spread(i, 0, inner)
        r = aligned(i, ROWS)
        n, rsd = normalise(res[r, :])
        g = wide[r, :]
        grad = norm_back(g, n, rsd, vec[3:4, :])
        wide[r, :] = grad
        low = grad.astype(BF16)
        df[r, :] = low
        add_small(small, "fg", down_sum(g * n))
        add_small(small, "fs", down_sum(g))
        add_small(small, "ob", down_sum(low.astype(F32)))
        normed[r, :] = dot(low, w_out[...], NT).astype(BF16)

    loop(blocks, norm_step)
    dw[:, :D] = dot(att[...], df[...], TN)
    load_x.start()
    pack(net, parts[6], dw.at[:, :384], dw.at[:, 384:D])
    move()()
    load_qkv.wait()
    d = (dh.at[:, pl.ds(0, D)], gp.at[0, :, pl.ds(0, D)], gp.at[1, :, pl.ds(0, D)])
    for t in range(3):
        inner = [move() for _ in range(2 * seqs)]

        def attend_step(i, t=t):
            spread(i, 0, inner)
            attend_back(w2, normed, mask_t, lse, d[t], small, i // 2, 2 * t + i % 2, i % 2)

        loop(2 * seqs, attend_step)
        if t == 0:
            load_x.wait()

            def turn_x(j):
                lanes = aligned(j, 128)
                normed_t[lanes, :] = att[:, lanes].T

            loop(D // 128, turn_x)
        dw[:, :D] = dot(normed_t[...], d[t][...])
        sent(t)
        pack(net, parts[t], dw.at[:, :384], dw.at[:, 384:D])
        if t == 2:
            pack_small(net, parts[t], small)
            parts[t][:, :, :, :, 32:48, 384:512] = jnp.zeros(parts[t].shape[:4] + (16, 128), BF16)
        move()()
    load_in.wait()
    inner = [move() for _ in range(blocks)]

    def token_step(i):
        spread(i, 0, inner)
        r = aligned(i, ROWS)
        wide[r, :] += sum(dot(d[t][r, :], w1[:, t * D : (t + 1) * D], NT) for t in range(3))

    loop(blocks, token_step)
    store = pltpu.make_async_copy(wide, dx_h, outs.at[0])
    store.start()
    stats[...] = sum_mine[len(sum_copies)]
    move()()
    assert not plan
    store.wait()
    for copy in sum_copies:
        copy.wait_send()
    for g in range(3, 10):
        sent(g)


def finish_of(g, w2_own, w1_own, out_own, in_own):
    def finish(first, rows, total):
        if g < 3:
            w2_own[first : first + rows, g * 256 : (g + 1) * 256] = total[:, :256]
            w2_own[48 + first : 48 + first + rows, g * 256 : (g + 1) * 256] = total[:, 256:]
        else:
            own = w1_own.at[g - 3] if g < 6 else out_own if g == 6 else in_own.at[g - 7]
            own[first : first + rows, : total.shape[1]] = total

    return finish


def backward(Z, Y, act, gp, df, dsec, normed, res, att, qkv, x, w1, w2, w_out, w_in, vec, small, stats, segment, valid, lse):
    T, S = df.shape[0], segment.shape[0]
    blocks = (2, 2, Y, Z, 48)
    rounds = rounds_of(Z, Y)
    outs = [
        SDS((T, D), F32), SDS((96, D), F32), SDS((3, 48, 512), F32), SDS((48, 384), F32), SDS((3, 48, 512), F32), SDS((8, 128), F32),
    ]
    rows = pltpu.VMEM((T, D), BF16)
    scratch = [pltpu.VMEM(blocks + (512,), BF16)] * 6 + [
        pltpu.VMEM(blocks + (384,), BF16),
        rows, pltpu.VMEM((T, D), F32), rows, pltpu.VMEM((D, T), BF16), rows, pltpu.VMEM((T, D), F32),
        pltpu.VMEM((D, FF), BF16), pltpu.VMEM((FF, D), BF16), pltpu.VMEM((D, D), BF16),
        pltpu.VMEM((2, T, 384), BF16), pltpu.VMEM((2, T, 1024), BF16), pltpu.VMEM((T, 1024), BF16),
        pltpu.VMEM((D, 1024), F32), pltpu.VMEM((S, LEN, LEN), F32), pltpu.VMEM((8, FF + 128), F32),
        pltpu.VMEM((rounds + 1, 8, 128), F32), pltpu.VMEM((rounds, 8, 128), F32),
        DMA((10, sem_count(Z))), DMA((10, sem_count(Z))), DMA((rounds,)), DMA((rounds,)), DMA((11,)), DMA((4,)), DMA((1,)),
    ] + lands(Z, Y, 512) * 6 + lands(Z, Y, 384)
    return pl.pallas_call(
        functools.partial(backward_kernel, Z, Y, BACKWARD_PLAN),
        out_shape=outs,
        in_specs=[ANY] * 13 + [VMEM] * 6,
        out_specs=[ANY] + [VMEM] * 5,
        scratch_shapes=scratch,
        compiler_params=pltpu.CompilerParams(collective_id=1, has_side_effects=True, vmem_limit_bytes=VMEM_LIMIT),
        name="backward",
    )(act, gp, df, dsec, normed, res, att, qkv, x, w1, w2, w_out, w_in, vec, small, stats, segment, valid, lse)


def hand_out_kernel(own_index, in_own, out_own, w1_own, w2_own, stats, *refs):
    w_in, w_out, w1, w2, mean, exp = refs[:6]
    vectors = refs[6:]
    for t in range(3):
        v = in_own[t, :, :384]
        v = jnp.concatenate([v[:24], v[24:]], axis=1)
        for j in range(3):
            w_in[:, j * D + t * 256 : j * D + (t + 1) * 256] = v[:, j * 256 : (j + 1) * 256]
        w1[:, t * 1024 : t * 1024 + 512] = w1_own[t, :24, :]
        w1[:, t * 1024 + 512 : (t + 1) * 1024] = w1_own[t, 24:, :]
    w_out[:, :384] = out_own[:24, :]
    w_out[:, 384:] = out_own[24:, :]
    w2[...] = w2_own[...]
    i = own_index()

    def window(first, rows, at):
        pair = jnp.concatenate([in_own[2, first : first + rows, 384:], in_own[2, 16 + first : 16 + first + rows, 384:]], axis=1)
        return pltpu.roll(pair, (256 - at % 128) % 256, axis=1)

    w = window(0, 8, 24 * i)
    for k in range(8):
        vectors[k][...] = w[k : k + 1, :24]
    exp[...] = window(8, 8, 96 * i)[0:1, :96]
    lane = lax.broadcasted_iota(jnp.int32, (1, 128), 1)
    total = jnp.sum(stats[...], axis=1, keepdims=True)
    packed = jnp.zeros((1, 128), F32)
    for k in range(5):
        packed = jnp.where(lane == k, total[k : k + 1, :], packed)
    mean[...] = packed


def hand_out(Z, Y, in_own, out_own, w1_own, w2_own, stats):
    def own_index():
        return lax.axis_index("dp") * Y + (lax.axis_index("fsdp") if Y == 2 else 0)

    outs = [
        SDS((24, 3 * D), F32), SDS((24, D), F32), SDS((24, FF), F32), SDS((96, D), F32), SDS((1, 128), F32), SDS((1, 96), F32),
    ] + [SDS((1, 24), F32)] * 8
    return pl.pallas_call(
        functools.partial(hand_out_kernel, own_index),
        out_shape=outs,
        in_specs=[VMEM] * 5,
        out_specs=[VMEM] * len(outs),
        name="hand_out",
    )(in_own, out_own, w1_own, w2_own, stats)


def per_device(
    Z, Y, fsdp, tokens, segment_ids, valid, input_weight, query_bias, value_bias, output_weight, output_bias,
    first_gain, first_shift, expand_weight, expand_bias, shrink_weight, shrink_bias, second_gain, second_shift, cotangent,
):
    shards = (input_weight, output_weight, expand_weight, shrink_weight)
    vectors = (query_bias, value_bias, output_bias, first_gain, first_shift, expand_bias, shrink_bias, second_gain, second_shift)
    split = Y == 1 and fsdp > 1
    if split:
        def whole(v):
            return lax.all_gather(v, "fsdp", axis=0, tiled=True)

        shards, vectors = tuple(map(whole, shards)), tuple(map(whole, vectors))
    vectors = [v.reshape(1, -1) for v in vectors]
    (res, qkv, att, normed, act, gp, df, lse, w_in, w_out, w1, w2, result, dsec, vec, small, stats) = forward(
        Z, Y, tokens, cotangent, segment_ids, valid, shards, vectors
    )
    dx, w2_own, w1_own, out_own, in_own, stats = backward(
        Z, Y, act, gp, df, dsec, normed, res, att, qkv, tokens, w1, w2, w_out, w_in, vec, small, stats, segment_ids, valid, lse
    )
    (*weights, stats, exp_own, qb, vb, ob, fg, fs, sb, sg, ss) = hand_out(Z, Y, in_own, out_own, w1_own, w2_own, stats)
    own = [v.reshape(-1) for v in (qb, vb, ob, fg, fs, sb, sg, ss, exp_own)]
    totals = stats[0, :5]
    if split:
        def share(v):
            return lax.psum_scatter(v, "fsdp", scatter_dimension=0, tiled=True)

        weights, own = [share(v) for v in weights], [share(v) for v in own]
        totals = lax.psum(totals, "fsdp")
    qb, vb, ob, fg, fs, sb, sg, ss, exp_own = own
    return (
        result, dx, totals[:4] / (D * totals[4]), weights[0], qb, vb, weights[1], ob, fg, fs,
        weights[2], exp_own, weights[3], sb, sg, ss,
    )


def solution(mesh):
    dp, fsdp = mesh.shape["dp"], mesh.shape["fsdp"]
    Z, Y = dp // 4, (2 if dp * fsdp == BLOCKS else 1)
    matrix, vector = P(("dp", "fsdp"), None), P(("dp", "fsdp"))
    params = (matrix, vector, vector, matrix, vector, vector, vector, matrix, vector, matrix, vector, vector, vector)
    return jax.shard_map(
        functools.partial(per_device, Z, Y, fsdp),
        mesh=mesh,
        in_specs=(matrix, matrix, matrix) + params + (matrix,),
        out_specs=(matrix, matrix, P()) + params,
        check_vma=False,
    )
```

```python
import functools

import jax
import jax.numpy as jnp
from jax import lax
from jax.experimental import pallas as pl
from jax.experimental.pallas import tpu as pltpu
from jax.sharding import PartitionSpec as P

BLOCKS = 32
F32, BF16 = jnp.float32, jnp.bfloat16
LOG2E = 1.4426950408889634
MESH = pl.DeviceIdType.MESH
ALL = slice(None)
ANY = pl.BlockSpec(memory_space=pl.ANY)
VMEM = pl.BlockSpec(memory_space=pltpu.VMEM)
SDS = jax.ShapeDtypeStruct
DMA = pltpu.SemaphoreType.DMA
NT = (((1,), (1,)), ((), ()))
TN = (((0,), (0,)), ((), ()))
NN = (((1,), (0,)), ((), ()))
D, FF, LEN, PAIRS = 768, 3072, 512, 6
ROWS = 256


def dot(a, b, dims=NN):
    return lax.dot_general(a, b, dims, preferred_element_type=F32)


def aligned(at, step, size=None):
    return pl.ds(pl.multiple_of(at * step, step), step if size is None else size)


def loop(count, body):
    def step(i, carry):
        body(i)
        return carry

    lax.fori_loop(0, count, step, 0)


VMEM_LIMIT = 63 * 2**20


class Net:
    def __init__(self, Z, Y):
        self.Z, self.Y = Z, Y
        dp, y = lax.axis_index("dp"), lax.axis_index("fsdp")
        self.fsdp = y
        self.at = {"z": dp // 4, "x": (dp // 2) % 2, "c": dp % 2, "y": y if Y == 2 else 0}
        self.own = dp * Y + (y if Y == 2 else 0)

    def device(self, **moved):
        p = dict(self.at, **moved)
        return (p["z"] * 4 + p["x"] * 2 + p["c"], p["y"] if self.Y == 2 else self.fsdp)

    def across(self, axis):
        return self.device(**{axis: 1 - self.at[axis]})

    def z_away(self, k):
        return (self.at["z"] + k) % self.Z

    def barrier(self):
        bar = pltpu.get_barrier_semaphore()
        others = [self.across(axis) for axis in (["c", "x", "y"] if self.Y == 2 else ["c", "x"])]
        others += [self.device(z=self.z_away(k)) for k in range(1, self.Z)]
        for other in others:
            pl.semaphore_signal(bar, inc=1, device_id=other, device_id_type=MESH)
        pl.semaphore_wait(bar, len(others))

    def place(self, i):
        Y = self.Y
        return ((i // Y) % 2, (i // (2 * Y)) % 2, i % Y, i // (4 * Y))

    def mine(self):
        at = self.at
        return (at["c"], at["x"], at["y"], at["z"])


STEPS = 5


def halves(buf):
    low = buf.shape[4] // 3
    return pl.ds(0, 2 * low), pl.ds(2 * low, low)


def sem_count(Z):
    return 2 * (Z - 1) + 5


def sem_ids(Z):
    n = Z - 1
    return {"tz": 0, "lz": n, "tx": 2 * n, "ty": 2 * n + 1, "lx": 2 * n + 2, "ly": 2 * n + 3, "c": 2 * n + 4}


def remote(src, dst, sems, sem, device):
    return pltpu.make_async_remote_copy(
        src_ref=src,
        dst_ref=dst,
        send_sem=sems[0].at[sem],
        recv_sem=sems[1].at[sem],
        device_id=device,
        device_id_type=MESH,
    )


class Move:
    def __init__(self, pairs):
        self.pairs = pairs

    def start(self):
        for send, _ in self.pairs:
            send().start()

    def receive(self):
        for _, take in self.pairs:
            take().wait_recv()

    def sent(self):
        for send, _ in self.pairs:
            send().wait_send()


def gather_moves(net, buf, sems):
    Z, Y, at, ids = net.Z, net.Y, net.at, sem_ids(net.Z)
    c, x, y, z = at["c"], at["x"], at["y"], at["z"]
    TOP, LOW = halves(buf)

    def swap(axis, ours, theirs, sem):
        device = net.across(axis)
        return [(lambda: remote(ours(), ours(), sems, sem, device), lambda: remote(theirs(), theirs(), sems, sem, device))]

    def along_z(part, sem):
        def pair(k):
            return (
                lambda: remote(part(z), part(z), sems, sem + k - 1, net.device(z=net.z_away(k))),
                lambda: remote(part(net.z_away(Z - k)), part(net.z_away(Z - k)), sems, sem + k - 1, net.device(z=net.z_away(k))),
            )

        return [pair(k) for k in range(1, Z)]

    yy = y if Y == 1 else ALL
    moves = [
        along_z(lambda zz: buf.at[c, x, y, zz, TOP], ids["tz"]),
        swap("x", lambda: buf.at[c, x, y, :, TOP], lambda: buf.at[c, 1 - x, y, :, TOP], ids["tx"])
        + along_z(lambda zz: buf.at[c, x, yy, zz, LOW], ids["lz"]),
        swap("x", lambda: buf.at[c, x, yy, :, LOW], lambda: buf.at[c, 1 - x, yy, :, LOW], ids["lx"]),
        swap("c", lambda: buf.at[c], lambda: buf.at[1 - c], ids["c"]),
    ]
    if Y == 2:
        moves[0] += swap("y", lambda: buf.at[c, x, y, z, LOW], lambda: buf.at[c, x, 1 - y, z, LOW], ids["ly"])
        moves[2] += swap("y", lambda: buf.at[c, :, y, :, TOP], lambda: buf.at[c, :, 1 - y, :, TOP], ids["ty"])
    return [Move(pairs) for pairs in moves]


def gather_steps(net, buf, sems):
    moves = gather_moves(net, buf, sems)

    def step(k):
        if k > 0:
            moves[k - 1].receive()
        if k < len(moves):
            moves[k].start()

    return [lambda k=k: step(k) for k in range(STEPS)], moves


def lands(Z, Y, rows, width):
    low = rows // 3
    top = 2 * low
    shapes = [(2, Y, Z, rows), (2, Z, top), (Y, Z, low), (Z, top), (Z - 1, Y, low), (Z - 1, top), (low,)]
    return [pltpu.VMEM(shape + (width,), BF16) for shape in shapes]


def add_blocks(count, at, dst, src):
    def one(i):
        idx = at(i)
        dst[idx] = dst[idx] + src[idx]

    loop(count, one)


def scatter_steps(net, buf, land, sems, finish):
    Z, Y, at, ids = net.Z, net.Y, net.at, sem_ids(net.Z)
    c, x, y, z = at["c"], at["x"], at["y"], at["z"]
    core, top_y, low_x, top_x, low_z, top_z, low_y = land
    TOP, LOW = halves(buf)
    low = buf.shape[4] // 3

    def swap(axis, what, where, sem):
        device = net.across(axis)

        def make():
            return remote(what(), where, sems, sem, device)

        return [(make, make)]

    def along_z(part, where, sem):
        def make(k):
            return lambda: remote(part(net.z_away(k)), where.at[k - 1], sems, sem + k - 1, net.device(z=net.z_away(k)))

        return [(make(k), make(k)) for k in range(1, Z)]

    yy = y if Y == 1 else ALL
    low_x_land, low_z_land = (low_x.at[0], low_z.at[:, 0]) if Y == 1 else (low_x, low_z)
    moves = [
        swap("c", lambda: buf.at[1 - c], core, ids["c"]),
        swap("x", lambda: buf.at[c, 1 - x, yy, :, LOW], low_x_land, ids["lx"]),
        swap("x", lambda: buf.at[c, 1 - x, y, :, TOP], top_x, ids["tx"])
        + along_z(lambda zz: buf.at[c, x, yy, zz, LOW], low_z_land, ids["lz"]),
        along_z(lambda zz: buf.at[c, x, y, zz, TOP], top_z, ids["tz"]),
    ]
    if Y == 2:
        moves[1] += swap("y", lambda: buf.at[c, :, 1 - y, :, TOP], top_y, ids["ty"])
        moves[3] += swap("y", lambda: buf.at[c, x, 1 - y, z, LOW], low_y, ids["ly"])
    moves = [Move(pairs) for pairs in moves]

    def sum_z(mine, where):
        total = mine.astype(F32)
        for k in range(Z - 1):
            total = total + where(k).astype(F32)
        return total

    def step(k):
        if k > 0:
            moves[k - 1].receive()
        if k == 1:
            add_blocks(2 * Y * Z, lambda i: (i // (Y * Z), (i // Z) % Y, i % Z), buf.at[c], core)
        if k == 2:
            if Y == 2:
                add_blocks(2 * Z, lambda i: (i // Z, i % Z), buf.at[c, :, y, :, TOP], top_y)
            add_blocks(Y * Z, lambda i: (i // Z, i % Z), buf.at[c, x, :, :, LOW], low_x)
        if k == 3:
            add_blocks(Z, lambda i: (i,), buf.at[c, x, y, :, TOP], top_x)
            for j in range(Y):
                own = buf.at[c, x, j, z, LOW]
                own[...] = sum_z(own[...], lambda i: low_z[i, j]).astype(BF16)
        if k < 4:
            moves[k].start()
        else:
            finish(0, 2 * low, sum_z(buf[c, x, y, z, TOP], lambda i: top_z[i]))
            rest = buf[c, x, y, z, LOW].astype(F32)
            finish(2 * low, low, rest + low_y[...].astype(F32) if Y == 2 else rest)

    return [lambda k=k: step(k) for k in range(STEPS)], moves


def together(todo):
    def call():
        for one in todo:
            one()

    return call


def train(steps, offsets):
    calls = []
    for t in range(len(steps) + offsets[-1]):
        todo = [steps[g][k] for g in range(len(steps)) for k in range(STEPS) if g + offsets[k] == t]
        calls.append(together(todo))
    return calls


def spread(i, first, calls, every=1):
    for k, call in enumerate(calls):
        pl.when(i == first + k * every)(call)


FORWARD_PLAN = (
    ((0, 0), (1, 0), (2, 0), (0, 1), (1, 1), (3, 0), (0, 2), (2, 1), (1, 2), (4, 0), (3, 1), (5, 0), (0, 3), (2, 2),),
    ((0, 4),),
    (),
    ((1, 3),),
    ((4, 1), (3, 2),),
    ((6, 0),),
    ((1, 4),),
    ((2, 3), (5, 1),),
    ((7, 0),),
    ((4, 2),),
    (),
    ((3, 3), (2, 4),),
    ((6, 1),),
    ((8, 0),),
    ((3, 4), (5, 2),),
    (),
    ((4, 3),),
    (),
    ((7, 1),),
    ((4, 4), (6, 2),),
    (),
    (),
    ((9, 0), (8, 1), (10, 0),),
    ((5, 3),),
    ((7, 2),),
    (),
    (),
    ((9, 1),),
    ((6, 3),),
    ((8, 2),),
    ((5, 4),),
    (),
    ((7, 3),),
    ((6, 4),),
    (),
    ((10, 1), (9, 2),),
    (),
    (),
    ((8, 3),),
    (),
    ((7, 4), (10, 2),),
    (),
    ((8, 4),),
    (),
    (),
    ((9, 3),),
    (),
    (),
    ((10, 3), (9, 4),),
    (),
    (),
    ((10, 4),),
)

BACKWARD_PLAN = (
    (),
    (),
    ((0, 0),),
    (),
    ((0, 1),),
    (),
    ((3, 0),),
    (),
    ((3, 1), (2, 0),),
    (),
    ((1, 0), (0, 2),),
    ((4, 0),),
    ((1, 1),),
    ((5, 0),),
    ((4, 1),),
    (),
    (),
    ((3, 2), (0, 3),),
    (),
    (),
    ((5, 1),),
    ((3, 3), (4, 2), (0, 4), (2, 1),),
    ((1, 2), (6, 0),),
    ((6, 1),),
    ((7, 0),),
    ((1, 3), (2, 2),),
    ((5, 2),),
    ((7, 1), (1, 4), (6, 2),),
    ((8, 0), (2, 3), (5, 3),),
    ((4, 3),),
    ((8, 1),),
    ((9, 0),),
    ((6, 3), (7, 2),),
    ((9, 1),),
    ((10, 0), (5, 4), (3, 4),),
    ((9, 2), (7, 3),),
    ((4, 4), (10, 1), (8, 2), (2, 4),),
    ((9, 3),),
    (),
    ((10, 2), (8, 3), (9, 4), (10, 3), (8, 4), (7, 4), (6, 4), (10, 4),),
)


def head_mask(head, shape):
    lane = lax.broadcasted_iota(jnp.int32, shape, len(shape) - 1)
    return (lane < 64) if head == 0 else (lane >= 64)


def column(row, count=128):
    return jnp.broadcast_to(row, (count, row.shape[1])).T


def build_mask(mask, down, across):
    n = mask.shape[0]
    down = column(down)
    at = lax.broadcasted_iota(jnp.int32, (n, 128), 0)
    lane = lax.broadcasted_iota(jnp.int32, (n, 128), 1)
    for j in range(n // 128):
        tile = slice(j * 128, (j + 1) * 128)
        mask[:, tile] = jnp.where((down == across[:, tile]) | (at == lane + j * 128), 0.0, -1e30).astype(mask.dtype)


def gelu_pair(h):
    cdf = 0.5 + 0.5 * lax.erf(h * 0.7071067811865476)
    return h * cdf, cdf + h * jnp.exp2(h * h * (-0.5 * LOG2E)) * 0.3989422804014327


def normalise(v):
    centred = v - jnp.sum(v, axis=1, keepdims=True) * (1.0 / D)
    r = lax.rsqrt(jnp.sum(centred * centred, axis=1, keepdims=True) * (1.0 / D) + 1e-12)
    return centred * r, r


def norm_back(g, n, r, gain):
    scaled = g * gain
    mean = jnp.sum(scaled, axis=1, keepdims=True) * (1.0 / D)
    along = jnp.sum(scaled * n, axis=1, keepdims=True) * (1.0 / D)
    return r * (scaled - mean - n * along)


def down_sum(v):
    return jnp.sum(v, axis=0, keepdims=True)


def square_sum(value, counted):
    v = value.astype(BF16).astype(F32)
    v = v * v
    total = v[:, :128]
    for j in range(1, D // 128):
        total = total + v[:, j * 128 : (j + 1) * 128]
    return down_sum(total * counted)


def fold(rows, half):
    return jnp.concatenate([rows[:, :half], rows[:, half:]], axis=0).astype(BF16)


def unfold(net, buf, half, dst, at=0):
    def pair(p):
        a = buf[net.place(2 * p) + (ALL, slice(0, half))].astype(F32)
        b = buf[net.place(2 * p + 1) + (ALL, slice(0, half))].astype(F32)
        rows = aligned(p, 48)
        dst[rows, at : at + half] = jnp.concatenate([a[:24], b[:24]], axis=0).astype(BF16)
        dst[rows, at + half : at + 2 * half] = jnp.concatenate([a[24:], b[24:]], axis=0).astype(BF16)

    loop(BLOCKS // 2, pair)


SMALL = ("qb", "vb", "ob", "fg", "fs", "sb", "sg", "ss")


def add_small(small, name, value):
    k = SMALL.index(name)
    small[k : k + 1, :D] += value


def pair_block(rows, last):
    return jnp.concatenate([rows[:, :128], rows[:, 128:256], rows[:, 256:], last], axis=0).astype(BF16)


def unfold_pair(net, buf, dst, at):
    def pair(p):
        a = buf[net.place(2 * p)].astype(F32)
        b = buf[net.place(2 * p + 1)].astype(F32)
        rows = aligned(p, 48)
        for j in range(3):
            part = slice(24 * j, 24 * j + 24)
            dst[rows, at + 128 * j : at + 128 * (j + 1)] = jnp.concatenate([a[part], b[part]], axis=0).astype(BF16)

    loop(BLOCKS // 2, pair)


def small_rows(vectors, expand, tmp):
    tmp[...] = jnp.zeros_like(tmp)
    for k, ref in enumerate(vectors):
        tmp[k : k + 1, :24] = ref[...].astype(F32)
    tmp[8:9, :96] = expand[...].astype(F32)
    return tmp[...]


def small_params(net, buf, vec, exp):
    vec[...] = jnp.zeros_like(vec)
    exp[...] = jnp.zeros_like(exp)
    for i in range(BLOCKS):
        w = buf[net.place(i) + (slice(64, 96), ALL)].astype(F32)
        for ref, first, at in ((vec, 8, 24 * i), (exp, 16, 96 * i)):
            part = jnp.concatenate([w[first : first + 8], jnp.zeros((8, 128), F32)], axis=1)
            if at % 128:
                part = pltpu.roll(part, at % 128, axis=1)
            tile = at // 128
            wide = min(256, ref.shape[1] - tile * 128)
            ref[:, tile * 128 : tile * 128 + wide] += part[:, :wide]


def pair_of(rows, p):
    return jnp.concatenate([rows[:, j * D + p * 128 : j * D + (p + 1) * 128] for j in range(3)], axis=1)


def attend(qkv, mask, att, lse, seq, p):
    T = att.shape[0]
    base = pl.multiple_of(seq * LEN, LEN)
    lanes = aligned(p, 128)
    q, k, v = (qkv[pl.ds(pl.multiple_of(j * T + seq * LEN, LEN), LEN), lanes] for j in range(3))
    lane = lax.broadcasted_iota(jnp.int32, (LEN, 128), 1)
    zero = jnp.zeros_like(k)
    here = [head_mask(h, k.shape) for h in range(2)]
    scores = [dot(q, jnp.where(m, k, zero), NT) for m in here]
    weights, totals, logs = [], [], lse[pl.ds(base, LEN), :]
    for h in range(2):
        t = scores[h] * (0.125 * LOG2E) + mask[seq]
        top = jnp.max(t, axis=1, keepdims=True)
        e = jnp.exp2(t - top)
        total = jnp.sum(e, axis=1, keepdims=True)
        weights.append(e.astype(BF16))
        totals.append(total)
        logs = jnp.where(lane == 2 * p + h, top + jnp.log2(total), logs)
    out = sum(dot(weights[h], jnp.where(here[h], v, zero)) * (1.0 / totals[h]) for h in range(2))
    lse[pl.ds(base, LEN), :] = logs
    att[pl.ds(base, LEN), lanes] = out.astype(BF16)


def forward_kernel(Z, Y, plan, *refs):
    (x_h, cot_h, segment, valid, w_in_s, w_out_s, w1_s, w2_s, qb, vb, ob, fg, fs, eb, sb, sg, ss) = refs[:17]
    (res_h, qkv_h, att_h, normed_h, act_h, gp_h, df_h, lse_h, w_in_h, w_out_h, w1_h, w2_h, result_h, dsec_h) = refs[17:31]
    vec, small, stats = refs[31:34]
    bufs = refs[34:45]
    (w_in, w_out, w1, w2, x, qkv, mask, att, lse, lse_rows, wide, normed, act, gp, cot, exp, tmp) = refs[45:62]
    ssem, rsem, loads, outs, gsem = refs[62:]
    net = Net(Z, Y)
    T = x.shape[0]
    seqs = T // LEN
    blocks = T // ROWS

    load_x = pltpu.make_async_copy(x_h, x, loads.at[0])
    load_x.start()
    load_cot = pltpu.make_async_copy(cot_h, cot, loads.at[1])
    load_cot.start()
    mine = net.mine()
    own_in = w_in_s[...].astype(F32)
    own_1 = w1_s[...].astype(F32)
    bufs[0][mine] = pair_block(pair_of(own_in, 0), small_rows((qb, vb, ob, fg, fs, sb, sg, ss), eb, tmp))
    bufs[1][mine] = pair_block(pair_of(own_in, 1), jnp.zeros((24, 128), F32))
    for t in (1, 2):
        bufs[1 + t][mine] = jnp.concatenate([pair_of(own_in, 2 * t), pair_of(own_in, 2 * t + 1)], axis=0).astype(BF16)
    bufs[4][mine] = fold(w_out_s[...].astype(F32), 384)
    for t in range(3):
        bufs[5 + t][mine] = fold(own_1[:, t * 1024 : (t + 1) * 1024], 512)
        bufs[8 + t][mine + (ALL, slice(0, 256))] = w2_s[0:48, t * 256 : (t + 1) * 256]
        bufs[8 + t][mine + (ALL, slice(256, 512))] = w2_s[48:96, t * 256 : (t + 1) * 256]
    net.barrier()
    steps, moves = [], []
    for g, buf in enumerate(bufs):
        calls, sends = gather_steps(net, buf, (ssem.at[g], rsem.at[g]))
        steps.append(calls)
        moves += sends
    plan = list(plan)

    def move():
        return together([steps[g][k] for g, k in plan.pop(0)])

    move()()
    small[...] = jnp.zeros_like(small)
    stats[...] = jnp.zeros_like(stats)
    for s in range(seqs):
        seg = segment[s : s + 1, :].astype(F32)
        live = valid[s : s + 1, :].astype(F32)
        build_mask(mask.at[s], seg, jnp.where(live > 0, seg, -1.0))
        stats[4:5, :] += sum(live[:, j * 128 : (j + 1) * 128] for j in range(LEN // 128))
    lse[...] = jnp.zeros_like(lse)
    move()()
    small_params(net, bufs[0], vec, exp)
    load_x.wait()
    stores = []

    def store(src, dst):
        copy = pltpu.make_async_copy(src, dst, outs.at[len(stores)])
        copy.start()
        stores.append(copy)
        return copy

    for g, pairs in enumerate(((0,), (1,), (2, 3), (4, 5))):
        if g > 0:
            move()()
        first, count = pairs[0], len(pairs)
        if count == 1:
            unfold_pair(net, bufs[g], w_in, first * 384)
        else:
            unfold(net, bufs[g], 384, w_in, first * 384)
        inner = [move(), move()]

        def project(i):
            spread(i, 0, inner)
            r = aligned(i, 2 * ROWS)
            c = dot(x[r, :], w_in[:, first * 384 : (first + count) * 384])
            for u, p in enumerate(pairs):
                for j in range(3):
                    part = c[:, u * 384 + j * 128 : u * 384 + (j + 1) * 128]
                    if j != 1:
                        part = part + vec[j // 2 : j // 2 + 1, p * 128 : (p + 1) * 128]
                    rows = pl.ds(pl.multiple_of(j * T + i * 2 * ROWS, 2 * ROWS), 2 * ROWS)
                    qkv[rows, p * 128 : (p + 1) * 128] = part.astype(BF16)

        loop(blocks // 2, project)
        inner = [move() for _ in range(seqs * count)]

        def attend_step(i):
            spread(i, 0, inner)
            attend(qkv, mask, att, lse, i // count, first + i % count)

        loop(seqs * count, attend_step)
    store(qkv, qkv_h)
    store(w_in, w_in_h)
    store_att = store(att, att_h)
    for s in range(seqs):
        rows = lse[s * LEN : (s + 1) * LEN, :].T
        for h in range(2 * PAIRS):
            lse_rows[s * 2 * PAIRS + h] = jnp.broadcast_to(rows[h : h + 1, :], (8, LEN))
    store(lse_rows, lse_h)
    move()()
    unfold(net, bufs[4], 384, w_out)
    store(w_out, w_out_h)

    def out_step(i):
        spread(i, 0, inner)
        r = aligned(i, ROWS)
        branch = dot(att[r, :], w_out[...]) + vec[2:3, :]
        residual = x[r, :].astype(F32) + branch
        wide[r, :] = residual
        n, _ = normalise(residual)
        normed[r, :] = (n * vec[3:4, :] + vec[4:5, :]).astype(BF16)
        live = live_rows(i)
        stats[0:1, :] += square_sum(residual, live)
        stats[1:2, :] += square_sum(branch, live)

    def live_rows(i):
        return live_col[aligned(i, ROWS), :]

    live_col = lse
    for s in range(seqs):
        live_col[s * LEN : (s + 1) * LEN, :] = column(valid[s : s + 1, :].astype(F32))
    inner = [move() for _ in range(blocks)]
    loop(blocks, out_step)
    store_wide = store(wide, res_h)
    store(normed, normed_h)

    def gp_copy(t, i):
        slot = (t * blocks + i) % 2
        return pltpu.make_async_copy(
            gp.at[slot], gp_h.at[aligned(i, ROWS), pl.ds(t * 1024, 1024)], gsem.at[slot]
        )

    for t in range(3):
        move()()
        unfold(net, bufs[5 + t], 512, w1, t * 1024)
        inner = [move() for _ in range(blocks)]

        def expand_step(i):
            spread(i, 0, inner)
            r = aligned(i, ROWS)
            nv = normed[r, :]
            slot = (t * blocks + i) % 2
            if t == 0:
                pl.when(i >= 2)(lambda: gp_copy(t, i).wait())
            else:
                gp_copy(t, i).wait()
            for j in range(2):
                c = slice(t * 1024 + j * 512, t * 1024 + (j + 1) * 512)
                a, g = gelu_pair(dot(nv, w1[:, c]) + exp[0:1, c])
                act[r, c] = a.astype(BF16)
                gp[slot, :, j * 512 : (j + 1) * 512] = g.astype(BF16)
            gp_copy(t, i).start()

        loop(blocks, expand_step)
    store(w1, w1_h)
    store(act, act_h)
    store_wide.wait()
    for t in range(3):
        move()()

        def unfold_last(i, t=t):
            blk = bufs[8 + t].at[net.place(i)]
            c = slice(t * 256, (t + 1) * 256)
            w2[aligned(i, 96, 48), c] = blk[:, :256]
            w2[pl.ds(pl.multiple_of(i * 96 + 48, 48), 48), c] = blk[:, 256:]

        loop(BLOCKS, unfold_last)
        if t < 2:
            inner = [move(), move()]

            def shrink_step(i, t=t):
                spread(i, 0, inner)
                r = aligned(i, 2 * ROWS)
                wide[r, t * 256 : (t + 1) * 256] = dot(act[r, :], w2[:, t * 256 : (t + 1) * 256])

            loop(blocks // 2, shrink_step)
    assert not plan
    store(w2, w2_h)
    store_att.wait()
    load_cot.wait()

    def last_step(i):
        r = aligned(i, ROWS)
        feedfwd = jnp.concatenate([wide[r, :512], dot(act[r, :], w2[:, 512:])], axis=1) + vec[5:6, :]
        second = normed[r, :].astype(F32) + feedfwd
        n, rs = normalise(second)
        gain = vec[6:7, :]
        att[r, :] = (n * gain + vec[7:8, :]).astype(BF16)
        g = cot[r, :].astype(F32)
        grad = norm_back(g, n, rs, gain)
        wide[r, :] = grad
        low = grad.astype(BF16)
        x[r, :] = low
        add_small(small, "sg", down_sum(g * n))
        add_small(small, "ss", down_sum(g))
        add_small(small, "sb", down_sum(low.astype(F32)))
        live = live_rows(i)
        stats[2:3, :] += square_sum(second, live)
        stats[3:4, :] += square_sum(feedfwd, live)

    loop(blocks, last_step)
    ends = [
        pltpu.make_async_copy(wide, dsec_h, loads.at[0]),
        pltpu.make_async_copy(att, result_h, loads.at[1]),
        pltpu.make_async_copy(x, df_h, loads.at[2]),
    ]
    for copy in ends:
        copy.start()
    for k in (0, 1):
        gp_copy(2, blocks - 2 + k).wait()
    for copy in stores:
        if copy is not store_wide and copy is not store_att:
            copy.wait()
    for copy in ends:
        copy.wait()
    for move in moves:
        move.sent()


def forward(Z, Y, x, cot, segment, valid, shards, vectors):
    T, S = x.shape[0], segment.shape[0]
    blocks = (2, 2, Y, Z)
    shapes = ((96, 128),) * 2 + ((48, 384),) * 3 + ((48, 512),) * 6
    outs = [
        SDS((T, D), F32), SDS((3 * T, D), BF16), SDS((T, D), BF16), SDS((T, D), BF16),
        SDS((T, FF), BF16), SDS((T, FF), BF16), SDS((T, D), BF16), SDS((S * 12, 8, LEN), F32),
        SDS((D, 3 * D), BF16), SDS((D, D), BF16), SDS((D, FF), BF16), SDS((FF, D), BF16),
        SDS((T, D), BF16), SDS((T, D), F32), SDS((8, D), F32), SDS((8, D), F32), SDS((8, 128), F32),
    ]
    scratch = [pltpu.VMEM(blocks + shape, BF16) for shape in shapes] + [
        pltpu.VMEM((D, 3 * D), BF16), pltpu.VMEM((D, D), BF16), pltpu.VMEM((D, FF), BF16), pltpu.VMEM((FF, D), BF16),
        pltpu.VMEM((T, D), BF16), pltpu.VMEM((3 * T, D), BF16), pltpu.VMEM((S, LEN, LEN), F32),
        pltpu.VMEM((T, D), BF16), pltpu.VMEM((T, 128), F32), pltpu.VMEM((S * 12, 8, LEN), F32),
        pltpu.VMEM((T, D), F32), pltpu.VMEM((T, D), BF16), pltpu.VMEM((T, FF), BF16), pltpu.VMEM((2, ROWS, 1024), BF16),
        pltpu.VMEM((T, D), BF16), pltpu.VMEM((8, FF), F32), pltpu.VMEM((24, 128), F32),
        DMA((len(shapes), sem_count(Z))), DMA((len(shapes), sem_count(Z))), DMA((3,)), DMA((16,)), DMA((2,)),
    ]
    return pl.pallas_call(
        functools.partial(forward_kernel, Z, Y, FORWARD_PLAN),
        out_shape=outs,
        in_specs=[ANY, ANY] + [VMEM] * 15,
        out_specs=[ANY] * 14 + [VMEM] * 3,
        scratch_shapes=scratch,
        compiler_params=pltpu.CompilerParams(collective_id=0, has_side_effects=True, vmem_limit_bytes=VMEM_LIMIT),
        name="forward",
    )(x, cot, segment, valid, *shards, *vectors)


def pack(net, buf, left, right):
    width = left.shape[1]

    def owner(i):
        rows = aligned(i, 24)
        v = jnp.concatenate([left[rows, :], right[rows, :]], axis=0).astype(BF16)
        buf[net.place(i) + (ALL, slice(0, width))] = v

    loop(BLOCKS, owner)


def all_sum_steps(net, mine, theirs, sems):
    partners = ["c", "x", "y"] if net.Y == 2 else ["c", "x"]
    devices = [net.across(axis) for axis in partners]
    bit = 1
    while bit < net.Z:
        z = net.at["z"]
        devices.append(net.device(z=z + bit - 2 * bit * ((z // bit) % 2)))
        bit *= 2
    copies = [remote(mine.at[k], theirs.at[k], sems, k, device) for k, device in enumerate(devices)]

    def step(k):
        if k > 0:
            copies[k - 1].wait_recv()
            mine[k] = mine[k - 1] + theirs[k - 1]
        if k < len(copies):
            copies[k].start()

    return [lambda k=k: step(k) for k in range(len(copies) + 1)], copies


def rounds_of(Z, Y):
    assert 2 ** (Z - 1).bit_length() == Z
    return 2 + (Y == 2) + (Z - 1).bit_length()


def attend_back(qkv, do, mask_t, lse, d, small, seq, p, u):
    T = do.shape[0]
    rows = aligned(seq, LEN)
    lanes = aligned(p, 128)
    q, k, v = (qkv[pl.ds(pl.multiple_of(j * T + seq * LEN, LEN), LEN), lanes] for j in range(3))
    g = do[rows, lanes]
    kt = k.T
    dk = dv = None
    dqt = []
    for h in range(2):
        here = head_mask(h, k.shape)
        km, vm, qm, gm = (jnp.where(here, a, jnp.zeros_like(a)) for a in (k, v, q, g))
        t = dot(km, q, NT) * (0.125 * LOG2E) + mask_t[seq] - lse[seq * 2 * PAIRS + 2 * p + h, 0:1, :]
        pt = jnp.exp2(t)
        dp = dot(vm, g, NT)
        w = pt * dp
        ds = (w - pt * jnp.sum(w, axis=0, keepdims=True)).astype(BF16)
        dvh = dot(pt.astype(BF16), gm)
        dkh = dot(ds, qm)
        dv = dvh if dv is None else dv + dvh
        dk = dkh if dk is None else dk + dkh
        dqt.append(dot(kt[64 * h : 64 * h + 64, :], ds))
    dq = (jnp.concatenate(dqt, axis=0).T * 0.125).astype(BF16)
    dv = dv.astype(BF16)
    for j, grad in enumerate((dq, (dk * 0.125).astype(BF16), dv)):
        d[rows, pl.ds(pl.multiple_of(u * 384 + j * 128, 128), 128)] = grad
    small[0:1, lanes] += down_sum(dq.astype(F32))
    small[1:2, lanes] += down_sum(dv.astype(F32))


def pack_pair(net, buf, dw, small=None, exp=None):
    for i in range(BLOCKS):
        own = dw[24 * i : 24 * i + 24, :384]
        last = [jnp.zeros((24, 128), F32)]
        if small is not None:
            last = []
            for ref, at in ((small, 24 * i), (exp, 96 * i)):
                part = ref[:, at // 128 * 128 : at // 128 * 128 + 256]
                last.append((pltpu.roll(part, 256 - at % 128, axis=1) if at % 128 else part)[:, :128])
            last.append(jnp.zeros((8, 128), F32))
        buf[net.place(i)] = pair_block(own, jnp.concatenate(last, axis=0))


def backward_kernel(Z, Y, plan, *refs):
    (act_h, gp_h, df_h, dsec_h, normed_h, res_h, att_h, qkv_h, x_h, w1_h, w2_h, w_out_h, w_in_h) = refs[:13]
    vec, small_in, stats_in, segment, valid, lse = refs[13:19]
    dx_h, w2_own, w1_own, out_own, in_own, pair_own, stats = refs[19:26]
    parts = refs[26:35]
    (df, wide, normed, normed_t, att, res, w1, w2, w_out, act, gp, dh, dw, mask_t, small, exp, sum_mine, sum_theirs) = refs[35:53]
    ssem, rsem, sss, srs, loads, chunks, outs = refs[53:60]
    land = refs[60:]
    net = Net(Z, Y)
    T = df.shape[0]
    seqs, blocks = T // LEN, T // ROWS
    plan = list(plan)

    def load(src, dst, k):
        return pltpu.make_async_copy(src, dst, loads.at[k])

    def act_copy(j):
        return pltpu.make_async_copy(act_h.at[:, aligned(j, 384)], act.at[j % 2], chunks.at[j % 2])

    def gp_copy(t):
        return pltpu.make_async_copy(gp_h.at[:, pl.ds(t * 1024, 1024)], gp.at[t % 2], chunks.at[2 + t % 2])

    def res_copy(i):
        return pltpu.make_async_copy(res_h.at[aligned(i, ROWS), :], res.at[i % 2], chunks.at[4 + i % 2])

    load_df = load(df_h, df, 0)
    load_w2 = load(w2_h, w2, 1)
    load_normed = load(normed_h, normed, 2)
    load_w1 = load(w1_h, w1, 3)
    load_dsec = load(dsec_h, wide, 4)
    load_att, load_out = load(att_h, att, 6), load(w_out_h, w_out, 7)
    load_qkv, load_in, load_x = load(qkv_h, w2, 8), load(w_in_h, w1.at[:, pl.ds(0, 3 * D)], 9), load(x_h, att, 10)
    act_copy(0).start()
    load_df.start()
    act_copy(1).start()
    small[...] = jnp.zeros_like(small)
    small[:, :D] = small_in[...]
    exp[...] = jnp.zeros_like(exp)
    sum_mine[0] = stats_in[...]
    for s in range(seqs):
        seg = segment[s : s + 1, :].astype(F32)
        build_mask(mask_t.at[s], jnp.where(valid[s : s + 1, :] > 0, seg, -1.0), seg)
    net.barrier()
    load_df.wait()
    waiting = (load_w2, load_normed, gp_copy(0), load_dsec, load_w1, gp_copy(1), res_copy(0), load_att)

    def shrink_step(j):
        spread(j, 0, [copy.start for copy in waiting])
        act_copy(j).wait()
        v = dot(act[j % 2], df[...], TN).astype(BF16)
        for k in range(4):
            place = net.place(4 * j + k)
            for t in range(3):
                c = slice(256 * t, 256 * t + 256)
                parts[t][place + (ALL, slice(0, 256))] = v[96 * k : 96 * k + 48, c]
                parts[t][place + (ALL, slice(256, 512))] = v[96 * k + 48 : 96 * k + 96, c]
        pl.when(j + 2 < FF // 384)(lambda: act_copy(j + 2).start())

    loop(FF // 384, shrink_step)
    load_out.start()
    steps, moves = [], []
    for g in range(11):
        k = g if g < 7 else g - 7 if g < 9 else g - 2
        group, lines = parts[k], land[7 * k : 7 * k + 7]
        if g in (7, 8):
            group, *lines = (r.at[(ALL,) * (len(r.shape) - 1) + (pl.ds(0, 384),)] for r in (group, *lines))
        calls, sends = scatter_steps(net, group, lines, (ssem.at[g], rsem.at[g]), finish_of(g, w2_own, w1_own, out_own, in_own, pair_own))
        steps.append(calls)
        moves.append(sends)
    sum_calls, sum_copies = all_sum_steps(net, sum_mine, sum_theirs, (sss, srs))

    def move():
        todo = [steps[g][k] for g, k in plan.pop(0)]
        if sum_calls:
            todo.append(sum_calls.pop(0))
        return together(todo)

    def sent(g):
        for copies in moves[g]:
            copies.sent()

    move()()
    load_normed.wait()

    def turn(j):
        lanes = aligned(j, 128)
        normed_t[lanes, :] = normed[:, lanes].T

    loop(D // 128, turn)
    move()()
    load_w2.wait()
    load_w1.wait()
    load_dsec.wait()
    for t in range(3):
        gp_copy(t).wait()
        c = slice(t * 1024, (t + 1) * 1024)
        inner = [move(), move()]

        def expand_step(i, t=t, c=c):
            spread(i, 0, inner)
            r = aligned(i, 2 * ROWS)
            d = (dot(df[r, :], w2[c, :], NT) * gp[t % 2, r, :].astype(F32)).astype(BF16)
            dh[r, :] = d
            exp[0:1, c] += down_sum(d.astype(F32))
            wide[r, :] += dot(d, w1[:, c], NT)

        loop(blocks // 2, expand_step)
        if t == 0:
            gp_copy(2).start()
        move()()
        dw[...] = dot(normed_t[...], dh[...])
        pack(net, parts[3 + t], dw.at[:, :512], dw.at[:, 512:])
        move()()
    load_qkv.start()
    load_in.start()
    res_copy(1).start()
    load_att.wait()
    load_out.wait()
    inner = [move() for _ in range(blocks)]

    def norm_step(i):
        spread(i, 0, inner)
        r = aligned(i, ROWS)
        res_copy(i).wait()
        n, rsd = normalise(res[i % 2])
        pl.when(i + 2 < blocks)(lambda: res_copy(i + 2).start())
        g = wide[r, :]
        grad = norm_back(g, n, rsd, vec[3:4, :])
        wide[r, :] = grad
        low = grad.astype(BF16)
        df[r, :] = low
        add_small(small, "fg", down_sum(g * n))
        add_small(small, "fs", down_sum(g))
        add_small(small, "ob", down_sum(low.astype(F32)))
        normed[r, :] = dot(low, w_out[...], NT).astype(BF16)

    loop(blocks, norm_step)
    dw[:, :D] = dot(att[...], df[...], TN)
    load_x.start()
    pack(net, parts[6], dw.at[:, :384], dw.at[:, 384:D])
    move()()
    load_qkv.wait()
    d = (dh.at[:, pl.ds(0, D)], gp.at[0, :, pl.ds(0, D)], gp.at[1, :, pl.ds(0, D)])
    for t in range(2):
        inner = [move() for _ in range(2 * seqs)]

        def attend_step(i, t=t):
            spread(i, 0, inner)
            attend_back(w2, normed, mask_t, lse, d[t], small, i // 2, 2 * t + i % 2, i % 2)

        loop(2 * seqs, attend_step)
        if t == 0:
            load_x.wait()

            def turn_x(j):
                lanes = aligned(j, 128)
                normed_t[lanes, :] = att[:, lanes].T

            loop(D // 128, turn_x)
        dw[:, :D] = dot(normed_t[...], d[t][...])
        sent(t)
        pack(net, parts[t], dw.at[:, :384], dw.at[:, 384:D])
        move()()
    for u in range(2):
        inner = [move() for _ in range(seqs)]

        def attend_step(i, u=u):
            spread(i, 0, inner)
            attend_back(w2, normed, mask_t, lse, d[2], small, i, 4 + u, u)

        loop(seqs, attend_step)
        dw[:, :384] = dot(normed_t[...], d[2][:, u * 384 : (u + 1) * 384])
        pack_pair(net, parts[7 + u], dw, *((small, exp) if u == 1 else ()))
        move()()
    load_in.wait()
    inner = [move() for _ in range(blocks)]

    def token_step(i):
        spread(i, 0, inner)
        r = aligned(i, ROWS)
        wide[r, :] += sum(dot(d[t][r, :], w1[:, t * D : (t + 1) * D], NT) for t in range(3))

    loop(blocks, token_step)
    store = pltpu.make_async_copy(wide, dx_h, outs.at[0])
    store.start()
    stats[...] = sum_mine[len(sum_copies)]
    move()()
    assert not plan
    store.wait()
    for copy in sum_copies:
        copy.wait_send()
    for g in range(2, 11):
        sent(g)


def finish_of(g, w2_own, w1_own, out_own, in_own, pair_own):
    def finish(first, rows, total):
        if g < 3:
            w2_own[first : first + rows, g * 256 : (g + 1) * 256] = total[:, :256]
            w2_own[48 + first : 48 + first + rows, g * 256 : (g + 1) * 256] = total[:, 256:]
        else:
            own = w1_own.at[g - 3] if g < 6 else out_own if g == 6 else in_own.at[g - 7] if g < 9 else pair_own.at[g - 9]
            own[first : first + rows, : total.shape[1]] = total

    return finish


def backward(Z, Y, act, gp, df, dsec, normed, res, att, qkv, x, w1, w2, w_out, w_in, vec, small, stats, segment, valid, lse):
    T, S = df.shape[0], segment.shape[0]
    blocks = (2, 2, Y, Z, 48)
    rounds = rounds_of(Z, Y)
    outs = [
        SDS((T, D), F32), SDS((96, D), F32), SDS((3, 48, 512), F32), SDS((48, 384), F32), SDS((2, 48, 384), F32),
        SDS((2, 96, 128), F32), SDS((8, 128), F32),
    ]
    rows = pltpu.VMEM((T, D), BF16)
    scratch = [pltpu.VMEM(blocks + (512,), BF16)] * 6 + [
        pltpu.VMEM(blocks + (384,), BF16), pltpu.VMEM(blocks[:4] + (96, 128), BF16), pltpu.VMEM(blocks[:4] + (96, 128), BF16),
        rows, pltpu.VMEM((T, D), F32), rows, pltpu.VMEM((D, T), BF16), rows, pltpu.VMEM((2, ROWS, D), F32),
        pltpu.VMEM((D, FF), BF16), pltpu.VMEM((FF, D), BF16), pltpu.VMEM((D, D), BF16),
        pltpu.VMEM((2, T, 384), BF16), pltpu.VMEM((2, T, 1024), BF16), pltpu.VMEM((T, 1024), BF16),
        pltpu.VMEM((D, 1024), F32), pltpu.VMEM((S, LEN, LEN), F32), pltpu.VMEM((8, D + 128), F32), pltpu.VMEM((8, FF + 128), F32),
        pltpu.VMEM((rounds + 1, 8, 128), F32), pltpu.VMEM((rounds, 8, 128), F32),
        DMA((11, sem_count(Z))), DMA((11, sem_count(Z))), DMA((rounds,)), DMA((rounds,)), DMA((11,)), DMA((6,)), DMA((1,)),
    ] + lands(Z, Y, 48, 512) * 6 + lands(Z, Y, 48, 384) + lands(Z, Y, 96, 128) * 2
    return pl.pallas_call(
        functools.partial(backward_kernel, Z, Y, BACKWARD_PLAN),
        out_shape=outs,
        in_specs=[ANY] * 13 + [VMEM] * 6,
        out_specs=[ANY] + [VMEM] * 6,
        scratch_shapes=scratch,
        compiler_params=pltpu.CompilerParams(collective_id=1, has_side_effects=True, vmem_limit_bytes=VMEM_LIMIT),
        name="backward",
    )(act, gp, df, dsec, normed, res, att, qkv, x, w1, w2, w_out, w_in, vec, small, stats, segment, valid, lse)


def hand_out_kernel(dx_in, result_in, in_own, pair_own, out_own, w1_own, w2_own, stats, *refs):
    dx, result, w_in, w_out, w1, w2, mean, total, exp = refs[:9]
    vectors, (dx_here, result_here, load_sems, store_sems) = refs[9:17], refs[17:]
    T = dx.shape[0]
    loads, stores = [], []
    for src, here, dst, count in ((dx_in, dx_here, dx, 4), (result_in, result_here, result, 2)):
        for k in range(count):
            rows = pl.ds(k * (T // count), T // count)
            n = len(loads)
            loads.append(pltpu.make_async_copy(src.at[rows, :], here.at[rows, :], load_sems.at[n]))
            stores.append(pltpu.make_async_copy(here.at[rows, :], dst.at[rows, :], store_sems.at[n]))
    for copy in loads:
        copy.start()
    for p in range(PAIRS):
        for j in range(3):
            if p < 4:
                v = in_own[p // 2, 24 * (p % 2) : 24 * (p % 2) + 24, 128 * j : 128 * (j + 1)]
            else:
                v = pair_own[p - 4, 24 * j : 24 * j + 24, :]
            w_in[:, j * D + p * 128 : j * D + (p + 1) * 128] = v
    for t in range(3):
        w1[:, t * 1024 : t * 1024 + 512] = w1_own[t, :24, :]
        w1[:, t * 1024 + 512 : (t + 1) * 1024] = w1_own[t, 24:, :]
    w_out[:, :384] = out_own[:24, :]
    w_out[:, 384:] = out_own[24:, :]
    w2[...] = w2_own[...]
    for k in range(8):
        vectors[k][...] = pair_own[1, 72 + k : 73 + k, :24]
    exp[...] = pair_own[1, 80:81, :96]
    lane = lax.broadcasted_iota(jnp.int32, (1, 128), 1)
    sums = jnp.sum(stats[...], axis=1, keepdims=True)
    packed = jnp.zeros((1, 128), F32)
    for k in range(5):
        packed = jnp.where(lane == k, sums[k : k + 1, :], packed)
    total[...] = packed
    mean[...] = (packed / (D * sums[4:5, :]))[:, :4]
    for load, store in zip(loads, stores):
        load.wait()
        store.start()
    for copy in stores:
        copy.wait()


def hand_out(dx, result, in_own, pair_own, out_own, w1_own, w2_own, stats):
    outs = [
        SDS(dx.shape, F32), SDS(result.shape, BF16),
        SDS((24, 3 * D), F32), SDS((24, D), F32), SDS((24, FF), F32), SDS((96, D), F32),
        SDS((1, 4), F32), SDS((1, 128), F32), SDS((1, 96), F32),
    ] + [SDS((1, 24), F32)] * 8
    return pl.pallas_call(
        hand_out_kernel,
        out_shape=outs,
        in_specs=[ANY] * 2 + [VMEM] * 6,
        out_specs=[ANY] * 2 + [VMEM] * (len(outs) - 2),
        scratch_shapes=[pltpu.VMEM(dx.shape, F32), pltpu.VMEM(result.shape, BF16), DMA((6,)), DMA((6,))],
        compiler_params=pltpu.CompilerParams(vmem_limit_bytes=VMEM_LIMIT),
        name="hand_out",
    )(dx, result, in_own, pair_own, out_own, w1_own, w2_own, stats)


def per_device(
    Z, Y, fsdp, tokens, segment_ids, valid, input_weight, query_bias, value_bias, output_weight, output_bias,
    first_gain, first_shift, expand_weight, expand_bias, shrink_weight, shrink_bias, second_gain, second_shift, cotangent,
):
    shards = (input_weight, output_weight, expand_weight, shrink_weight)
    vectors = (query_bias, value_bias, output_bias, first_gain, first_shift, expand_bias, shrink_bias, second_gain, second_shift)
    split = Y == 1 and fsdp > 1
    if split:
        def whole(v):
            return lax.all_gather(v, "fsdp", axis=0, tiled=True)

        shards, vectors = tuple(map(whole, shards)), tuple(map(whole, vectors))
    vectors = [v.reshape(1, -1) for v in vectors]
    (res, qkv, att, normed, act, gp, df, lse, w_in, w_out, w1, w2, result, dsec, vec, small, stats) = forward(
        Z, Y, tokens, cotangent, segment_ids, valid, shards, vectors
    )
    dx, w2_own, w1_own, out_own, in_own, pair_own, stats = backward(
        Z, Y, act, gp, df, dsec, normed, res, att, qkv, tokens, w1, w2, w_out, w_in, vec, small, stats, segment_ids, valid, lse
    )
    (dx, result, *weights, mean, total, exp_own, qb, vb, ob, fg, fs, sb, sg, ss) = hand_out(
        dx, result, in_own, pair_own, out_own, w1_own, w2_own, stats
    )
    own = [v.reshape(-1) for v in (qb, vb, ob, fg, fs, sb, sg, ss, exp_own)]
    mean = mean.reshape(-1)
    if split:
        def share(v):
            return lax.psum_scatter(v, "fsdp", scatter_dimension=0, tiled=True)

        weights, own = [share(v) for v in weights], [share(v) for v in own]
        totals = lax.psum(total[0, :5], "fsdp")
        mean = totals[:4] / (D * totals[4])
    qb, vb, ob, fg, fs, sb, sg, ss, exp_own = own
    return (
        result, dx, mean, weights[0], qb, vb, weights[1], ob, fg, fs,
        weights[2], exp_own, weights[3], sb, sg, ss,
    )


def solution(mesh):
    dp, fsdp = mesh.shape["dp"], mesh.shape["fsdp"]
    Z, Y = dp // 4, (2 if dp * fsdp == BLOCKS else 1)
    matrix, vector = P(("dp", "fsdp"), None), P(("dp", "fsdp"))
    params = (matrix, vector, vector, matrix, vector, vector, vector, matrix, vector, matrix, vector, vector, vector)
    return jax.shard_map(
        functools.partial(per_device, Z, Y, fsdp),
        mesh=mesh,
        in_specs=(matrix, matrix, matrix) + params + (matrix,),
        out_specs=(matrix, matrix, P()) + params,
        check_vma=False,
    )
```

```python
import functools

import jax
import jax.numpy as jnp
from jax import lax
from jax.experimental import pallas as pl
from jax.experimental.pallas import tpu as pltpu
from jax.sharding import PartitionSpec as P

BLOCKS = 32
F32, BF16 = jnp.float32, jnp.bfloat16
LOG2E = 1.4426950408889634
MESH = pl.DeviceIdType.MESH
ALL = slice(None)
ANY = pl.BlockSpec(memory_space=pl.ANY)
VMEM = pl.BlockSpec(memory_space=pltpu.VMEM)
SDS = jax.ShapeDtypeStruct
DMA = pltpu.SemaphoreType.DMA
NT = (((1,), (1,)), ((), ()))
TN = (((0,), (0,)), ((), ()))
NN = (((1,), (0,)), ((), ()))
D, FF, LEN, PAIRS = 768, 3072, 512, 6
ROWS = 256


def dot(a, b, dims=NN):
    return lax.dot_general(a, b, dims, preferred_element_type=F32)


def aligned(at, step, size=None):
    return pl.ds(pl.multiple_of(at * step, step), step if size is None else size)


def loop(count, body):
    def step(i, carry):
        body(i)
        return carry

    lax.fori_loop(0, count, step, 0)


VMEM_LIMIT = 63 * 2**20


class Net:
    def __init__(self, Z, Y):
        self.Z, self.Y = Z, Y
        dp, y = lax.axis_index("dp"), lax.axis_index("fsdp")
        self.fsdp = y
        self.at = {"z": dp // 4, "x": (dp // 2) % 2, "c": dp % 2, "y": y if Y == 2 else 0}
        self.own = dp * Y + (y if Y == 2 else 0)

    def device(self, **moved):
        p = dict(self.at, **moved)
        return (p["z"] * 4 + p["x"] * 2 + p["c"], p["y"] if self.Y == 2 else self.fsdp)

    def across(self, axis):
        return self.device(**{axis: 1 - self.at[axis]})

    def z_away(self, k):
        return (self.at["z"] + k) % self.Z

    def others(self):
        axes = ["c", "x", "y"] if self.Y == 2 else ["c", "x"]
        return [self.across(axis) for axis in axes] + [self.device(z=self.z_away(k)) for k in range(1, self.Z)]

    def greet(self):
        for other in self.others():
            pl.semaphore_signal(pltpu.get_barrier_semaphore(), inc=1, device_id=other, device_id_type=MESH)

    def meet(self):
        pl.semaphore_wait(pltpu.get_barrier_semaphore(), len(self.others()))

    def place(self, i):
        Y = self.Y
        return ((i // Y) % 2, (i // (2 * Y)) % 2, i % Y, i // (4 * Y))

    def mine(self):
        at = self.at
        return (at["c"], at["x"], at["y"], at["z"])


STEPS = 5


def halves(buf):
    low = buf.shape[4] // 3
    return pl.ds(0, 2 * low), pl.ds(2 * low, low)


def sem_count(Z):
    return 2 * (Z - 1) + 5


def sem_ids(Z):
    n = Z - 1
    return {"tz": 0, "lz": n, "tx": 2 * n, "ty": 2 * n + 1, "lx": 2 * n + 2, "ly": 2 * n + 3, "c": 2 * n + 4}


def remote(src, dst, sems, sem, device):
    return pltpu.make_async_remote_copy(
        src_ref=src,
        dst_ref=dst,
        send_sem=sems[0].at[sem],
        recv_sem=sems[1].at[sem],
        device_id=device,
        device_id_type=MESH,
    )


class Move:
    def __init__(self, pairs):
        self.pairs = pairs

    def start(self):
        for send, _ in self.pairs:
            send().start()

    def receive(self):
        for _, take in self.pairs:
            take().wait_recv()

    def sent(self):
        for send, _ in self.pairs:
            send().wait_send()


def gather_moves(net, buf, sems):
    Z, Y, at, ids = net.Z, net.Y, net.at, sem_ids(net.Z)
    c, x, y, z = at["c"], at["x"], at["y"], at["z"]
    TOP, LOW = halves(buf)

    def swap(axis, ours, theirs, sem):
        device = net.across(axis)
        return [(lambda: remote(ours(), ours(), sems, sem, device), lambda: remote(theirs(), theirs(), sems, sem, device))]

    def along_z(part, sem):
        def pair(k):
            return (
                lambda: remote(part(z), part(z), sems, sem + k - 1, net.device(z=net.z_away(k))),
                lambda: remote(part(net.z_away(Z - k)), part(net.z_away(Z - k)), sems, sem + k - 1, net.device(z=net.z_away(k))),
            )

        return [pair(k) for k in range(1, Z)]

    yy = y if Y == 1 else ALL
    moves = [
        along_z(lambda zz: buf.at[c, x, y, zz, TOP], ids["tz"]),
        swap("x", lambda: buf.at[c, x, y, :, TOP], lambda: buf.at[c, 1 - x, y, :, TOP], ids["tx"])
        + along_z(lambda zz: buf.at[c, x, yy, zz, LOW], ids["lz"]),
        swap("x", lambda: buf.at[c, x, yy, :, LOW], lambda: buf.at[c, 1 - x, yy, :, LOW], ids["lx"]),
        swap("c", lambda: buf.at[c], lambda: buf.at[1 - c], ids["c"]),
    ]
    if Y == 2:
        moves[0] += swap("y", lambda: buf.at[c, x, y, z, LOW], lambda: buf.at[c, x, 1 - y, z, LOW], ids["ly"])
        moves[2] += swap("y", lambda: buf.at[c, :, y, :, TOP], lambda: buf.at[c, :, 1 - y, :, TOP], ids["ty"])
    return [Move(pairs) for pairs in moves]


def gather_steps(net, buf, sems):
    moves = gather_moves(net, buf, sems)

    def step(k):
        if k > 0:
            moves[k - 1].receive()
        if k < len(moves):
            moves[k].start()

    return [lambda k=k: step(k) for k in range(STEPS)], moves


def lands(Z, Y, rows, width):
    low = rows // 3
    top = 2 * low
    shapes = [(2, Y, Z, rows), (2, Z, top), (Y, Z, low), (Z, top), (Z - 1, Y, low), (Z - 1, top), (low,)]
    return [pltpu.VMEM(shape + (width,), BF16) for shape in shapes]


def add_blocks(count, at, dst, src):
    def one(i):
        idx = at(i)
        dst[idx] = dst[idx] + src[idx]

    loop(count, one)


def scatter_steps(net, buf, land, sems, finish):
    Z, Y, at, ids = net.Z, net.Y, net.at, sem_ids(net.Z)
    c, x, y, z = at["c"], at["x"], at["y"], at["z"]
    core, top_y, low_x, top_x, low_z, top_z, low_y = land
    TOP, LOW = halves(buf)
    low = buf.shape[4] // 3

    def swap(axis, what, where, sem):
        device = net.across(axis)

        def make():
            return remote(what(), where, sems, sem, device)

        return [(make, make)]

    def along_z(part, where, sem):
        def make(k):
            return lambda: remote(part(net.z_away(k)), where.at[k - 1], sems, sem + k - 1, net.device(z=net.z_away(k)))

        return [(make(k), make(k)) for k in range(1, Z)]

    yy = y if Y == 1 else ALL
    low_x_land, low_z_land = (low_x.at[0], low_z.at[:, 0]) if Y == 1 else (low_x, low_z)
    moves = [
        swap("c", lambda: buf.at[1 - c], core, ids["c"]),
        swap("x", lambda: buf.at[c, 1 - x, yy, :, LOW], low_x_land, ids["lx"]),
        swap("x", lambda: buf.at[c, 1 - x, y, :, TOP], top_x, ids["tx"])
        + along_z(lambda zz: buf.at[c, x, yy, zz, LOW], low_z_land, ids["lz"]),
        along_z(lambda zz: buf.at[c, x, y, zz, TOP], top_z, ids["tz"]),
    ]
    if Y == 2:
        moves[1] += swap("y", lambda: buf.at[c, :, 1 - y, :, TOP], top_y, ids["ty"])
        moves[3] += swap("y", lambda: buf.at[c, x, 1 - y, z, LOW], low_y, ids["ly"])
    moves = [Move(pairs) for pairs in moves]

    def sum_z(mine, where):
        total = mine.astype(F32)
        for k in range(Z - 1):
            total = total + where(k).astype(F32)
        return total

    def step(k):
        if k > 0:
            moves[k - 1].receive()
        if k == 1:
            add_blocks(2 * Y * Z, lambda i: (i // (Y * Z), (i // Z) % Y, i % Z), buf.at[c], core)
        if k == 2:
            if Y == 2:
                add_blocks(2 * Z, lambda i: (i // Z, i % Z), buf.at[c, :, y, :, TOP], top_y)
            add_blocks(Y * Z, lambda i: (i // Z, i % Z), buf.at[c, x, :, :, LOW], low_x)
        if k == 3:
            add_blocks(Z, lambda i: (i,), buf.at[c, x, y, :, TOP], top_x)
            for j in range(Y):
                own = buf.at[c, x, j, z, LOW]
                own[...] = sum_z(own[...], lambda i: low_z[i, j]).astype(BF16)
        if k < 4:
            moves[k].start()
        else:
            finish(0, 2 * low, sum_z(buf[c, x, y, z, TOP], lambda i: top_z[i]))
            rest = buf[c, x, y, z, LOW].astype(F32)
            finish(2 * low, low, rest + low_y[...].astype(F32) if Y == 2 else rest)

    return [lambda k=k: step(k) for k in range(STEPS)], moves


def together(todo):
    def call():
        for one in todo:
            one()

    return call


def train(steps, offsets):
    calls = []
    for t in range(len(steps) + offsets[-1]):
        todo = [steps[g][k] for g in range(len(steps)) for k in range(STEPS) if g + offsets[k] == t]
        calls.append(together(todo))
    return calls


def spread(i, first, calls, every=1):
    for k, call in enumerate(calls):
        pl.when(i == first + k * every)(call)


FORWARD_PLAN = (
    ((0, 0), (1, 0), (2, 0), (0, 1), (1, 1), (3, 0), (0, 2), (2, 1), (1, 2), (4, 0), (3, 1), (5, 0), (0, 3), (2, 2),),
    ((0, 4),),
    (),
    ((1, 3),),
    ((4, 1), (3, 2),),
    ((6, 0),),
    ((1, 4),),
    ((2, 3), (5, 1),),
    ((7, 0),),
    ((4, 2),),
    (),
    ((3, 3), (2, 4),),
    ((6, 1),),
    ((8, 0),),
    ((3, 4), (5, 2),),
    (),
    ((4, 3),),
    (),
    ((7, 1),),
    ((4, 4), (6, 2),),
    (),
    (),
    ((9, 0), (8, 1), (10, 0),),
    ((5, 3),),
    ((7, 2),),
    (),
    (),
    ((9, 1),),
    ((6, 3),),
    ((8, 2),),
    ((5, 4),),
    (),
    ((7, 3),),
    ((6, 4),),
    (),
    ((10, 1), (9, 2),),
    (),
    (),
    ((8, 3),),
    (),
    ((7, 4), (10, 2),),
    (),
    ((8, 4),),
    (),
    (),
    ((9, 3),),
    (),
    (),
    ((10, 3), (9, 4),),
    (),
    (),
    ((10, 4),),
)

BACKWARD_PLAN = (
    (),
    (),
    ((0, 0),),
    (),
    ((0, 1),),
    (),
    ((3, 0),),
    (),
    ((3, 1), (2, 0),),
    (),
    ((1, 0), (0, 2),),
    ((4, 0),),
    ((1, 1),),
    ((5, 0),),
    ((4, 1),),
    (),
    (),
    ((3, 2), (0, 3),),
    (),
    (),
    ((5, 1),),
    ((3, 3), (4, 2), (0, 4), (2, 1),),
    ((1, 2), (6, 0),),
    ((6, 1),),
    ((7, 0),),
    ((1, 3), (2, 2),),
    ((5, 2),),
    ((7, 1), (1, 4), (6, 2),),
    ((8, 0), (2, 3), (5, 3),),
    ((4, 3),),
    ((8, 1),),
    ((9, 0),),
    ((6, 3), (7, 2),),
    ((9, 1),),
    ((10, 0), (5, 4), (3, 4),),
    ((9, 2), (7, 3),),
    ((4, 4), (10, 1), (8, 2), (2, 4),),
    ((9, 3),),
    (),
    ((10, 2), (8, 3), (9, 4), (10, 3), (8, 4), (7, 4), (6, 4), (10, 4),),
)


def head_mask(head, shape):
    lane = lax.broadcasted_iota(jnp.int32, shape, len(shape) - 1)
    return (lane < 64) if head == 0 else (lane >= 64)


def column(row, count=128):
    return jnp.broadcast_to(row, (count, row.shape[1])).T


def build_mask(mask, down, across):
    n = mask.shape[0]
    down = column(down)
    at = lax.broadcasted_iota(jnp.int32, (n, 128), 0)
    lane = lax.broadcasted_iota(jnp.int32, (n, 128), 1)
    for j in range(n // 128):
        tile = slice(j * 128, (j + 1) * 128)
        mask[:, tile] = jnp.where((down == across[:, tile]) | (at == lane + j * 128), 0.0, -1e30).astype(mask.dtype)


def gelu_pair(h):
    cdf = 0.5 + 0.5 * lax.erf(h * 0.7071067811865476)
    return h * cdf, cdf + h * jnp.exp2(h * h * (-0.5 * LOG2E)) * 0.3989422804014327


def normalise(v):
    centred = v - jnp.sum(v, axis=1, keepdims=True) * (1.0 / D)
    r = lax.rsqrt(jnp.sum(centred * centred, axis=1, keepdims=True) * (1.0 / D) + 1e-12)
    return centred * r, r


def norm_back(g, n, r, gain):
    scaled = g * gain
    mean = jnp.sum(scaled, axis=1, keepdims=True) * (1.0 / D)
    along = jnp.sum(scaled * n, axis=1, keepdims=True) * (1.0 / D)
    return r * (scaled - mean - n * along)


def down_sum(v):
    return jnp.sum(v, axis=0, keepdims=True)


def square_sum(value, counted):
    v = value.astype(BF16).astype(F32)
    v = v * v
    total = v[:, :128]
    for j in range(1, D // 128):
        total = total + v[:, j * 128 : (j + 1) * 128]
    return down_sum(total * counted)


def fold(rows, half):
    return jnp.concatenate([rows[:, :half], rows[:, half:]], axis=0).astype(BF16)


def unfold(net, buf, half, dst, at=0):
    def pair(p):
        a = buf[net.place(2 * p) + (ALL, slice(0, half))].astype(F32)
        b = buf[net.place(2 * p + 1) + (ALL, slice(0, half))].astype(F32)
        rows = aligned(p, 48)
        dst[rows, at : at + half] = jnp.concatenate([a[:24], b[:24]], axis=0).astype(BF16)
        dst[rows, at + half : at + 2 * half] = jnp.concatenate([a[24:], b[24:]], axis=0).astype(BF16)

    loop(BLOCKS // 2, pair)


SMALL = ("qb", "vb", "ob", "fg", "fs", "sb", "sg", "ss")


def add_small(small, name, value):
    k = SMALL.index(name)
    small[k : k + 1, :D] += value


def pair_block(rows, last):
    return jnp.concatenate([rows[:, :128], rows[:, 128:256], rows[:, 256:], last], axis=0).astype(BF16)


def unfold_pair(net, buf, dst, at):
    def pair(p):
        a = buf[net.place(2 * p)].astype(F32)
        b = buf[net.place(2 * p + 1)].astype(F32)
        rows = aligned(p, 48)
        for j in range(3):
            part = slice(24 * j, 24 * j + 24)
            dst[rows, at + 128 * j : at + 128 * (j + 1)] = jnp.concatenate([a[part], b[part]], axis=0).astype(BF16)

    loop(BLOCKS // 2, pair)


def small_rows(vectors, expand, tmp):
    tmp[...] = jnp.zeros_like(tmp)
    for k, ref in enumerate(vectors):
        tmp[k : k + 1, :24] = ref[...].astype(F32)
    tmp[8:9, :96] = expand[...].astype(F32)
    return tmp[...]


def small_params(net, buf, vec, exp):
    vec[...] = jnp.zeros_like(vec)
    exp[...] = jnp.zeros_like(exp)
    for i in range(BLOCKS):
        w = buf[net.place(i) + (slice(64, 96), ALL)].astype(F32)
        for ref, first, at in ((vec, 8, 24 * i), (exp, 16, 96 * i)):
            part = jnp.concatenate([w[first : first + 8], jnp.zeros((8, 128), F32)], axis=1)
            if at % 128:
                part = pltpu.roll(part, at % 128, axis=1)
            tile = at // 128
            wide = min(256, ref.shape[1] - tile * 128)
            ref[:, tile * 128 : tile * 128 + wide] += part[:, :wide]


def pair_of(rows, p):
    return jnp.concatenate([rows[:, j * D + p * 128 : j * D + (p + 1) * 128] for j in range(3)], axis=1)


def attend(qkv, mask, att, lse, seq, p):
    T = att.shape[0]
    base = pl.multiple_of(seq * LEN, LEN)
    lanes = aligned(p, 128)
    q, k, v = (qkv[pl.ds(pl.multiple_of(j * T + seq * LEN, LEN), LEN), lanes] for j in range(3))
    lane = lax.broadcasted_iota(jnp.int32, (LEN, 128), 1)
    zero = jnp.zeros_like(k)
    here = [head_mask(h, k.shape) for h in range(2)]
    scores = [dot(q, jnp.where(m, k, zero), NT) for m in here]
    weights, totals, logs = [], [], lse[pl.ds(base, LEN), :]
    for h in range(2):
        t = scores[h] * (0.125 * LOG2E) + mask[seq]
        top = jnp.max(t, axis=1, keepdims=True)
        e = jnp.exp2(t - top)
        total = jnp.sum(e, axis=1, keepdims=True)
        weights.append(e.astype(BF16))
        totals.append(total)
        logs = jnp.where(lane == 2 * p + h, top + jnp.log2(total), logs)
    out = sum(dot(weights[h], jnp.where(here[h], v, zero)) * (1.0 / totals[h]) for h in range(2))
    lse[pl.ds(base, LEN), :] = logs
    att[pl.ds(base, LEN), lanes] = out.astype(BF16)


def forward_kernel(Z, Y, plan, *refs):
    (x_h, cot_h, segment, valid, w_in_s, w_out_s, w1_s, w2_s, qb, vb, ob, fg, fs, eb, sb, sg, ss) = refs[:17]
    (res_h, qkv_h, att_h, normed_h, act_h, gp_h, df_h, lse_h, w_in_h, w_out_h, w1_h, w2_h, result_h, dsec_h) = refs[17:31]
    vec, small, stats = refs[31:34]
    bufs = refs[34:45]
    (w_in, w_out, w1, w2, x, qkv, mask, att, lse, lse_rows, wide, normed, act, gp, cot, exp, tmp) = refs[45:62]
    ssem, rsem, loads, outs, gsem = refs[62:]
    net = Net(Z, Y)
    T = x.shape[0]
    seqs = T // LEN
    blocks = T // ROWS

    net.greet()
    load_x = pltpu.make_async_copy(x_h, x, loads.at[0])
    load_x.start()
    load_cot = pltpu.make_async_copy(cot_h, cot, loads.at[1])
    load_cot.start()
    mine = net.mine()
    own_in = w_in_s[...].astype(F32)
    own_1 = w1_s[...].astype(F32)
    bufs[0][mine] = pair_block(pair_of(own_in, 0), small_rows((qb, vb, ob, fg, fs, sb, sg, ss), eb, tmp))
    bufs[1][mine] = pair_block(pair_of(own_in, 1), jnp.zeros((24, 128), F32))
    for t in (1, 2):
        bufs[1 + t][mine] = jnp.concatenate([pair_of(own_in, 2 * t), pair_of(own_in, 2 * t + 1)], axis=0).astype(BF16)
    bufs[4][mine] = fold(w_out_s[...].astype(F32), 384)
    for t in range(3):
        bufs[5 + t][mine] = fold(own_1[:, t * 1024 : (t + 1) * 1024], 512)
        bufs[8 + t][mine + (ALL, slice(0, 256))] = w2_s[0:48, t * 256 : (t + 1) * 256]
        bufs[8 + t][mine + (ALL, slice(256, 512))] = w2_s[48:96, t * 256 : (t + 1) * 256]
    net.meet()
    steps, moves = [], []
    for g, buf in enumerate(bufs):
        calls, sends = gather_steps(net, buf, (ssem.at[g], rsem.at[g]))
        steps.append(calls)
        moves += sends
    plan = list(plan)

    def move():
        return together([steps[g][k] for g, k in plan.pop(0)])

    move()()
    small[...] = jnp.zeros_like(small)
    stats[...] = jnp.zeros_like(stats)
    for s in range(seqs):
        seg = segment[s : s + 1, :].astype(F32)
        live = valid[s : s + 1, :].astype(F32)
        build_mask(mask.at[s], seg, jnp.where(live > 0, seg, -1.0))
        stats[4:5, :] += sum(live[:, j * 128 : (j + 1) * 128] for j in range(LEN // 128))
    lse[...] = jnp.zeros_like(lse)
    move()()
    small_params(net, bufs[0], vec, exp)
    load_x.wait()
    stores = []

    def store(src, dst):
        copy = pltpu.make_async_copy(src, dst, outs.at[len(stores)])
        copy.start()
        stores.append(copy)
        return copy

    for g, pairs in enumerate(((0,), (1,), (2, 3), (4, 5))):
        if g > 0:
            move()()
        first, count = pairs[0], len(pairs)
        if count == 1:
            unfold_pair(net, bufs[g], w_in, first * 384)
        else:
            unfold(net, bufs[g], 384, w_in, first * 384)
        inner = [move(), move()]

        def project(i):
            spread(i, 0, inner)
            r = aligned(i, 2 * ROWS)
            c = dot(x[r, :], w_in[:, first * 384 : (first + count) * 384])
            for u, p in enumerate(pairs):
                for j in range(3):
                    part = c[:, u * 384 + j * 128 : u * 384 + (j + 1) * 128]
                    if j != 1:
                        part = part + vec[j // 2 : j // 2 + 1, p * 128 : (p + 1) * 128]
                    rows = pl.ds(pl.multiple_of(j * T + i * 2 * ROWS, 2 * ROWS), 2 * ROWS)
                    qkv[rows, p * 128 : (p + 1) * 128] = part.astype(BF16)

        loop(blocks // 2, project)
        inner = [move() for _ in range(seqs * count)]

        def attend_step(i):
            spread(i, 0, inner)
            attend(qkv, mask, att, lse, i // count, first + i % count)

        loop(seqs * count, attend_step)
    store(qkv, qkv_h)
    store(w_in, w_in_h)
    store_att = store(att, att_h)
    for s in range(seqs):
        rows = lse[s * LEN : (s + 1) * LEN, :].T
        for h in range(2 * PAIRS):
            lse_rows[s * 2 * PAIRS + h] = jnp.broadcast_to(rows[h : h + 1, :], (8, LEN))
    store(lse_rows, lse_h)
    move()()
    unfold(net, bufs[4], 384, w_out)
    store(w_out, w_out_h)

    def out_step(i):
        spread(i, 0, inner)
        r = aligned(i, ROWS)
        branch = dot(att[r, :], w_out[...]) + vec[2:3, :]
        residual = x[r, :].astype(F32) + branch
        wide[r, :] = residual
        n, _ = normalise(residual)
        normed[r, :] = (n * vec[3:4, :] + vec[4:5, :]).astype(BF16)
        live = live_rows(i)
        stats[0:1, :] += square_sum(residual, live)
        stats[1:2, :] += square_sum(branch, live)

    def live_rows(i):
        return live_col[aligned(i, ROWS), :]

    live_col = lse
    for s in range(seqs):
        live_col[s * LEN : (s + 1) * LEN, :] = column(valid[s : s + 1, :].astype(F32))
    inner = [move() for _ in range(blocks)]
    loop(blocks, out_step)
    store_wide = store(wide, res_h)
    store(normed, normed_h)

    def gp_copy(t, i):
        slot = (t * blocks + i) % 2
        return pltpu.make_async_copy(
            gp.at[slot], gp_h.at[aligned(i, ROWS), pl.ds(t * 1024, 1024)], gsem.at[slot]
        )

    for t in range(3):
        move()()
        unfold(net, bufs[5 + t], 512, w1, t * 1024)
        inner = [move() for _ in range(blocks)]

        def expand_step(i):
            spread(i, 0, inner)
            r = aligned(i, ROWS)
            nv = normed[r, :]
            slot = (t * blocks + i) % 2
            if t == 0:
                pl.when(i >= 2)(lambda: gp_copy(t, i).wait())
            else:
                gp_copy(t, i).wait()
            for j in range(2):
                c = slice(t * 1024 + j * 512, t * 1024 + (j + 1) * 512)
                a, g = gelu_pair(dot(nv, w1[:, c]) + exp[0:1, c])
                act[r, c] = a.astype(BF16)
                gp[slot, :, j * 512 : (j + 1) * 512] = g.astype(BF16)
            gp_copy(t, i).start()

        loop(blocks, expand_step)
    store(w1, w1_h)
    store(act, act_h)
    store_wide.wait()
    for t in range(3):
        move()()

        def unfold_last(i, t=t):
            blk = bufs[8 + t].at[net.place(i)]
            c = slice(t * 256, (t + 1) * 256)
            w2[aligned(i, 96, 48), c] = blk[:, :256]
            w2[pl.ds(pl.multiple_of(i * 96 + 48, 48), 48), c] = blk[:, 256:]

        loop(BLOCKS, unfold_last)
        if t < 2:
            inner = [move(), move()]

            def shrink_step(i, t=t):
                spread(i, 0, inner)
                r = aligned(i, 2 * ROWS)
                wide[r, t * 256 : (t + 1) * 256] = dot(act[r, :], w2[:, t * 256 : (t + 1) * 256])

            loop(blocks // 2, shrink_step)
    assert not plan
    store(w2, w2_h)
    store_att.wait()
    load_cot.wait()

    def end_copies(r):
        pairs = ((wide, dsec_h), (att, result_h), (x, df_h))
        return [pltpu.make_async_copy(src.at[r, :], dst.at[r, :], loads.at[k]) for k, (src, dst) in enumerate(pairs)]

    def last_step(i):
        r = aligned(i, ROWS)
        feedfwd = jnp.concatenate([wide[r, :512], dot(act[r, :], w2[:, 512:])], axis=1) + vec[5:6, :]
        second = normed[r, :].astype(F32) + feedfwd
        n, rs = normalise(second)
        gain = vec[6:7, :]
        att[r, :] = (n * gain + vec[7:8, :]).astype(BF16)
        g = cot[r, :].astype(F32)
        grad = norm_back(g, n, rs, gain)
        wide[r, :] = grad
        low = grad.astype(BF16)
        x[r, :] = low
        for copy in end_copies(r):
            copy.start()
        add_small(small, "sg", down_sum(g * n))
        add_small(small, "ss", down_sum(g))
        add_small(small, "sb", down_sum(low.astype(F32)))
        live = live_rows(i)
        stats[2:3, :] += square_sum(second, live)
        stats[3:4, :] += square_sum(feedfwd, live)

    loop(blocks, last_step)
    for k in (0, 1):
        gp_copy(2, blocks - 2 + k).wait()
    for copy in stores:
        if copy is not store_wide and copy is not store_att:
            copy.wait()
    for copy in end_copies(ALL):
        copy.wait()
    for move in moves:
        move.sent()


def forward(Z, Y, x, cot, segment, valid, shards, vectors):
    T, S = x.shape[0], segment.shape[0]
    blocks = (2, 2, Y, Z)
    shapes = ((96, 128),) * 2 + ((48, 384),) * 3 + ((48, 512),) * 6
    outs = [
        SDS((T, D), F32), SDS((3 * T, D), BF16), SDS((T, D), BF16), SDS((T, D), BF16),
        SDS((T, FF), BF16), SDS((T, FF), BF16), SDS((T, D), BF16), SDS((S * 12, 8, LEN), F32),
        SDS((D, 3 * D), BF16), SDS((D, D), BF16), SDS((D, FF), BF16), SDS((FF, D), BF16),
        SDS((T, D), BF16), SDS((T, D), F32), SDS((8, D), F32), SDS((8, D), F32), SDS((8, 128), F32),
    ]
    scratch = [pltpu.VMEM(blocks + shape, BF16) for shape in shapes] + [
        pltpu.VMEM((D, 3 * D), BF16), pltpu.VMEM((D, D), BF16), pltpu.VMEM((D, FF), BF16), pltpu.VMEM((FF, D), BF16),
        pltpu.VMEM((T, D), BF16), pltpu.VMEM((3 * T, D), BF16), pltpu.VMEM((S, LEN, LEN), F32),
        pltpu.VMEM((T, D), BF16), pltpu.VMEM((T, 128), F32), pltpu.VMEM((S * 12, 8, LEN), F32),
        pltpu.VMEM((T, D), F32), pltpu.VMEM((T, D), BF16), pltpu.VMEM((T, FF), BF16), pltpu.VMEM((2, ROWS, 1024), BF16),
        pltpu.VMEM((T, D), BF16), pltpu.VMEM((8, FF), F32), pltpu.VMEM((24, 128), F32),
        DMA((len(shapes), sem_count(Z))), DMA((len(shapes), sem_count(Z))), DMA((3,)), DMA((16,)), DMA((2,)),
    ]
    return pl.pallas_call(
        functools.partial(forward_kernel, Z, Y, FORWARD_PLAN),
        out_shape=outs,
        in_specs=[ANY, ANY] + [VMEM] * 15,
        out_specs=[ANY] * 14 + [VMEM] * 3,
        scratch_shapes=scratch,
        compiler_params=pltpu.CompilerParams(collective_id=0, has_side_effects=True, vmem_limit_bytes=VMEM_LIMIT),
        name="forward",
    )(x, cot, segment, valid, *shards, *vectors)


def pack(net, buf, left, right):
    width = left.shape[1]

    def owner(i):
        rows = aligned(i, 24)
        v = jnp.concatenate([left[rows, :], right[rows, :]], axis=0).astype(BF16)
        buf[net.place(i) + (ALL, slice(0, width))] = v

    loop(BLOCKS, owner)


def all_sum_steps(net, mine, theirs, sems):
    partners = ["c", "x", "y"] if net.Y == 2 else ["c", "x"]
    devices = [net.across(axis) for axis in partners]
    bit = 1
    while bit < net.Z:
        z = net.at["z"]
        devices.append(net.device(z=z + bit - 2 * bit * ((z // bit) % 2)))
        bit *= 2
    copies = [remote(mine.at[k], theirs.at[k], sems, k, device) for k, device in enumerate(devices)]

    def step(k):
        if k > 0:
            copies[k - 1].wait_recv()
            mine[k] = mine[k - 1] + theirs[k - 1]
        if k < len(copies):
            copies[k].start()

    return [lambda k=k: step(k) for k in range(len(copies) + 1)], copies


def rounds_of(Z, Y):
    assert 2 ** (Z - 1).bit_length() == Z
    return 2 + (Y == 2) + (Z - 1).bit_length()


def attend_back(qkv, do, mask_t, lse, d, small, seq, p, u):
    T = do.shape[0]
    rows = aligned(seq, LEN)
    lanes = aligned(p, 128)
    q, k, v = (qkv[pl.ds(pl.multiple_of(j * T + seq * LEN, LEN), LEN), lanes] for j in range(3))
    g = do[rows, lanes]
    kt = k.T
    dk = dv = None
    dqt = []
    for h in range(2):
        here = head_mask(h, k.shape)
        km, vm, qm, gm = (jnp.where(here, a, jnp.zeros_like(a)) for a in (k, v, q, g))
        t = dot(km, q, NT) * (0.125 * LOG2E) + mask_t[seq] - lse[seq * 2 * PAIRS + 2 * p + h, 0:1, :]
        pt = jnp.exp2(t)
        dp = dot(vm, g, NT)
        w = pt * dp
        ds = (w - pt * jnp.sum(w, axis=0, keepdims=True)).astype(BF16)
        dvh = dot(pt.astype(BF16), gm)
        dkh = dot(ds, qm)
        dv = dvh if dv is None else dv + dvh
        dk = dkh if dk is None else dk + dkh
        dqt.append(dot(kt[64 * h : 64 * h + 64, :], ds))
    dq = (jnp.concatenate(dqt, axis=0).T * 0.125).astype(BF16)
    dv = dv.astype(BF16)
    for j, grad in enumerate((dq, (dk * 0.125).astype(BF16), dv)):
        d[rows, pl.ds(pl.multiple_of(u * 384 + j * 128, 128), 128)] = grad
    small[0:1, lanes] += down_sum(dq.astype(F32))
    small[1:2, lanes] += down_sum(dv.astype(F32))


def pack_pair(net, buf, dw, small=None, exp=None):
    for i in range(BLOCKS):
        own = dw[24 * i : 24 * i + 24, :384]
        last = [jnp.zeros((24, 128), F32)]
        if small is not None:
            last = []
            for ref, at in ((small, 24 * i), (exp, 96 * i)):
                part = ref[:, at // 128 * 128 : at // 128 * 128 + 256]
                last.append((pltpu.roll(part, 256 - at % 128, axis=1) if at % 128 else part)[:, :128])
            last.append(jnp.zeros((8, 128), F32))
        buf[net.place(i)] = pair_block(own, jnp.concatenate(last, axis=0))


def backward_kernel(Z, Y, plan, *refs):
    (act_h, gp_h, df_h, dsec_h, normed_h, res_h, att_h, qkv_h, x_h, w1_h, w2_h, w_out_h, w_in_h) = refs[:13]
    vec, small_in, stats_in, segment, valid, lse = refs[13:19]
    dx_h, w2_own, w1_own, out_own, in_own, pair_own, stats = refs[19:26]
    parts = refs[26:35]
    (df, wide, normed, normed_t, att, res, w1, w2, w_out, act, gp, dh, dw, mask_t, small, exp, sum_mine, sum_theirs) = refs[35:53]
    ssem, rsem, sss, srs, loads, chunks, outs = refs[53:60]
    land = refs[60:]
    net = Net(Z, Y)
    T = df.shape[0]
    seqs, blocks = T // LEN, T // ROWS
    plan = list(plan)

    def load(src, dst, k):
        return pltpu.make_async_copy(src, dst, loads.at[k])

    def act_copy(j):
        return pltpu.make_async_copy(act_h.at[:, aligned(j, 384)], act.at[j % 2], chunks.at[j % 2])

    def gp_copy(t):
        return pltpu.make_async_copy(gp_h.at[:, pl.ds(t * 1024, 1024)], gp.at[t % 2], chunks.at[2 + t % 2])

    def res_copy(i):
        return pltpu.make_async_copy(res_h.at[aligned(i, ROWS), :], res.at[i % 2], chunks.at[4 + i % 2])

    load_df = load(df_h, df, 0)
    load_w2 = load(w2_h, w2, 1)
    load_normed = load(normed_h, normed, 2)
    load_w1 = load(w1_h, w1, 3)
    load_dsec = load(dsec_h, wide, 4)
    load_att, load_out = load(att_h, att, 6), load(w_out_h, w_out, 7)
    load_qkv, load_in, load_x = load(qkv_h, w2, 8), load(w_in_h, w1.at[:, pl.ds(0, 3 * D)], 9), load(x_h, att, 10)
    net.greet()
    act_copy(0).start()
    load_df.start()
    act_copy(1).start()
    small[...] = jnp.zeros_like(small)
    small[:, :D] = small_in[...]
    exp[...] = jnp.zeros_like(exp)
    sum_mine[0] = stats_in[...]
    for s in range(seqs):
        seg = segment[s : s + 1, :].astype(F32)
        build_mask(mask_t.at[s], jnp.where(valid[s : s + 1, :] > 0, seg, -1.0), seg)
    net.meet()
    load_df.wait()
    waiting = (load_w2, load_normed, gp_copy(0), load_dsec, load_w1, gp_copy(1), res_copy(0), load_att)

    def shrink_step(j):
        spread(j, 0, [copy.start for copy in waiting])
        act_copy(j).wait()
        v = dot(act[j % 2], df[...], TN).astype(BF16)
        for k in range(4):
            place = net.place(4 * j + k)
            for t in range(3):
                c = slice(256 * t, 256 * t + 256)
                parts[t][place + (ALL, slice(0, 256))] = v[96 * k : 96 * k + 48, c]
                parts[t][place + (ALL, slice(256, 512))] = v[96 * k + 48 : 96 * k + 96, c]
        pl.when(j + 2 < FF // 384)(lambda: act_copy(j + 2).start())

    loop(FF // 384, shrink_step)
    load_out.start()
    steps, moves = [], []
    for g in range(11):
        k = g if g < 7 else g - 7 if g < 9 else g - 2
        group, lines = parts[k], land[7 * k : 7 * k + 7]
        if g in (7, 8):
            group, *lines = (r.at[(ALL,) * (len(r.shape) - 1) + (pl.ds(0, 384),)] for r in (group, *lines))
        calls, sends = scatter_steps(net, group, lines, (ssem.at[g], rsem.at[g]), finish_of(g, w2_own, w1_own, out_own, in_own, pair_own))
        steps.append(calls)
        moves.append(sends)
    sum_calls, sum_copies = all_sum_steps(net, sum_mine, sum_theirs, (sss, srs))

    def move():
        todo = [steps[g][k] for g, k in plan.pop(0)]
        if sum_calls:
            todo.append(sum_calls.pop(0))
        return together(todo)

    def sent(g):
        for copies in moves[g]:
            copies.sent()

    move()()
    load_normed.wait()

    def turn(j):
        lanes = aligned(j, 128)
        normed_t[lanes, :] = normed[:, lanes].T

    loop(D // 128, turn)
    move()()
    load_w2.wait()
    load_w1.wait()
    load_dsec.wait()
    for t in range(3):
        gp_copy(t).wait()
        c = slice(t * 1024, (t + 1) * 1024)
        inner = [move(), move()]

        def expand_step(i, t=t, c=c):
            spread(i, 0, inner)
            r = aligned(i, 2 * ROWS)
            d = (dot(df[r, :], w2[c, :], NT) * gp[t % 2, r, :].astype(F32)).astype(BF16)
            dh[r, :] = d
            exp[0:1, c] += down_sum(d.astype(F32))
            wide[r, :] += dot(d, w1[:, c], NT)

        loop(blocks // 2, expand_step)
        if t == 0:
            gp_copy(2).start()
        move()()
        dw[...] = dot(normed_t[...], dh[...])
        pack(net, parts[3 + t], dw.at[:, :512], dw.at[:, 512:])
        move()()
    load_qkv.start()
    load_in.start()
    res_copy(1).start()
    load_att.wait()
    load_out.wait()
    inner = [move() for _ in range(blocks)]

    def norm_step(i):
        spread(i, 0, inner)
        r = aligned(i, ROWS)
        res_copy(i).wait()
        n, rsd = normalise(res[i % 2])
        pl.when(i + 2 < blocks)(lambda: res_copy(i + 2).start())
        g = wide[r, :]
        grad = norm_back(g, n, rsd, vec[3:4, :])
        wide[r, :] = grad
        low = grad.astype(BF16)
        df[r, :] = low
        add_small(small, "fg", down_sum(g * n))
        add_small(small, "fs", down_sum(g))
        add_small(small, "ob", down_sum(low.astype(F32)))
        normed[r, :] = dot(low, w_out[...], NT).astype(BF16)

    loop(blocks, norm_step)
    dw[:, :D] = dot(att[...], df[...], TN)
    load_x.start()
    pack(net, parts[6], dw.at[:, :384], dw.at[:, 384:D])
    move()()
    load_qkv.wait()
    d = (dh.at[:, pl.ds(0, D)], gp.at[0, :, pl.ds(0, D)], gp.at[1, :, pl.ds(0, D)])
    for t in range(2):
        inner = [move() for _ in range(2 * seqs)]

        def attend_step(i, t=t):
            spread(i, 0, inner)
            attend_back(w2, normed, mask_t, lse, d[t], small, i // 2, 2 * t + i % 2, i % 2)

        loop(2 * seqs, attend_step)
        if t == 0:
            load_x.wait()

            def turn_x(j):
                lanes = aligned(j, 128)
                normed_t[lanes, :] = att[:, lanes].T

            loop(D // 128, turn_x)
        dw[:, :D] = dot(normed_t[...], d[t][...])
        sent(t)
        pack(net, parts[t], dw.at[:, :384], dw.at[:, 384:D])
        move()()
    for u in range(2):
        inner = [move() for _ in range(seqs)]

        def attend_step(i, u=u):
            spread(i, 0, inner)
            attend_back(w2, normed, mask_t, lse, d[2], small, i, 4 + u, u)

        loop(seqs, attend_step)
        dw[:, :384] = dot(normed_t[...], d[2][:, u * 384 : (u + 1) * 384])
        pack_pair(net, parts[7 + u], dw, *((small, exp) if u == 1 else ()))
        move()()
    load_in.wait()
    inner = [move() for _ in range(blocks)]

    def token_step(i):
        spread(i, 0, inner)
        r = aligned(i, ROWS)
        wide[r, :] += sum(dot(d[t][r, :], w1[:, t * D : (t + 1) * D], NT) for t in range(3))

    loop(blocks, token_step)
    store = pltpu.make_async_copy(wide, dx_h, outs.at[0])
    store.start()
    stats[...] = sum_mine[len(sum_copies)]
    move()()
    assert not plan
    store.wait()
    for copy in sum_copies:
        copy.wait_send()
    for g in range(2, 11):
        sent(g)


def finish_of(g, w2_own, w1_own, out_own, in_own, pair_own):
    def finish(first, rows, total):
        if g < 3:
            w2_own[first : first + rows, g * 256 : (g + 1) * 256] = total[:, :256]
            w2_own[48 + first : 48 + first + rows, g * 256 : (g + 1) * 256] = total[:, 256:]
        else:
            own = w1_own.at[g - 3] if g < 6 else out_own if g == 6 else in_own.at[g - 7] if g < 9 else pair_own.at[g - 9]
            own[first : first + rows, : total.shape[1]] = total

    return finish


def backward(Z, Y, act, gp, df, dsec, normed, res, att, qkv, x, w1, w2, w_out, w_in, vec, small, stats, segment, valid, lse):
    T, S = df.shape[0], segment.shape[0]
    blocks = (2, 2, Y, Z, 48)
    rounds = rounds_of(Z, Y)
    outs = [
        SDS((T, D), F32), SDS((96, D), F32), SDS((3, 48, 512), F32), SDS((48, 384), F32), SDS((2, 48, 384), F32),
        SDS((2, 96, 128), F32), SDS((8, 128), F32),
    ]
    rows = pltpu.VMEM((T, D), BF16)
    scratch = [pltpu.VMEM(blocks + (512,), BF16)] * 6 + [
        pltpu.VMEM(blocks + (384,), BF16), pltpu.VMEM(blocks[:4] + (96, 128), BF16), pltpu.VMEM(blocks[:4] + (96, 128), BF16),
        rows, pltpu.VMEM((T, D), F32), rows, pltpu.VMEM((D, T), BF16), rows, pltpu.VMEM((2, ROWS, D), F32),
        pltpu.VMEM((D, FF), BF16), pltpu.VMEM((FF, D), BF16), pltpu.VMEM((D, D), BF16),
        pltpu.VMEM((2, T, 384), BF16), pltpu.VMEM((2, T, 1024), BF16), pltpu.VMEM((T, 1024), BF16),
        pltpu.VMEM((D, 1024), F32), pltpu.VMEM((S, LEN, LEN), F32), pltpu.VMEM((8, D + 128), F32), pltpu.VMEM((8, FF + 128), F32),
        pltpu.VMEM((rounds + 1, 8, 128), F32), pltpu.VMEM((rounds, 8, 128), F32),
        DMA((11, sem_count(Z))), DMA((11, sem_count(Z))), DMA((rounds,)), DMA((rounds,)), DMA((11,)), DMA((6,)), DMA((1,)),
    ] + lands(Z, Y, 48, 512) * 6 + lands(Z, Y, 48, 384) + lands(Z, Y, 96, 128) * 2
    return pl.pallas_call(
        functools.partial(backward_kernel, Z, Y, BACKWARD_PLAN),
        out_shape=outs,
        in_specs=[ANY] * 13 + [VMEM] * 6,
        out_specs=[ANY] + [VMEM] * 6,
        scratch_shapes=scratch,
        compiler_params=pltpu.CompilerParams(collective_id=1, has_side_effects=True, vmem_limit_bytes=VMEM_LIMIT),
        name="backward",
    )(act, gp, df, dsec, normed, res, att, qkv, x, w1, w2, w_out, w_in, vec, small, stats, segment, valid, lse)


def hand_out_kernel(dx_in, result_in, in_own, pair_own, out_own, w1_own, w2_own, stats, *refs):
    dx, result, w_in, w_out, w1, w2, mean, total, exp = refs[:9]
    vectors, (dx_here, result_here, load_sems, store_sems) = refs[9:17], refs[17:]
    T = dx.shape[0]
    loads, stores = [], []
    for src, here, dst, count in ((dx_in, dx_here, dx, 4), (result_in, result_here, result, 2)):
        for k in range(count):
            rows = pl.ds(k * (T // count), T // count)
            n = len(loads)
            loads.append(pltpu.make_async_copy(src.at[rows, :], here.at[rows, :], load_sems.at[n]))
            stores.append(pltpu.make_async_copy(here.at[rows, :], dst.at[rows, :], store_sems.at[n]))
    for copy in loads:
        copy.start()
    for p in range(PAIRS):
        for j in range(3):
            if p < 4:
                v = in_own[p // 2, 24 * (p % 2) : 24 * (p % 2) + 24, 128 * j : 128 * (j + 1)]
            else:
                v = pair_own[p - 4, 24 * j : 24 * j + 24, :]
            w_in[:, j * D + p * 128 : j * D + (p + 1) * 128] = v
    for t in range(3):
        w1[:, t * 1024 : t * 1024 + 512] = w1_own[t, :24, :]
        w1[:, t * 1024 + 512 : (t + 1) * 1024] = w1_own[t, 24:, :]
    w_out[:, :384] = out_own[:24, :]
    w_out[:, 384:] = out_own[24:, :]
    w2[...] = w2_own[...]
    for k in range(8):
        vectors[k][...] = pair_own[1, 72 + k : 73 + k, :24]
    exp[...] = pair_own[1, 80:81, :96]
    lane = lax.broadcasted_iota(jnp.int32, (1, 128), 1)
    sums = jnp.sum(stats[...], axis=1, keepdims=True)
    packed = jnp.zeros((1, 128), F32)
    for k in range(5):
        packed = jnp.where(lane == k, sums[k : k + 1, :], packed)
    total[...] = packed
    mean[...] = (packed / (D * sums[4:5, :]))[:, :4]
    for load, store in zip(loads, stores):
        load.wait()
        store.start()
    for copy in stores:
        copy.wait()


def hand_out(dx, result, in_own, pair_own, out_own, w1_own, w2_own, stats):
    outs = [
        SDS(dx.shape, F32), SDS(result.shape, BF16),
        SDS((24, 3 * D), F32), SDS((24, D), F32), SDS((24, FF), F32), SDS((96, D), F32),
        SDS((1, 4), F32), SDS((1, 128), F32), SDS((1, 96), F32),
    ] + [SDS((1, 24), F32)] * 8
    return pl.pallas_call(
        hand_out_kernel,
        out_shape=outs,
        in_specs=[ANY] * 2 + [VMEM] * 6,
        out_specs=[ANY] * 2 + [VMEM] * (len(outs) - 2),
        scratch_shapes=[pltpu.VMEM(dx.shape, F32), pltpu.VMEM(result.shape, BF16), DMA((6,)), DMA((6,))],
        compiler_params=pltpu.CompilerParams(vmem_limit_bytes=VMEM_LIMIT),
        name="hand_out",
    )(dx, result, in_own, pair_own, out_own, w1_own, w2_own, stats)


def per_device(
    Z, Y, fsdp, tokens, segment_ids, valid, input_weight, query_bias, value_bias, output_weight, output_bias,
    first_gain, first_shift, expand_weight, expand_bias, shrink_weight, shrink_bias, second_gain, second_shift, cotangent,
):
    shards = (input_weight, output_weight, expand_weight, shrink_weight)
    vectors = (query_bias, value_bias, output_bias, first_gain, first_shift, expand_bias, shrink_bias, second_gain, second_shift)
    split = Y == 1 and fsdp > 1
    if split:
        def whole(v):
            return lax.all_gather(v, "fsdp", axis=0, tiled=True)

        shards, vectors = tuple(map(whole, shards)), tuple(map(whole, vectors))
    vectors = [v.reshape(1, -1) for v in vectors]
    (res, qkv, att, normed, act, gp, df, lse, w_in, w_out, w1, w2, result, dsec, vec, small, stats) = forward(
        Z, Y, tokens, cotangent, segment_ids, valid, shards, vectors
    )
    dx, w2_own, w1_own, out_own, in_own, pair_own, stats = backward(
        Z, Y, act, gp, df, dsec, normed, res, att, qkv, tokens, w1, w2, w_out, w_in, vec, small, stats, segment_ids, valid, lse
    )
    (dx, result, *weights, mean, total, exp_own, qb, vb, ob, fg, fs, sb, sg, ss) = hand_out(
        dx, result, in_own, pair_own, out_own, w1_own, w2_own, stats
    )
    own = [v.reshape(-1) for v in (qb, vb, ob, fg, fs, sb, sg, ss, exp_own)]
    mean = mean.reshape(-1)
    if split:
        def share(v):
            return lax.psum_scatter(v, "fsdp", scatter_dimension=0, tiled=True)

        weights, own = [share(v) for v in weights], [share(v) for v in own]
        totals = lax.psum(total[0, :5], "fsdp")
        mean = totals[:4] / (D * totals[4])
    qb, vb, ob, fg, fs, sb, sg, ss, exp_own = own
    return (
        result, dx, mean, weights[0], qb, vb, weights[1], ob, fg, fs,
        weights[2], exp_own, weights[3], sb, sg, ss,
    )


def solution(mesh):
    dp, fsdp = mesh.shape["dp"], mesh.shape["fsdp"]
    Z, Y = dp // 4, (2 if dp * fsdp == BLOCKS else 1)
    matrix, vector = P(("dp", "fsdp"), None), P(("dp", "fsdp"))
    params = (matrix, vector, vector, matrix, vector, vector, vector, matrix, vector, matrix, vector, vector, vector)
    return jax.shard_map(
        functools.partial(per_device, Z, Y, fsdp),
        mesh=mesh,
        in_specs=(matrix, matrix, matrix) + params + (matrix,),
        out_specs=(matrix, matrix, P()) + params,
        check_vma=False,
    )
```

```python
import functools

import jax
import jax.numpy as jnp
from jax import lax
from jax.experimental import pallas as pl
from jax.experimental.pallas import tpu as pltpu
from jax.sharding import PartitionSpec as P

BLOCKS = 32
F32, BF16 = jnp.float32, jnp.bfloat16
LOG2E = 1.4426950408889634
MESH = pl.DeviceIdType.MESH
ALL = slice(None)
ANY = pl.BlockSpec(memory_space=pl.ANY)
VMEM = pl.BlockSpec(memory_space=pltpu.VMEM)
SDS = jax.ShapeDtypeStruct
DMA = pltpu.SemaphoreType.DMA
NT = (((1,), (1,)), ((), ()))
TN = (((0,), (0,)), ((), ()))
NN = (((1,), (0,)), ((), ()))
D, FF, LEN, PAIRS = 768, 3072, 512, 6
ROWS = 256


def dot(a, b, dims=NN):
    return lax.dot_general(a, b, dims, preferred_element_type=F32)


def aligned(at, step, size=None):
    return pl.ds(pl.multiple_of(at * step, step), step if size is None else size)


def loop(count, body):
    def step(i, carry):
        body(i)
        return carry

    lax.fori_loop(0, count, step, 0)


VMEM_LIMIT = 63 * 2**20


class Net:
    def __init__(self, Z, Y):
        self.Z, self.Y = Z, Y
        dp, y = lax.axis_index("dp"), lax.axis_index("fsdp")
        self.fsdp = y
        self.at = {"z": dp // 4, "x": (dp // 2) % 2, "c": dp % 2, "y": y if Y == 2 else 0}
        self.own = dp * Y + (y if Y == 2 else 0)

    def device(self, **moved):
        p = dict(self.at, **moved)
        return (p["z"] * 4 + p["x"] * 2 + p["c"], p["y"] if self.Y == 2 else self.fsdp)

    def across(self, axis):
        return self.device(**{axis: 1 - self.at[axis]})

    def z_away(self, k):
        return (self.at["z"] + k) % self.Z

    def others(self):
        axes = ["c", "x", "y"] if self.Y == 2 else ["c", "x"]
        return [self.across(axis) for axis in axes] + [self.device(z=self.z_away(k)) for k in range(1, self.Z)]

    def greet(self):
        for other in self.others():
            pl.semaphore_signal(pltpu.get_barrier_semaphore(), inc=1, device_id=other, device_id_type=MESH)

    def meet(self):
        pl.semaphore_wait(pltpu.get_barrier_semaphore(), len(self.others()))

    def place(self, i):
        Y = self.Y
        return ((i // Y) % 2, (i // (2 * Y)) % 2, i % Y, i // (4 * Y))

    def mine(self):
        at = self.at
        return (at["c"], at["x"], at["y"], at["z"])


STEPS = 5


def halves(buf):
    low = buf.shape[4] // 3
    return pl.ds(0, 2 * low), pl.ds(2 * low, low)


def sem_count(Z):
    return 2 * (Z - 1) + 5


def sem_ids(Z):
    n = Z - 1
    return {"tz": 0, "lz": n, "tx": 2 * n, "ty": 2 * n + 1, "lx": 2 * n + 2, "ly": 2 * n + 3, "c": 2 * n + 4}


def remote(src, dst, sems, sem, device):
    return pltpu.make_async_remote_copy(
        src_ref=src,
        dst_ref=dst,
        send_sem=sems[0].at[sem],
        recv_sem=sems[1].at[sem],
        device_id=device,
        device_id_type=MESH,
    )


class Move:
    def __init__(self, pairs):
        self.pairs = pairs

    def start(self):
        for send, _ in self.pairs:
            send().start()

    def receive(self):
        for _, take in self.pairs:
            take().wait_recv()

    def sent(self):
        for send, _ in self.pairs:
            send().wait_send()


def gather_moves(net, buf, sems):
    Z, Y, at, ids = net.Z, net.Y, net.at, sem_ids(net.Z)
    c, x, y, z = at["c"], at["x"], at["y"], at["z"]
    TOP, LOW = halves(buf)

    def swap(axis, ours, theirs, sem):
        device = net.across(axis)
        return [(lambda: remote(ours(), ours(), sems, sem, device), lambda: remote(theirs(), theirs(), sems, sem, device))]

    def along_z(part, sem):
        def pair(k):
            return (
                lambda: remote(part(z), part(z), sems, sem + k - 1, net.device(z=net.z_away(k))),
                lambda: remote(part(net.z_away(Z - k)), part(net.z_away(Z - k)), sems, sem + k - 1, net.device(z=net.z_away(k))),
            )

        return [pair(k) for k in range(1, Z)]

    yy = y if Y == 1 else ALL
    moves = [
        along_z(lambda zz: buf.at[c, x, y, zz, TOP], ids["tz"]),
        swap("x", lambda: buf.at[c, x, y, :, TOP], lambda: buf.at[c, 1 - x, y, :, TOP], ids["tx"])
        + along_z(lambda zz: buf.at[c, x, yy, zz, LOW], ids["lz"]),
        swap("x", lambda: buf.at[c, x, yy, :, LOW], lambda: buf.at[c, 1 - x, yy, :, LOW], ids["lx"]),
        swap("c", lambda: buf.at[c], lambda: buf.at[1 - c], ids["c"]),
    ]
    if Y == 2:
        moves[0] += swap("y", lambda: buf.at[c, x, y, z, LOW], lambda: buf.at[c, x, 1 - y, z, LOW], ids["ly"])
        moves[2] += swap("y", lambda: buf.at[c, :, y, :, TOP], lambda: buf.at[c, :, 1 - y, :, TOP], ids["ty"])
    return [Move(pairs) for pairs in moves]


def gather_steps(net, buf, sems):
    moves = gather_moves(net, buf, sems)

    def step(k):
        if k > 0:
            moves[k - 1].receive()
        if k < len(moves):
            moves[k].start()

    return [lambda k=k: step(k) for k in range(STEPS)], moves


def lands(Z, Y, rows, width):
    low = rows // 3
    top = 2 * low
    shapes = [(2, Y, Z, rows), (2, Z, top), (Y, Z, low), (Z, top), (Z - 1, Y, low), (Z - 1, top), (low,)]
    return [pltpu.VMEM(shape + (width,), BF16) for shape in shapes]


def add_blocks(count, at, dst, src):
    def one(i):
        idx = at(i)
        dst[idx] = dst[idx] + src[idx]

    loop(count, one)


def scatter_steps(net, buf, land, sems, finish):
    Z, Y, at, ids = net.Z, net.Y, net.at, sem_ids(net.Z)
    c, x, y, z = at["c"], at["x"], at["y"], at["z"]
    core, top_y, low_x, top_x, low_z, top_z, low_y = land
    TOP, LOW = halves(buf)
    low = buf.shape[4] // 3

    def swap(axis, what, where, sem):
        device = net.across(axis)

        def make():
            return remote(what(), where, sems, sem, device)

        return [(make, make)]

    def along_z(part, where, sem):
        def make(k):
            return lambda: remote(part(net.z_away(k)), where.at[k - 1], sems, sem + k - 1, net.device(z=net.z_away(k)))

        return [(make(k), make(k)) for k in range(1, Z)]

    yy = y if Y == 1 else ALL
    low_x_land, low_z_land = (low_x.at[0], low_z.at[:, 0]) if Y == 1 else (low_x, low_z)
    moves = [
        swap("c", lambda: buf.at[1 - c], core, ids["c"]),
        swap("x", lambda: buf.at[c, 1 - x, yy, :, LOW], low_x_land, ids["lx"]),
        swap("x", lambda: buf.at[c, 1 - x, y, :, TOP], top_x, ids["tx"])
        + along_z(lambda zz: buf.at[c, x, yy, zz, LOW], low_z_land, ids["lz"]),
        along_z(lambda zz: buf.at[c, x, y, zz, TOP], top_z, ids["tz"]),
    ]
    if Y == 2:
        moves[1] += swap("y", lambda: buf.at[c, :, 1 - y, :, TOP], top_y, ids["ty"])
        moves[3] += swap("y", lambda: buf.at[c, x, 1 - y, z, LOW], low_y, ids["ly"])
    moves = [Move(pairs) for pairs in moves]

    def sum_z(mine, where):
        total = mine.astype(F32)
        for k in range(Z - 1):
            total = total + where(k).astype(F32)
        return total

    def step(k):
        if k > 0:
            moves[k - 1].receive()
        if k == 1:
            add_blocks(2 * Y * Z, lambda i: (i // (Y * Z), (i // Z) % Y, i % Z), buf.at[c], core)
        if k == 2:
            if Y == 2:
                add_blocks(2 * Z, lambda i: (i // Z, i % Z), buf.at[c, :, y, :, TOP], top_y)
            add_blocks(Y * Z, lambda i: (i // Z, i % Z), buf.at[c, x, :, :, LOW], low_x)
        if k == 3:
            add_blocks(Z, lambda i: (i,), buf.at[c, x, y, :, TOP], top_x)
            for j in range(Y):
                own = buf.at[c, x, j, z, LOW]
                own[...] = sum_z(own[...], lambda i: low_z[i, j]).astype(BF16)
        if k < 4:
            moves[k].start()
        else:
            finish(0, 2 * low, sum_z(buf[c, x, y, z, TOP], lambda i: top_z[i]))
            rest = buf[c, x, y, z, LOW].astype(F32)
            finish(2 * low, low, rest + low_y[...].astype(F32) if Y == 2 else rest)

    return [lambda k=k: step(k) for k in range(STEPS)], moves


def together(todo):
    def call():
        for one in todo:
            one()

    return call


def train(steps, offsets):
    calls = []
    for t in range(len(steps) + offsets[-1]):
        todo = [steps[g][k] for g in range(len(steps)) for k in range(STEPS) if g + offsets[k] == t]
        calls.append(together(todo))
    return calls


def spread(i, first, calls, every=1):
    for k, call in enumerate(calls):
        pl.when(i == first + k * every)(call)


FORWARD_PLAN = (
    ((0, 0), (1, 0), (2, 0), (0, 1), (1, 1), (3, 0), (0, 2), (2, 1), (1, 2), (4, 0), (3, 1), (5, 0), (0, 3), (2, 2),),
    ((0, 4),),
    (),
    ((1, 3),),
    ((4, 1), (3, 2),),
    ((6, 0),),
    ((1, 4),),
    ((2, 3), (5, 1),),
    ((7, 0),),
    ((4, 2),),
    (),
    ((3, 3), (2, 4),),
    ((6, 1),),
    ((8, 0),),
    ((3, 4), (5, 2),),
    (),
    ((4, 3),),
    (),
    ((7, 1),),
    ((4, 4), (6, 2),),
    (),
    (),
    ((9, 0), (8, 1), (10, 0),),
    ((5, 3),),
    ((7, 2),),
    (),
    (),
    ((9, 1),),
    ((6, 3),),
    ((8, 2),),
    ((5, 4),),
    (),
    ((7, 3),),
    ((6, 4),),
    (),
    ((10, 1), (9, 2),),
    (),
    (),
    ((8, 3),),
    (),
    ((7, 4), (10, 2),),
    (),
    ((8, 4),),
    (),
    (),
    ((9, 3),),
    (),
    (),
    ((10, 3), (9, 4),),
    (),
    (),
    ((10, 4),),
)

BACKWARD_PLAN = (
    (),
    (),
    ((0, 0),),
    (),
    ((0, 1),),
    (),
    ((3, 0),),
    (),
    ((3, 1), (2, 0),),
    (),
    ((1, 0), (0, 2),),
    ((4, 0),),
    ((1, 1),),
    ((5, 0),),
    ((4, 1),),
    (),
    (),
    ((3, 2), (0, 3),),
    (),
    (),
    ((5, 1),),
    ((3, 3), (4, 2), (0, 4), (2, 1),),
    ((1, 2), (6, 0),),
    ((6, 1),),
    ((7, 0),),
    ((1, 3), (2, 2),),
    ((5, 2),),
    ((7, 1), (1, 4), (6, 2),),
    ((8, 0), (2, 3), (5, 3),),
    ((4, 3),),
    ((8, 1),),
    ((9, 0),),
    ((6, 3), (7, 2),),
    ((9, 1),),
    ((10, 0), (5, 4), (3, 4),),
    ((9, 2), (7, 3),),
    ((4, 4), (10, 1), (8, 2), (2, 4),),
    ((9, 3),),
    (),
    ((10, 2), (8, 3), (9, 4), (10, 3), (8, 4), (7, 4), (6, 4), (10, 4),),
)


def head_mask(head, shape):
    lane = lax.broadcasted_iota(jnp.int32, shape, len(shape) - 1)
    return (lane < 64) if head == 0 else (lane >= 64)


def column(row, count=128):
    return jnp.broadcast_to(row, (count, row.shape[1])).T


def build_mask(mask, down, across):
    n = mask.shape[0]
    down = column(down)
    at = lax.broadcasted_iota(jnp.int32, (n, 128), 0)
    lane = lax.broadcasted_iota(jnp.int32, (n, 128), 1)
    for j in range(n // 128):
        tile = slice(j * 128, (j + 1) * 128)
        mask[:, tile] = jnp.where((down == across[:, tile]) | (at == lane + j * 128), 0.0, -1e30).astype(mask.dtype)


def gelu_pair(h):
    cdf = 0.5 + 0.5 * lax.erf(h * 0.7071067811865476)
    return h * cdf, cdf + h * jnp.exp2(h * h * (-0.5 * LOG2E)) * 0.3989422804014327


def normalise(v):
    centred = v - jnp.sum(v, axis=1, keepdims=True) * (1.0 / D)
    r = lax.rsqrt(jnp.sum(centred * centred, axis=1, keepdims=True) * (1.0 / D) + 1e-12)
    return centred * r, r


def norm_back(g, n, r, gain):
    scaled = g * gain
    mean = jnp.sum(scaled, axis=1, keepdims=True) * (1.0 / D)
    along = jnp.sum(scaled * n, axis=1, keepdims=True) * (1.0 / D)
    return r * (scaled - mean - n * along)


def down_sum(v):
    return jnp.sum(v, axis=0, keepdims=True)


def square_sum(value, counted):
    v = value.astype(BF16).astype(F32)
    v = v * v
    total = v[:, :128]
    for j in range(1, D // 128):
        total = total + v[:, j * 128 : (j + 1) * 128]
    return down_sum(total * counted)


def fold(rows, half):
    return jnp.concatenate([rows[:, :half], rows[:, half:]], axis=0).astype(BF16)


def unfold(net, buf, half, dst, at=0):
    def pair(p):
        a = buf[net.place(2 * p) + (ALL, slice(0, half))].astype(F32)
        b = buf[net.place(2 * p + 1) + (ALL, slice(0, half))].astype(F32)
        rows = aligned(p, 48)
        dst[rows, at : at + half] = jnp.concatenate([a[:24], b[:24]], axis=0).astype(BF16)
        dst[rows, at + half : at + 2 * half] = jnp.concatenate([a[24:], b[24:]], axis=0).astype(BF16)

    loop(BLOCKS // 2, pair)


SMALL = ("qb", "vb", "ob", "fg", "fs", "sb", "sg", "ss")


def add_small(small, name, value):
    k = SMALL.index(name)
    small[k : k + 1, :D] += value


def pair_block(rows, last):
    return jnp.concatenate([rows[:, :128], rows[:, 128:256], rows[:, 256:], last], axis=0).astype(BF16)


def unfold_pair(net, buf, dst, at):
    def pair(p):
        a = buf[net.place(2 * p)].astype(F32)
        b = buf[net.place(2 * p + 1)].astype(F32)
        rows = aligned(p, 48)
        for j in range(3):
            part = slice(24 * j, 24 * j + 24)
            dst[rows, at + 128 * j : at + 128 * (j + 1)] = jnp.concatenate([a[part], b[part]], axis=0).astype(BF16)

    loop(BLOCKS // 2, pair)


def small_rows(vectors, expand, tmp):
    tmp[...] = jnp.zeros_like(tmp)
    for k, ref in enumerate(vectors):
        tmp[k : k + 1, :24] = ref[...].astype(F32)
    tmp[8:9, :96] = expand[...].astype(F32)
    return tmp[...]


def small_params(net, buf, vec, exp):
    vec[...] = jnp.zeros_like(vec)
    exp[...] = jnp.zeros_like(exp)
    for i in range(BLOCKS):
        w = buf[net.place(i) + (slice(64, 96), ALL)].astype(F32)
        for ref, first, at in ((vec, 8, 24 * i), (exp, 16, 96 * i)):
            part = jnp.concatenate([w[first : first + 8], jnp.zeros((8, 128), F32)], axis=1)
            if at % 128:
                part = pltpu.roll(part, at % 128, axis=1)
            tile = at // 128
            wide = min(256, ref.shape[1] - tile * 128)
            ref[:, tile * 128 : tile * 128 + wide] += part[:, :wide]


def pair_of(rows, p):
    return jnp.concatenate([rows[:, j * D + p * 128 : j * D + (p + 1) * 128] for j in range(3)], axis=1)


def attend(qkv, mask, att, lse, seq, p):
    T = att.shape[0]
    base = pl.multiple_of(seq * LEN, LEN)
    lanes = aligned(p, 128)
    q, k, v = (qkv[pl.ds(pl.multiple_of(j * T + seq * LEN, LEN), LEN), lanes] for j in range(3))
    lane = lax.broadcasted_iota(jnp.int32, (LEN, 128), 1)
    zero = jnp.zeros_like(k)
    here = [head_mask(h, k.shape) for h in range(2)]
    scores = [dot(q, jnp.where(m, k, zero), NT) for m in here]
    weights, totals, logs = [], [], lse[pl.ds(base, LEN), :]
    for h in range(2):
        t = scores[h] * (0.125 * LOG2E) + mask[seq]
        top = jnp.max(t, axis=1, keepdims=True)
        e = jnp.exp2(t - top)
        total = jnp.sum(e, axis=1, keepdims=True)
        weights.append(e.astype(BF16))
        totals.append(total)
        logs = jnp.where(lane == 2 * p + h, top + jnp.log2(total), logs)
    out = sum(dot(weights[h], jnp.where(here[h], v, zero)) * (1.0 / totals[h]) for h in range(2))
    lse[pl.ds(base, LEN), :] = logs
    att[pl.ds(base, LEN), lanes] = out.astype(BF16)


def forward_kernel(Z, Y, plan, *refs):
    (x_h, cot_h, segment, valid, w_in_s, w_out_s, w1_s, w2_s, qb, vb, ob, fg, fs, eb, sb, sg, ss) = refs[:17]
    (res_h, qkv_h, att_h, normed_h, act_h, gp_h, df_h, lse_h, w_in_h, w_out_h, w1_h, w2_h, result_h, dsec_h) = refs[17:31]
    vec, small, stats = refs[31:34]
    bufs = refs[34:45]
    (w_in, w_out, w1, w2, x, qkv, mask, att, lse, lse_rows, wide, normed, act, gp, cot, exp, tmp) = refs[45:62]
    ssem, rsem, loads, outs, gsem = refs[62:]
    net = Net(Z, Y)
    T = x.shape[0]
    seqs = T // LEN
    blocks = T // ROWS

    net.greet()
    load_x = pltpu.make_async_copy(x_h, x, loads.at[0])
    load_x.start()
    load_cot = pltpu.make_async_copy(cot_h, cot, loads.at[1])
    load_cot.start()
    mine = net.mine()
    own_in = w_in_s[...].astype(F32)
    own_1 = w1_s[...].astype(F32)
    bufs[0][mine] = pair_block(pair_of(own_in, 0), small_rows((qb, vb, ob, fg, fs, sb, sg, ss), eb, tmp))
    bufs[1][mine] = pair_block(pair_of(own_in, 1), jnp.zeros((24, 128), F32))
    for t in (1, 2):
        bufs[1 + t][mine] = jnp.concatenate([pair_of(own_in, 2 * t), pair_of(own_in, 2 * t + 1)], axis=0).astype(BF16)
    bufs[4][mine] = fold(w_out_s[...].astype(F32), 384)
    for t in range(3):
        bufs[5 + t][mine] = fold(own_1[:, t * 1024 : (t + 1) * 1024], 512)
        bufs[8 + t][mine + (ALL, slice(0, 256))] = w2_s[0:48, t * 256 : (t + 1) * 256]
        bufs[8 + t][mine + (ALL, slice(256, 512))] = w2_s[48:96, t * 256 : (t + 1) * 256]
    net.meet()
    steps, moves = [], []
    for g, buf in enumerate(bufs):
        calls, sends = gather_steps(net, buf, (ssem.at[g], rsem.at[g]))
        steps.append(calls)
        moves += sends
    plan = list(plan)

    def move():
        return together([steps[g][k] for g, k in plan.pop(0)])

    move()()
    small[...] = jnp.zeros_like(small)
    stats[...] = jnp.zeros_like(stats)
    for s in range(seqs):
        seg = segment[s : s + 1, :].astype(F32)
        live = valid[s : s + 1, :].astype(F32)
        build_mask(mask.at[s], seg, jnp.where(live > 0, seg, -1.0))
        stats[4:5, :] += sum(live[:, j * 128 : (j + 1) * 128] for j in range(LEN // 128))
    lse[...] = jnp.zeros_like(lse)
    move()()
    small_params(net, bufs[0], vec, exp)
    load_x.wait()
    stores = []

    def store(src, dst):
        copy = pltpu.make_async_copy(src, dst, outs.at[len(stores)])
        copy.start()
        stores.append(copy)
        return copy

    for g, pairs in enumerate(((0,), (1,), (2, 3), (4, 5))):
        if g > 0:
            move()()
        first, count = pairs[0], len(pairs)
        if count == 1:
            unfold_pair(net, bufs[g], w_in, first * 384)
        else:
            unfold(net, bufs[g], 384, w_in, first * 384)
        inner = [move(), move()]

        def project(i):
            spread(i, 0, inner)
            r = aligned(i, 2 * ROWS)
            c = dot(x[r, :], w_in[:, first * 384 : (first + count) * 384])
            for u, p in enumerate(pairs):
                for j in range(3):
                    part = c[:, u * 384 + j * 128 : u * 384 + (j + 1) * 128]
                    if j != 1:
                        part = part + vec[j // 2 : j // 2 + 1, p * 128 : (p + 1) * 128]
                    rows = pl.ds(pl.multiple_of(j * T + i * 2 * ROWS, 2 * ROWS), 2 * ROWS)
                    qkv[rows, p * 128 : (p + 1) * 128] = part.astype(BF16)

        loop(blocks // 2, project)
        inner = [move() for _ in range(seqs * count)]

        def attend_step(i):
            spread(i, 0, inner)
            attend(qkv, mask, att, lse, i // count, first + i % count)

        loop(seqs * count, attend_step)
    store(qkv, qkv_h)
    store(w_in, w_in_h)
    store_att = store(att, att_h)
    for s in range(seqs):
        rows = lse[s * LEN : (s + 1) * LEN, :].T
        for h in range(2 * PAIRS):
            lse_rows[s * 2 * PAIRS + h] = jnp.broadcast_to(rows[h : h + 1, :], (8, LEN))
    store(lse_rows, lse_h)
    move()()
    unfold(net, bufs[4], 384, w_out)
    store(w_out, w_out_h)

    def out_step(i):
        spread(i, 0, inner)
        r = aligned(i, ROWS)
        branch = dot(att[r, :], w_out[...]) + vec[2:3, :]
        residual = x[r, :].astype(F32) + branch
        wide[r, :] = residual
        n, _ = normalise(residual)
        normed[r, :] = (n * vec[3:4, :] + vec[4:5, :]).astype(BF16)
        live = live_rows(i)
        stats[0:1, :] += square_sum(residual, live)
        stats[1:2, :] += square_sum(branch, live)

    def live_rows(i):
        return live_col[aligned(i, ROWS), :]

    live_col = lse
    for s in range(seqs):
        live_col[s * LEN : (s + 1) * LEN, :] = column(valid[s : s + 1, :].astype(F32))
    inner = [move() for _ in range(blocks)]
    loop(blocks, out_step)
    store_wide = store(wide, res_h)
    store(normed, normed_h)

    def gp_copy(t, i):
        slot = (t * blocks + i) % 2
        return pltpu.make_async_copy(
            gp.at[slot], gp_h.at[aligned(i, ROWS), pl.ds(t * 1024, 1024)], gsem.at[slot]
        )

    for t in range(3):
        move()()
        unfold(net, bufs[5 + t], 512, w1, t * 1024)
        inner = [move() for _ in range(blocks)]

        def expand_step(i):
            spread(i, 0, inner)
            r = aligned(i, ROWS)
            nv = normed[r, :]
            slot = (t * blocks + i) % 2
            if t == 0:
                pl.when(i >= 2)(lambda: gp_copy(t, i).wait())
            else:
                gp_copy(t, i).wait()
            for j in range(2):
                c = slice(t * 1024 + j * 512, t * 1024 + (j + 1) * 512)
                a, g = gelu_pair(dot(nv, w1[:, c]) + exp[0:1, c])
                act[r, c] = a.astype(BF16)
                gp[slot, :, j * 512 : (j + 1) * 512] = g.astype(BF16)
            gp_copy(t, i).start()

        loop(blocks, expand_step)
    store(w1, w1_h)
    store(act, act_h)
    store_wide.wait()
    for t in range(3):
        move()()

        def unfold_last(i, t=t):
            blk = bufs[8 + t].at[net.place(i)]
            c = slice(t * 256, (t + 1) * 256)
            w2[aligned(i, 96, 48), c] = blk[:, :256]
            w2[pl.ds(pl.multiple_of(i * 96 + 48, 48), 48), c] = blk[:, 256:]

        loop(BLOCKS, unfold_last)
        if t < 2:
            inner = [move(), move()]

            def shrink_step(i, t=t):
                spread(i, 0, inner)
                r = aligned(i, 2 * ROWS)
                wide[r, t * 256 : (t + 1) * 256] = dot(act[r, :], w2[:, t * 256 : (t + 1) * 256])

            loop(blocks // 2, shrink_step)
    assert not plan
    store(w2, w2_h)
    store_att.wait()
    load_cot.wait()

    def end_copies(r):
        pairs = ((wide, dsec_h), (att, result_h), (x, df_h))
        return [pltpu.make_async_copy(src.at[r, :], dst.at[r, :], loads.at[k]) for k, (src, dst) in enumerate(pairs)]

    def last_step(i):
        r = aligned(i, ROWS)
        feedfwd = jnp.concatenate([wide[r, :512], dot(act[r, :], w2[:, 512:])], axis=1) + vec[5:6, :]
        second = normed[r, :].astype(F32) + feedfwd
        n, rs = normalise(second)
        gain = vec[6:7, :]
        att[r, :] = (n * gain + vec[7:8, :]).astype(BF16)
        g = cot[r, :].astype(F32)
        grad = norm_back(g, n, rs, gain)
        wide[r, :] = grad
        low = grad.astype(BF16)
        x[r, :] = low
        for copy in end_copies(r):
            copy.start()
        add_small(small, "sg", down_sum(g * n))
        add_small(small, "ss", down_sum(g))
        add_small(small, "sb", down_sum(low.astype(F32)))
        live = live_rows(i)
        stats[2:3, :] += square_sum(second, live)
        stats[3:4, :] += square_sum(feedfwd, live)

    loop(blocks, last_step)
    for k in (0, 1):
        gp_copy(2, blocks - 2 + k).wait()
    for copy in stores:
        if copy is not store_wide and copy is not store_att:
            copy.wait()
    for copy in end_copies(ALL):
        copy.wait()
    for move in moves:
        move.sent()


def forward(Z, Y, x, cot, segment, valid, shards, vectors):
    T, S = x.shape[0], segment.shape[0]
    blocks = (2, 2, Y, Z)
    shapes = ((96, 128),) * 2 + ((48, 384),) * 3 + ((48, 512),) * 6
    outs = [
        SDS((T, D), F32), SDS((3 * T, D), BF16), SDS((T, D), BF16), SDS((T, D), BF16),
        SDS((T, FF), BF16), SDS((T, FF), BF16), SDS((T, D), BF16), SDS((S * 12, 8, LEN), F32),
        SDS((D, 3 * D), BF16), SDS((D, D), BF16), SDS((D, FF), BF16), SDS((FF, D), BF16),
        SDS((T, D), BF16), SDS((T, D), F32), SDS((8, D), F32), SDS((8, D), F32), SDS((8, 128), F32),
    ]
    scratch = [pltpu.VMEM(blocks + shape, BF16) for shape in shapes] + [
        pltpu.VMEM((D, 3 * D), BF16), pltpu.VMEM((D, D), BF16), pltpu.VMEM((D, FF), BF16), pltpu.VMEM((FF, D), BF16),
        pltpu.VMEM((T, D), BF16), pltpu.VMEM((3 * T, D), BF16), pltpu.VMEM((S, LEN, LEN), F32),
        pltpu.VMEM((T, D), BF16), pltpu.VMEM((T, 128), F32), pltpu.VMEM((S * 12, 8, LEN), F32),
        pltpu.VMEM((T, D), F32), pltpu.VMEM((T, D), BF16), pltpu.VMEM((T, FF), BF16), pltpu.VMEM((2, ROWS, 1024), BF16),
        pltpu.VMEM((T, D), BF16), pltpu.VMEM((8, FF), F32), pltpu.VMEM((24, 128), F32),
        DMA((len(shapes), sem_count(Z))), DMA((len(shapes), sem_count(Z))), DMA((3,)), DMA((16,)), DMA((2,)),
    ]
    return pl.pallas_call(
        functools.partial(forward_kernel, Z, Y, FORWARD_PLAN),
        out_shape=outs,
        in_specs=[ANY, ANY] + [VMEM] * 15,
        out_specs=[ANY] * 14 + [VMEM] * 3,
        scratch_shapes=scratch,
        compiler_params=pltpu.CompilerParams(collective_id=0, has_side_effects=True, vmem_limit_bytes=VMEM_LIMIT),
        name="forward",
    )(x, cot, segment, valid, *shards, *vectors)


def pack(net, buf, left, right):
    width = left.shape[1]

    def owner(i):
        rows = aligned(i, 24)
        v = jnp.concatenate([left[rows, :], right[rows, :]], axis=0).astype(BF16)
        buf[net.place(i) + (ALL, slice(0, width))] = v

    loop(BLOCKS, owner)


def all_sum_steps(net, mine, theirs, sems):
    partners = ["c", "x", "y"] if net.Y == 2 else ["c", "x"]
    devices = [net.across(axis) for axis in partners]
    bit = 1
    while bit < net.Z:
        z = net.at["z"]
        devices.append(net.device(z=z + bit - 2 * bit * ((z // bit) % 2)))
        bit *= 2
    copies = [remote(mine.at[k], theirs.at[k], sems, k, device) for k, device in enumerate(devices)]

    def step(k):
        if k > 0:
            copies[k - 1].wait_recv()
            mine[k] = mine[k - 1] + theirs[k - 1]
        if k < len(copies):
            copies[k].start()

    return [lambda k=k: step(k) for k in range(len(copies) + 1)], copies


def rounds_of(Z, Y):
    assert 2 ** (Z - 1).bit_length() == Z
    return 2 + (Y == 2) + (Z - 1).bit_length()


def attend_back(qkv, do, mask_t, lse, d, small, seq, p, u):
    T = do.shape[0]
    rows = aligned(seq, LEN)
    lanes = aligned(p, 128)
    q, k, v = (qkv[pl.ds(pl.multiple_of(j * T + seq * LEN, LEN), LEN), lanes] for j in range(3))
    g = do[rows, lanes]
    kt = k.T
    dk = dv = None
    dqt = []
    for h in range(2):
        here = head_mask(h, k.shape)
        km, vm, qm, gm = (jnp.where(here, a, jnp.zeros_like(a)) for a in (k, v, q, g))
        t = dot(km, q, NT) * (0.125 * LOG2E) + mask_t[seq] - lse[seq * 2 * PAIRS + 2 * p + h, 0:1, :]
        pt = jnp.exp2(t)
        dp = dot(vm, g, NT)
        w = pt * dp
        ds = (w - pt * jnp.sum(w, axis=0, keepdims=True)).astype(BF16)
        dvh = dot(pt.astype(BF16), gm)
        dkh = dot(ds, qm)
        dv = dvh if dv is None else dv + dvh
        dk = dkh if dk is None else dk + dkh
        dqt.append(dot(kt[64 * h : 64 * h + 64, :], ds))
    dq = (jnp.concatenate(dqt, axis=0).T * 0.125).astype(BF16)
    dv = dv.astype(BF16)
    for j, grad in enumerate((dq, (dk * 0.125).astype(BF16), dv)):
        d[rows, pl.ds(pl.multiple_of(u * 384 + j * 128, 128), 128)] = grad
    small[0:1, lanes] += down_sum(dq.astype(F32))
    small[1:2, lanes] += down_sum(dv.astype(F32))


def pack_pair(net, buf, dw, small=None, exp=None):
    for i in range(BLOCKS):
        own = dw[24 * i : 24 * i + 24, :384]
        last = [jnp.zeros((24, 128), F32)]
        if small is not None:
            last = []
            for ref, at in ((small, 24 * i), (exp, 96 * i)):
                part = ref[:, at // 128 * 128 : at // 128 * 128 + 256]
                last.append((pltpu.roll(part, 256 - at % 128, axis=1) if at % 128 else part)[:, :128])
            last.append(jnp.zeros((8, 128), F32))
        buf[net.place(i)] = pair_block(own, jnp.concatenate(last, axis=0))


def backward_kernel(Z, Y, plan, *refs):
    (act_h, gp_h, df_h, dsec_h, normed_h, res_h, att_h, qkv_h, x_h, w1_h, w2_h, w_out_h, w_in_h) = refs[:13]
    vec, small_in, stats_in, segment, valid, lse = refs[13:19]
    dx_h, w2_own, w1_own, out_own, in_own, pair_own, stats = refs[19:26]
    parts = refs[26:35]
    (df, wide, normed, normed_t, att, res, w1, w2, w_out, act, gp, dh, dw, mask_t, small, exp, sum_mine, sum_theirs) = refs[35:53]
    ssem, rsem, sss, srs, loads, chunks, outs = refs[53:60]
    land = refs[60:]
    net = Net(Z, Y)
    T = df.shape[0]
    seqs, blocks = T // LEN, T // ROWS
    plan = list(plan)

    def load(src, dst, k):
        return pltpu.make_async_copy(src, dst, loads.at[k])

    slots = (act.at[0], act.at[1], dh.at[:, pl.ds(0, 384)], dh.at[:, pl.ds(384, 384)])

    def act_copy(j, s):
        return pltpu.make_async_copy(act_h.at[:, aligned(j, 384)], slots[s], chunks.at[(0, 1, 6, 7)[s]])

    def gp_copy(t):
        return pltpu.make_async_copy(gp_h.at[:, pl.ds(t * 1024, 1024)], gp.at[t % 2], chunks.at[2 + t % 2])

    def res_copy(i):
        return pltpu.make_async_copy(res_h.at[aligned(i, ROWS), :], res.at[i % 2], chunks.at[4 + i % 2])

    load_df = load(df_h, df, 0)
    load_w2 = load(w2_h, w2, 1)
    load_normed = load(normed_h, normed, 2)
    load_w1 = load(w1_h, w1, 3)
    load_dsec = load(dsec_h, wide, 4)
    load_att, load_out = load(att_h, att, 6), load(w_out_h, w_out, 7)
    load_qkv, load_in, load_x = load(qkv_h, w2, 8), load(w_in_h, w1.at[:, pl.ds(0, 3 * D)], 9), load(x_h, att, 10)
    net.greet()
    act_copy(0, 0).start()
    load_df.start()
    for s in range(1, 4):
        act_copy(s, s).start()
    small[...] = jnp.zeros_like(small)
    small[:, :D] = small_in[...]
    exp[...] = jnp.zeros_like(exp)
    sum_mine[0] = stats_in[...]
    for s in range(seqs):
        seg = segment[s : s + 1, :].astype(F32)
        build_mask(mask_t.at[s], jnp.where(valid[s : s + 1, :] > 0, seg, -1.0), seg)
    net.meet()
    load_df.wait()
    waiting = (load_w2, load_normed, gp_copy(0), load_dsec, load_w1, gp_copy(1), res_copy(0), load_att)

    def shrink_step(i):
        for s in range(4):
            j = 4 * i + s
            spread(i, 0, [copy.start for copy in waiting[s::4]])
            act_copy(j, s).wait()
            v = dot(slots[s][...], df[...], TN).astype(BF16)
            for k in range(4):
                place = net.place(4 * j + k)
                for t in range(3):
                    c = slice(256 * t, 256 * t + 256)
                    parts[t][place + (ALL, slice(0, 256))] = v[96 * k : 96 * k + 48, c]
                    parts[t][place + (ALL, slice(256, 512))] = v[96 * k + 48 : 96 * k + 96, c]
            pl.when(i == 0)(lambda j=j, s=s: act_copy(j + 4, s).start())

    loop(FF // 384 // 4, shrink_step)
    load_out.start()
    steps, moves = [], []
    for g in range(11):
        k = g if g < 7 else g - 7 if g < 9 else g - 2
        group, lines = parts[k], land[7 * k : 7 * k + 7]
        if g in (7, 8):
            group, *lines = (r.at[(ALL,) * (len(r.shape) - 1) + (pl.ds(0, 384),)] for r in (group, *lines))
        calls, sends = scatter_steps(net, group, lines, (ssem.at[g], rsem.at[g]), finish_of(g, w2_own, w1_own, out_own, in_own, pair_own))
        steps.append(calls)
        moves.append(sends)
    sum_calls, sum_copies = all_sum_steps(net, sum_mine, sum_theirs, (sss, srs))

    def move():
        todo = [steps[g][k] for g, k in plan.pop(0)]
        if sum_calls:
            todo.append(sum_calls.pop(0))
        return together(todo)

    def sent(g):
        for copies in moves[g]:
            copies.sent()

    move()()
    load_normed.wait()

    def turn(j):
        lanes = aligned(j, 128)
        normed_t[lanes, :] = normed[:, lanes].T

    loop(D // 128, turn)
    move()()
    load_w2.wait()
    load_w1.wait()
    load_dsec.wait()
    for t in range(3):
        gp_copy(t).wait()
        c = slice(t * 1024, (t + 1) * 1024)
        inner = [move(), move()]

        def expand_step(i, t=t, c=c):
            spread(i, 0, inner)
            r = aligned(i, 2 * ROWS)
            d = (dot(df[r, :], w2[c, :], NT) * gp[t % 2, r, :].astype(F32)).astype(BF16)
            dh[r, :] = d
            exp[0:1, c] += down_sum(d.astype(F32))
            wide[r, :] += dot(d, w1[:, c], NT)

        loop(blocks // 2, expand_step)
        if t == 0:
            gp_copy(2).start()
        move()()
        dw[...] = dot(normed_t[...], dh[...])
        pack(net, parts[3 + t], dw.at[:, :512], dw.at[:, 512:])
        move()()
    load_qkv.start()
    load_in.start()
    res_copy(1).start()
    load_att.wait()
    load_out.wait()
    inner = [move() for _ in range(blocks)]

    def norm_step(i):
        spread(i, 0, inner)
        r = aligned(i, ROWS)
        res_copy(i).wait()
        n, rsd = normalise(res[i % 2])
        pl.when(i + 2 < blocks)(lambda: res_copy(i + 2).start())
        g = wide[r, :]
        grad = norm_back(g, n, rsd, vec[3:4, :])
        wide[r, :] = grad
        low = grad.astype(BF16)
        df[r, :] = low
        add_small(small, "fg", down_sum(g * n))
        add_small(small, "fs", down_sum(g))
        add_small(small, "ob", down_sum(low.astype(F32)))
        normed[r, :] = dot(low, w_out[...], NT).astype(BF16)

    loop(blocks, norm_step)
    dw[:, :D] = dot(att[...], df[...], TN)
    load_x.start()
    pack(net, parts[6], dw.at[:, :384], dw.at[:, 384:D])
    move()()
    load_qkv.wait()
    d = (dh.at[:, pl.ds(0, D)], gp.at[0, :, pl.ds(0, D)], gp.at[1, :, pl.ds(0, D)])
    for t in range(2):
        inner = [move() for _ in range(2 * seqs)]

        def attend_step(i, t=t):
            spread(i, 0, inner)
            attend_back(w2, normed, mask_t, lse, d[t], small, i // 2, 2 * t + i % 2, i % 2)

        loop(2 * seqs, attend_step)
        if t == 0:
            load_x.wait()

            def turn_x(j):
                lanes = aligned(j, 128)
                normed_t[lanes, :] = att[:, lanes].T

            loop(D // 128, turn_x)
        dw[:, :D] = dot(normed_t[...], d[t][...])
        sent(t)
        pack(net, parts[t], dw.at[:, :384], dw.at[:, 384:D])
        move()()
    for u in range(2):
        inner = [move() for _ in range(seqs)]

        def attend_step(i, u=u):
            spread(i, 0, inner)
            attend_back(w2, normed, mask_t, lse, d[2], small, i, 4 + u, u)

        loop(seqs, attend_step)
        dw[:, :384] = dot(normed_t[...], d[2][:, u * 384 : (u + 1) * 384])
        pack_pair(net, parts[7 + u], dw, *((small, exp) if u == 1 else ()))
        move()()
    load_in.wait()
    inner = [move() for _ in range(blocks)]

    def token_step(i):
        spread(i, 0, inner)
        r = aligned(i, ROWS)
        wide[r, :] += sum(dot(d[t][r, :], w1[:, t * D : (t + 1) * D], NT) for t in range(3))

    loop(blocks, token_step)
    store = pltpu.make_async_copy(wide, dx_h, outs.at[0])
    store.start()
    stats[...] = sum_mine[len(sum_copies)]
    move()()
    assert not plan
    store.wait()
    for copy in sum_copies:
        copy.wait_send()
    for g in range(2, 11):
        sent(g)


def finish_of(g, w2_own, w1_own, out_own, in_own, pair_own):
    def finish(first, rows, total):
        if g < 3:
            w2_own[first : first + rows, g * 256 : (g + 1) * 256] = total[:, :256]
            w2_own[48 + first : 48 + first + rows, g * 256 : (g + 1) * 256] = total[:, 256:]
        else:
            own = w1_own.at[g - 3] if g < 6 else out_own if g == 6 else in_own.at[g - 7] if g < 9 else pair_own.at[g - 9]
            own[first : first + rows, : total.shape[1]] = total

    return finish


def backward(Z, Y, act, gp, df, dsec, normed, res, att, qkv, x, w1, w2, w_out, w_in, vec, small, stats, segment, valid, lse):
    T, S = df.shape[0], segment.shape[0]
    blocks = (2, 2, Y, Z, 48)
    rounds = rounds_of(Z, Y)
    outs = [
        SDS((T, D), F32), SDS((96, D), F32), SDS((3, 48, 512), F32), SDS((48, 384), F32), SDS((2, 48, 384), F32),
        SDS((2, 96, 128), F32), SDS((8, 128), F32),
    ]
    rows = pltpu.VMEM((T, D), BF16)
    scratch = [pltpu.VMEM(blocks + (512,), BF16)] * 6 + [
        pltpu.VMEM(blocks + (384,), BF16), pltpu.VMEM(blocks[:4] + (96, 128), BF16), pltpu.VMEM(blocks[:4] + (96, 128), BF16),
        rows, pltpu.VMEM((T, D), F32), rows, pltpu.VMEM((D, T), BF16), rows, pltpu.VMEM((2, ROWS, D), F32),
        pltpu.VMEM((D, FF), BF16), pltpu.VMEM((FF, D), BF16), pltpu.VMEM((D, D), BF16),
        pltpu.VMEM((2, T, 384), BF16), pltpu.VMEM((2, T, 1024), BF16), pltpu.VMEM((T, 1024), BF16),
        pltpu.VMEM((D, 1024), F32), pltpu.VMEM((S, LEN, LEN), F32), pltpu.VMEM((8, D + 128), F32), pltpu.VMEM((8, FF + 128), F32),
        pltpu.VMEM((rounds + 1, 8, 128), F32), pltpu.VMEM((rounds, 8, 128), F32),
        DMA((11, sem_count(Z))), DMA((11, sem_count(Z))), DMA((rounds,)), DMA((rounds,)), DMA((11,)), DMA((8,)), DMA((1,)),
    ] + lands(Z, Y, 48, 512) * 6 + lands(Z, Y, 48, 384) + lands(Z, Y, 96, 128) * 2
    return pl.pallas_call(
        functools.partial(backward_kernel, Z, Y, BACKWARD_PLAN),
        out_shape=outs,
        in_specs=[ANY] * 13 + [VMEM] * 6,
        out_specs=[ANY] + [VMEM] * 6,
        scratch_shapes=scratch,
        compiler_params=pltpu.CompilerParams(collective_id=1, has_side_effects=True, vmem_limit_bytes=VMEM_LIMIT),
        name="backward",
    )(act, gp, df, dsec, normed, res, att, qkv, x, w1, w2, w_out, w_in, vec, small, stats, segment, valid, lse)


def hand_out_kernel(dx_in, result_in, *refs):
    given, refs = refs[:6], refs[6:]
    dx, result, w_in, w_out, w1, w2, mean, total, exp = refs[:9]
    vectors, (dx_here, result_here, load_sems, store_sems, given_sems) = refs[9:17], refs[17:22]
    in_own, pair_own, out_own, w1_own, w2_own, stats = here = refs[22:]
    takes = [pltpu.make_async_copy(src, dst, given_sems.at[k]) for k, (src, dst) in enumerate(zip(given, here))]
    for copy in takes:
        copy.start()
    T = dx.shape[0]
    loads, stores = [], []
    for src, here, dst, count in ((dx_in, dx_here, dx, 4), (result_in, result_here, result, 2)):
        for k in range(count):
            rows = pl.ds(k * (T // count), T // count)
            n = len(loads)
            loads.append(pltpu.make_async_copy(src.at[rows, :], here.at[rows, :], load_sems.at[n]))
            stores.append(pltpu.make_async_copy(here.at[rows, :], dst.at[rows, :], store_sems.at[n]))
    for copy in loads:
        copy.start()
    for copy in takes:
        copy.wait()
    for p in range(PAIRS):
        for j in range(3):
            if p < 4:
                v = in_own[p // 2, 24 * (p % 2) : 24 * (p % 2) + 24, 128 * j : 128 * (j + 1)]
            else:
                v = pair_own[p - 4, 24 * j : 24 * j + 24, :]
            w_in[:, j * D + p * 128 : j * D + (p + 1) * 128] = v
    for t in range(3):
        w1[:, t * 1024 : t * 1024 + 512] = w1_own[t, :24, :]
        w1[:, t * 1024 + 512 : (t + 1) * 1024] = w1_own[t, 24:, :]
    w_out[:, :384] = out_own[:24, :]
    w_out[:, 384:] = out_own[24:, :]
    w2[...] = w2_own[...]
    for k in range(8):
        vectors[k][...] = pair_own[1, 72 + k : 73 + k, :24]
    exp[...] = pair_own[1, 80:81, :96]
    lane = lax.broadcasted_iota(jnp.int32, (1, 128), 1)
    sums = jnp.sum(stats[...], axis=1, keepdims=True)
    packed = jnp.zeros((1, 128), F32)
    for k in range(5):
        packed = jnp.where(lane == k, sums[k : k + 1, :], packed)
    total[...] = packed
    mean[...] = (packed / (D * sums[4:5, :]))[:, :4]
    for load, store in zip(loads, stores):
        load.wait()
        store.start()
    for copy in stores:
        copy.wait()


def hand_out(dx, result, in_own, pair_own, out_own, w1_own, w2_own, stats):
    outs = [
        SDS(dx.shape, F32), SDS(result.shape, BF16),
        SDS((24, 3 * D), F32), SDS((24, D), F32), SDS((24, FF), F32), SDS((96, D), F32),
        SDS((1, 4), F32), SDS((1, 128), F32), SDS((1, 96), F32),
    ] + [SDS((1, 24), F32)] * 8
    return pl.pallas_call(
        hand_out_kernel,
        out_shape=outs,
        in_specs=[ANY] * 8,
        out_specs=[ANY] * 2 + [VMEM] * (len(outs) - 2),
        scratch_shapes=[pltpu.VMEM(dx.shape, F32), pltpu.VMEM(result.shape, BF16), DMA((6,)), DMA((6,)), DMA((6,))]
        + [pltpu.VMEM(v.shape, F32) for v in (in_own, pair_own, out_own, w1_own, w2_own, stats)],
        compiler_params=pltpu.CompilerParams(vmem_limit_bytes=VMEM_LIMIT),
        name="hand_out",
    )(dx, result, in_own, pair_own, out_own, w1_own, w2_own, stats)


def per_device(
    Z, Y, fsdp, tokens, segment_ids, valid, input_weight, query_bias, value_bias, output_weight, output_bias,
    first_gain, first_shift, expand_weight, expand_bias, shrink_weight, shrink_bias, second_gain, second_shift, cotangent,
):
    shards = (input_weight, output_weight, expand_weight, shrink_weight)
    vectors = (query_bias, value_bias, output_bias, first_gain, first_shift, expand_bias, shrink_bias, second_gain, second_shift)
    split = Y == 1 and fsdp > 1
    if split:
        def whole(v):
            return lax.all_gather(v, "fsdp", axis=0, tiled=True)

        shards, vectors = tuple(map(whole, shards)), tuple(map(whole, vectors))
    vectors = [v.reshape(1, -1) for v in vectors]
    (res, qkv, att, normed, act, gp, df, lse, w_in, w_out, w1, w2, result, dsec, vec, small, stats) = forward(
        Z, Y, tokens, cotangent, segment_ids, valid, shards, vectors
    )
    dx, w2_own, w1_own, out_own, in_own, pair_own, stats = backward(
        Z, Y, act, gp, df, dsec, normed, res, att, qkv, tokens, w1, w2, w_out, w_in, vec, small, stats, segment_ids, valid, lse
    )
    (dx, result, *weights, mean, total, exp_own, qb, vb, ob, fg, fs, sb, sg, ss) = hand_out(
        dx, result, in_own, pair_own, out_own, w1_own, w2_own, stats
    )
    own = [v.reshape(-1) for v in (qb, vb, ob, fg, fs, sb, sg, ss, exp_own)]
    mean = mean.reshape(-1)
    if split:
        def share(v):
            return lax.psum_scatter(v, "fsdp", scatter_dimension=0, tiled=True)

        weights, own = [share(v) for v in weights], [share(v) for v in own]
        totals = lax.psum(total[0, :5], "fsdp")
        mean = totals[:4] / (D * totals[4])
    qb, vb, ob, fg, fs, sb, sg, ss, exp_own = own
    return (
        result, dx, mean, weights[0], qb, vb, weights[1], ob, fg, fs,
        weights[2], exp_own, weights[3], sb, sg, ss,
    )


def solution(mesh):
    dp, fsdp = mesh.shape["dp"], mesh.shape["fsdp"]
    Z, Y = dp // 4, (2 if dp * fsdp == BLOCKS else 1)
    matrix, vector = P(("dp", "fsdp"), None), P(("dp", "fsdp"))
    params = (matrix, vector, vector, matrix, vector, vector, vector, matrix, vector, matrix, vector, vector, vector)
    return jax.shard_map(
        functools.partial(per_device, Z, Y, fsdp),
        mesh=mesh,
        in_specs=(matrix, matrix, matrix) + params + (matrix,),
        out_specs=(matrix, matrix, P()) + params,
        check_vma=False,
    )
```
